128 devices in a mesh: dp: 16 (over y, x_hi, core), frame: 8 (over x_lo, z).
Axes of the slice: x: 4 (x_hi: 2, x_lo: 2; x = x_hi * 2 + x_lo), y: 4, z: 4, core: 2. Of those that a mesh axis runs over, the one named last changes fastest.
Arguments:
- frames: bfloat16 [64, 8, 197, 768], P('dp', 'frame'), may hold values from -6 to 6
- cotangent: bfloat16 [64, 8, 197, 768], P('dp', 'frame'), may hold values from -6 to 6
- group_ids: int32 [64], replicated, may hold values from 0 to 31, as said below
- message_weight: bfloat16 [768, 768], replicated, may hold values from -0.21875 to 0.21875
- message_bias: bfloat16 [768], replicated, may hold values from -1.75 to 1.75
- message_gain: bfloat16 [768], replicated, may hold values from 0.099609375 to 1.8984375
- message_shift: bfloat16 [768], replicated, may hold values from -1.75 to 1.75
- message_project: bfloat16 [768, 2304], replicated, may hold values from -0.21875 to 0.21875
- message_project_bias: bfloat16 [1536], replicated, may hold values from -3 to 3
- message_output: bfloat16 [768, 768], replicated, may hold values from -0.4375 to 0.4375
- message_output_bias: bfloat16 [768], replicated, may hold values from -1.75 to 1.75
- first_gain: bfloat16 [768], replicated, may hold values from 0.099609375 to 1.8984375
- first_shift: bfloat16 [768], replicated, may hold values from -1.75 to 1.75
- attend_project: bfloat16 [768, 2304], replicated, may hold values from -0.21875 to 0.21875
- attend_project_bias: bfloat16 [1536], replicated, may hold values from -3 to 3
- attend_output: bfloat16 [768, 768], replicated, may hold values from -0.875 to 0.875
- attend_output_bias: bfloat16 [768], replicated, may hold values from -0.625 to 0.625
- second_gain: bfloat16 [768], replicated, may hold values from 0.099609375 to 1.8984375
- second_shift: bfloat16 [768], replicated, may hold values from -1.75 to 1.75
- expand_weight: bfloat16 [768, 3072], replicated, may hold values from -0.21875 to 0.21875
- expand_bias: bfloat16 [3072], replicated, may hold values from -1.75 to 1.75
- shrink_weight: bfloat16 [3072, 768], replicated, may hold values from -0.109375 to 0.109375
- shrink_bias: bfloat16 [768], replicated, may hold values from -0.625 to 0.625
Outputs:
- result: bfloat16 [64, 8, 197, 768], P('dp', 'frame')
- loss: float32 [], replicated
- pooled: float32 [64, 768], P('dp')
- delta_frames: bfloat16 [64, 8, 197, 768], P('dp', 'frame')
- delta_message_weight: float32 [768, 768], P(('dp', 'frame'))
- delta_message_bias: float32 [768], P(('dp', 'frame'))
- delta_message_gain: float32 [768], P(('dp', 'frame'))
- delta_message_shift: float32 [768], P(('dp', 'frame'))
- delta_message_project: float32 [768, 2304], P(('dp', 'frame'))
- delta_message_project_bias: float32 [1536], P(('dp', 'frame'))
- delta_message_output: float32 [768, 768], P(('dp', 'frame'))
- delta_message_output_bias: float32 [768], P(('dp', 'frame'))
- delta_first_gain: float32 [768], P(('dp', 'frame'))
- delta_first_shift: float32 [768], P(('dp', 'frame'))
- delta_attend_project: float32 [768, 2304], P(('dp', 'frame'))
- delta_attend_project_bias: float32 [1536], P(('dp', 'frame'))
- delta_attend_output: float32 [768, 768], P(('dp', 'frame'))
- delta_attend_output_bias: float32 [768], P(('dp', 'frame'))
- delta_second_gain: float32 [768], P(('dp', 'frame'))
- delta_second_shift: float32 [768], P(('dp', 'frame'))
- delta_expand_weight: float32 [768, 3072], P(('dp', 'frame'))
- delta_expand_bias: float32 [3072], P(('dp', 'frame'))
- delta_shrink_weight: float32 [3072, 768], P(('dp', 'frame'))
- delta_shrink_bias: float32 [768], P(('dp', 'frame'))
The draws below stay inside these ranges and needn't reach their ends.
Inputs may be any that keep to these rules, and one draw needn't show every extreme that they name: `group_ids`: each id from 0 to 31 names exactly two clips.
All inputs are finite; a program needn't handle non-finite values.
Results may differ from the reference program's by a relative error of at most 0.038.
Values may be sent and summed in bfloat16 or wider, within the bound.
A program may use at most 256 MiB of HBM per device.

```python
import jax
import jax.numpy as jnp
from jax import lax

D = 768
HEADS = 12
FF = 3072
PATCHES = 197
FRAMES = 8
CLIPS = 64


def draw_group_ids(key, part):
    key = jax.random.fold_in(key, 11)
    order = jax.random.permutation(key, CLIPS).astype(jnp.int32)
    pair_index = jnp.arange(CLIPS, dtype=jnp.int32) // 2
    return jnp.zeros((CLIPS,), jnp.int32).at[order].set(pair_index)


def steps_of(stream_key, shape, cuts, low, high):
    level = 1.0
    for position, blocks in cuts:
        heights = jax.random.uniform(jax.random.fold_in(jax.random.fold_in(stream_key, 6), position), (blocks,), jnp.float32, low / len(cuts), high / len(cuts))
        level = level * jnp.repeat(jnp.exp(heights), shape[position] // blocks).reshape((-1,) + (1,) * (len(shape) - 1 - position))
    return level


def scatter_about(stream_key, shape, scale, limit, shards=(), kind=jnp.bfloat16):
    array = jax.random.normal(stream_key, shape, jnp.float32) * scale
    if len(shards) > 0:
        array = steps_of(stream_key, shape, shards, -0.22, 0.18) * array
    return jnp.clip(array, min=-limit, max=limit).astype(kind)


def setup_inputs(seed: int = 0) -> dict:
    key_of = jax.random.split(jax.random.key(seed), 24)
    frames = scatter_about(key_of[0], (CLIPS, FRAMES, PATCHES, D), 1.0, 6.0, ((0, 16), (1, 8)))
    cotangent = scatter_about(key_of[1], (CLIPS, FRAMES, PATCHES, D), 1.0, 6.0, ((0, 16), (1, 8)))
    group_ids = draw_group_ids(jax.random.fold_in(key_of[23], 71), 0)
    message_weight = scatter_about(key_of[3], (D, D), D ** -0.5, 0.21875)
    message_bias = scatter_about(key_of[4], (D,), 0.3, 1.75)
    message_gain = jnp.clip(1.0 + 0.18 * jax.random.normal(key_of[5], (D,), jnp.float32), 0.099609375, 1.8984375).astype(jnp.bfloat16)
    message_shift = scatter_about(key_of[6], (D,), 0.3, 1.75)
    message_project = scatter_about(key_of[7], (D, 3 * D), D ** -0.5, 0.21875)
    message_project_bias = scatter_about(key_of[8], (2 * D,), 0.5, 3.0)
    message_output = scatter_about(key_of[9], (D, D), (D // 4) ** -0.5, 0.4375)
    message_output_bias = scatter_about(key_of[10], (D,), 0.3, 1.75)
    first_gain = jnp.clip(1.0 + 0.18 * jax.random.normal(key_of[11], (D,), jnp.float32), 0.099609375, 1.8984375).astype(jnp.bfloat16)
    first_shift = scatter_about(key_of[12], (D,), 0.3, 1.75)
    attend_project = scatter_about(key_of[13], (D, 3 * D), D ** -0.5, 0.21875)
    attend_project_bias = scatter_about(key_of[14], (2 * D,), 0.5, 3.0)
    attend_output = scatter_about(key_of[15], (D, D), (D // 16) ** -0.5, 0.875)
    attend_output_bias = scatter_about(key_of[16], (D,), 0.1, 0.625)
    second_gain = jnp.clip(1.0 + 0.18 * jax.random.normal(key_of[17], (D,), jnp.float32), 0.099609375, 1.8984375).astype(jnp.bfloat16)
    second_shift = scatter_about(key_of[18], (D,), 0.3, 1.75)
    expand_weight = scatter_about(key_of[19], (D, FF), D ** -0.5, 0.21875)
    expand_bias = scatter_about(key_of[20], (FF,), 0.3, 1.75)
    shrink_weight = scatter_about(key_of[21], (FF, D), FF ** -0.5, 0.109375)
    shrink_bias = scatter_about(key_of[22], (D,), 0.1, 0.625)
    return dict(frames=frames, cotangent=cotangent, group_ids=group_ids, message_weight=message_weight, message_bias=message_bias, message_gain=message_gain, message_shift=message_shift, message_project=message_project, message_project_bias=message_project_bias, message_output=message_output, message_output_bias=message_output_bias, first_gain=first_gain, first_shift=first_shift, attend_project=attend_project, attend_project_bias=attend_project_bias, attend_output=attend_output, attend_output_bias=attend_output_bias, second_gain=second_gain, second_shift=second_shift, expand_weight=expand_weight, expand_bias=expand_bias, shrink_weight=shrink_weight, shrink_bias=shrink_bias)


@jax.custom_vjp
def low(v):
    return lax.optimization_barrier(v.astype(jnp.bfloat16)).astype(jnp.float32)

@jax.custom_vjp
def low_back(v):
    return v

def low_keep(v):
    return (low(v), None)

def low_pass(kept, grad):
    return (grad,)

def back_keep(v):
    return (v, None)

def back_low(kept, grad):
    return (low(grad),)
low.defvjp(low_keep, low_pass)
low_back.defvjp(back_keep, back_low)

def precise_dot(left, right):
    return jnp.dot(left, right, precision=lax.Precision.HIGHEST, preferred_element_type=jnp.float32)

def norm_rows(value, gain, shift):
    row_mean = lax.optimization_barrier(jnp.mean(value, axis=-1, keepdims=True))
    centered = value - row_mean
    normed = centered * lax.rsqrt(lax.optimization_barrier(jnp.mean(centered * centered, axis=-1, keepdims=True)) + 1e-05)
    return normed * gain + shift

def soft_rows(scores):
    row_max = lax.optimization_barrier(jnp.max(scores, axis=-1, keepdims=True))
    exponent = jnp.exp(scores - row_max)
    return exponent / lax.optimization_barrier(jnp.sum(exponent, axis=-1, keepdims=True))

def log_total(scores):
    row_max = lax.optimization_barrier(jnp.max(scores, axis=-1, keepdims=True))
    return row_max[..., 0] + jnp.log(lax.optimization_barrier(jnp.sum(jnp.exp(scores - row_max), axis=-1)))

def attend(query, key_part, value_part):
    score_scale = query.shape[-1] ** (-0.5)
    scores = jnp.einsum('...qe,...ke->...qk', query, key_part, precision=lax.Precision.HIGHEST) * score_scale
    attn_probs = soft_rows(low_back(scores))
    return jnp.einsum('...qk,...ke->...qe', low(attn_probs), value_part, precision=lax.Precision.HIGHEST)

def clip_forward(clip_tokens, weights):
    message_weight, message_bias, message_gain, message_shift, message_project, message_project_bias, message_output, message_output_bias, first_gain, first_shift, attend_project, attend_project_bias, attend_output, attend_output_bias, second_gain, second_shift, expand_weight, expand_bias, shrink_weight, shrink_bias = weights
    frame_count, patch_count, model_width = clip_tokens.shape
    head_count = HEADS
    head_width = model_width // head_count
    zero_cols = jnp.zeros((model_width,), jnp.float32)
    msg_pre = low_back(precise_dot(clip_tokens[:, 0], message_weight) + message_bias)
    msg_norm = low(norm_rows(msg_pre, message_gain, message_shift))
    msg_bias_full = jnp.concatenate([message_project_bias[:model_width], zero_cols, message_project_bias[model_width:]])
    msg_qkv = low(low_back(precise_dot(msg_norm, message_project) + msg_bias_full))
    msg_qkv = msg_qkv.reshape(frame_count, 3, head_count, head_width).transpose(1, 2, 0, 3)
    msg_mixed = attend(msg_qkv[0], msg_qkv[1], msg_qkv[2])
    msg_mixed = low(low_back(msg_mixed.transpose(1, 0, 2).reshape(frame_count, model_width)))
    message = msg_pre + low_back(precise_dot(msg_mixed, message_output) + message_output_bias)
    joined = jnp.concatenate([clip_tokens, message[:, None, :]], axis=1)
    row_count = patch_count + 1
    first_normed = low(norm_rows(joined, first_gain, first_shift)).reshape(frame_count * row_count, model_width)
    attn_bias_full = jnp.concatenate([attend_project_bias[:model_width], zero_cols, attend_project_bias[model_width:]])
    projected = low(low_back(precise_dot(first_normed, attend_project) + attn_bias_full))
    projected = projected.reshape(frame_count, row_count, 3, head_count, head_width).transpose(2, 0, 3, 1, 4)
    mixed_rows = attend(projected[0], projected[1], projected[2])
    mixed_rows = low(low_back(mixed_rows.transpose(0, 2, 1, 3).reshape(frame_count * row_count, model_width)))
    branch_attn = low_back(precise_dot(mixed_rows, attend_output) + attend_output_bias)
    after_attend = joined + branch_attn.reshape(frame_count, row_count, model_width)
    residual = after_attend[:, :patch_count]
    second_normed = low(norm_rows(residual, second_gain, second_shift)).reshape(frame_count * patch_count, model_width)
    hidden_pre = low_back(precise_dot(second_normed, expand_weight) + expand_bias)
    hidden = low(hidden_pre * jax.nn.sigmoid(1.702 * hidden_pre))
    branch_out = low_back(precise_dot(hidden, shrink_weight) + shrink_bias)
    return residual + branch_out.reshape(frame_count, patch_count, model_width)

def forward_loss(inputs, weights, group_ids):

    def one_clip(clip_tokens):
        return clip_forward(clip_tokens, weights)
    layer_out = lax.map(jax.checkpoint(one_clip), inputs)
    pooled = lax.optimization_barrier(jnp.mean(layer_out[:, :, 0, :], axis=1))
    embed = pooled * lax.rsqrt(lax.optimization_barrier(jnp.sum(pooled * pooled, axis=-1, keepdims=True)) + 1e-06)
    sims = 50.0 * precise_dot(embed, embed.T)
    clip_count = sims.shape[0]
    diagonal_mask = lax.broadcasted_iota(jnp.int32, (clip_count, clip_count), 0) == lax.broadcasted_iota(jnp.int32, (clip_count, clip_count), 1)
    positive_mask = (group_ids[:, None] == group_ids[None, :]) & jnp.logical_not(diagonal_mask)
    all_terms = log_total(jnp.where(diagonal_mask, -10000.0, sims))
    pos_terms = log_total(jnp.where(positive_mask, sims, -10000.0))
    return ((layer_out, jnp.mean(all_terms - pos_terms)), pooled)

def reference(frames, cotangent, group_ids, message_weight, message_bias, message_gain, message_shift, message_project, message_project_bias, message_output, message_output_bias, first_gain, first_shift, attend_project, attend_project_bias, attend_output, attend_output_bias, second_gain, second_shift, expand_weight, expand_bias, shrink_weight, shrink_bias):
    params = tuple((weight.astype(jnp.float32) for weight in (message_weight, message_bias, message_gain, message_shift, message_project, message_project_bias, message_output, message_output_bias, first_gain, first_shift, attend_project, attend_project_bias, attend_output, attend_output_bias, second_gain, second_shift, expand_weight, expand_bias, shrink_weight, shrink_bias)))

    def objective(inputs, weights):
        return forward_loss(inputs, weights, group_ids)
    (layer_out, loss), pull, pooled = jax.vjp(objective, frames.astype(jnp.float32), params, has_aux=True)
    loss_weight = jnp.full((), CLIPS, jnp.float32)
    grad_inputs, grads = pull((cotangent.astype(jnp.float32), loss_weight))
    return (layer_out.astype(jnp.bfloat16), loss, pooled, grad_inputs.astype(jnp.bfloat16), grads[0], grads[1], grads[2], grads[3], grads[4], grads[5], grads[6], grads[7], grads[8], grads[9], grads[10], grads[11], grads[12], grads[13], grads[14], grads[15], grads[16], grads[17], grads[18], grads[19])
```

```python
import functools

import jax
import jax.numpy as jnp
import numpy as np
from jax import lax
from jax.experimental import pallas as pl
from jax.experimental.pallas import tpu as pltpu
from jax.sharding import PartitionSpec as P

f32, low = jnp.float32, jnp.bfloat16
CLIPS_HERE, PATCH, ROWS, D, FF = 4, 197, 208, 768, 3072
ALL = CLIPS_HERE * ROWS
BIG = 58 * 2**20
(R_MB, R_MG, R_MS, R_MPB, R_MOB, R_FG, R_FS, R_APB, R_AOB, R_SG, R_SS, R_EB, R_SB) = (
    0, 1, 2, 3, 6, 7, 8, 9, 12, 13, 14, 15, 19)


def dot(a, b):
    return jnp.dot(a, b, preferred_element_type=f32)


def dot_t(a, b):
    return lax.dot_general(a, b, (((1,), (1,)), ((), ())), preferred_element_type=f32)


def dot_tl(a, b):
    return lax.dot_general(a, b, (((0,), (0,)), ((), ())), preferred_element_type=f32)


def stats(x):
    mean = jnp.mean(x, axis=-1, keepdims=True)
    centered = x - mean
    inv = lax.rsqrt(jnp.mean(centered * centered, axis=-1, keepdims=True) + 1e-05)
    return centered * inv, inv


def norm_back(grad, u, inv, gain):
    h = grad * gain
    return (h - jnp.mean(h, axis=-1, keepdims=True) - u * jnp.mean(h * u, axis=-1, keepdims=True)) * inv


def attend_kernel(frames, message, vec, wp, wo, first_low, proj, probs, mixed, resid, second_low, xs):
    clip = pl.program_id(0)
    xs[pl.ds(192, 16)] = jnp.zeros((16, D), f32)
    xs[pl.ds(0, PATCH)] = frames[0, 0].astype(f32)
    xs[pl.ds(PATCH, 1)] = message[pl.ds(clip, 1)]
    x = xs[...]
    u, _ = stats(x)
    normed = (u * vec[R_FG : R_FG + 1] + vec[R_FS : R_FS + 1]).astype(low)
    first_low[...] = normed
    for j in range(3):
        part = dot(normed, wp[:, j * D : (j + 1) * D]) + vec[R_APB + j : R_APB + j + 1]
        proj[:, j * D : (j + 1) * D] = part.astype(low)
    lane = lax.broadcasted_iota(jnp.int32, (ROWS, 128), 1)
    keep = lax.broadcasted_iota(jnp.int32, (ROWS, ROWS), 1) < PATCH + 1
    zero = jnp.zeros((), low)
    for pair in range(6):
        q = proj[:, pair * 128 : pair * 128 + 128]
        k = proj[:, D + pair * 128 : D + pair * 128 + 128]
        v = proj[:, 2 * D + pair * 128 : 2 * D + pair * 128 + 128]
        outs = []
        for half in range(2):
            mine = (lane < 64) if half == 0 else (lane >= 64)
            s = dot_t(jnp.where(mine, q, zero), k) * 0.125
            s = jnp.where(keep, s, -1e30)
            e = jnp.exp(s - jnp.max(s, axis=-1, keepdims=True))
            p = (e * (1.0 / jnp.sum(e, axis=-1, keepdims=True))).astype(low)
            probs[0, 2 * pair + half] = p
            outs.append(dot(p, v))
        mixed[:, pair * 128 : pair * 128 + 128] = jnp.where(lane < 64, outs[0], outs[1]).astype(low)
    after = x + (dot(mixed[...], wo[...]) + vec[R_AOB : R_AOB + 1])
    resid[...] = after
    u2, _ = stats(after)
    second_low[...] = (u2 * vec[R_SG : R_SG + 1] + vec[R_SS : R_SS + 1]).astype(low)


def const(shape):
    return pl.BlockSpec(shape, lambda *i: (0,) * len(shape))


def attend_forward(frames, message, vec, wp, wo):
    row = lambda w: pl.BlockSpec((ROWS, w), lambda c: (c, 0))
    return pl.pallas_call(
        attend_kernel,
        grid=(CLIPS_HERE,),
        in_specs=[pl.BlockSpec((1, 1, PATCH, D), lambda c: (c, 0, 0, 0)), const((8, D)), const((24, D)),
                  const((D, 3 * D)), const((D, D))],
        out_specs=[row(D), row(3 * D), pl.BlockSpec((1, 12, ROWS, ROWS), lambda c: (c, 0, 0, 0)), row(D), row(D), row(D)],
        out_shape=[jax.ShapeDtypeStruct((ALL, D), low), jax.ShapeDtypeStruct((ALL, 3 * D), low),
                   jax.ShapeDtypeStruct((CLIPS_HERE, 12, ROWS, ROWS), low), jax.ShapeDtypeStruct((ALL, D), low),
                   jax.ShapeDtypeStruct((ALL, D), f32), jax.ShapeDtypeStruct((ALL, D), low)],
        scratch_shapes=[pltpu.VMEM((ROWS, D), f32)],
        compiler_params=pltpu.CompilerParams(vmem_limit_bytes=BIG),
        name="attend_forward",
    )(frames, message, vec, wp, wo)


def mlp_kernel(second_low, resid, vec, we, ws, hidden, dgate, result, cls, acc):
    j = pl.program_id(0)

    @pl.when(j == 0)
    def _():
        acc[...] = resid[...] + vec[R_SB : R_SB + 1]

    bias = vec[pl.ds(R_EB + j, 1)]
    for c in range(CLIPS_HERE):
        rows = pl.ds(c * ROWS, ROWS)
        h = dot(second_low[rows], we[...]) + bias
        sg = 1.0 / (1.0 + jnp.exp(-1.702 * h))
        hs = h * sg
        hid = hs.astype(low)
        hidden[rows] = hid
        dgate[rows] = (sg + 1.702 * hs * (1.0 - sg)).astype(low)
        acc[rows] += dot(hid, ws[...])

    @pl.when(j == 3)
    def _():
        cls[...] = jnp.zeros((8, D), f32)
        for c in range(CLIPS_HERE):
            result[c, 0] = acc[pl.ds(c * ROWS, PATCH)].astype(low)
            cls[pl.ds(c, 1)] = acc[pl.ds(c * ROWS, 1)]


def mlp_forward(second_low, resid, vec, we, ws):
    tile = pl.BlockSpec((ALL, D), lambda j: (0, j))
    return pl.pallas_call(
        mlp_kernel,
        grid=(4,),
        in_specs=[const((ALL, D)), const((ALL, D)), const((24, D)), pl.BlockSpec((D, D), lambda j: (0, j)),
                  pl.BlockSpec((D, D), lambda j: (j, 0))],
        out_specs=[tile, tile, const((CLIPS_HERE, 1, PATCH, D)), const((8, D))],
        out_shape=[jax.ShapeDtypeStruct((ALL, FF), low), jax.ShapeDtypeStruct((ALL, FF), low),
                   jax.ShapeDtypeStruct((CLIPS_HERE, 1, PATCH, D), low), jax.ShapeDtypeStruct((8, D), f32)],
        scratch_shapes=[pltpu.VMEM((ALL, D), f32)],
        compiler_params=pltpu.CompilerParams(vmem_limit_bytes=BIG),
        name="mlp_forward",
    )(second_low, resid, vec, we, ws)


def unit_order():
    row = np.arange(D)
    source = row % 192 // 6 * 24 + row // 192 * 6 + row % 6
    return (source[:, None] == np.arange(D)[None, :]).astype(np.float32)


def mlp_back_kernel(cot, gpool, vec, hidden, dgate, second_low, we, ws, resid, turn,
                    d_shrink, d_expand, after, sums, gl, gb, st, gsec):
    j = pl.program_id(0)

    @pl.when(j == 0)
    def _():
        gl[...] = jnp.zeros((ALL, D), f32)
        for c in range(CLIPS_HERE):
            gl[pl.ds(c * ROWS, PATCH)] = cot[c, 0].astype(f32)
            gl[pl.ds(c * ROWS, 1)] += gpool[pl.ds(c, 1)]
        gb[...] = gl[...].astype(low)
        gsec[...] = jnp.zeros((ALL, D), f32)
        rows = lax.broadcasted_iota(jnp.int32, (D, D), 0)
        cols = lax.broadcasted_iota(jnp.int32, (D, D), 1)
        eye = (rows == cols).astype(low)
        st[...] = dot_t(eye, second_low[...]).astype(low)
        sums[...] = jnp.zeros((24, D), f32)
        sums[11:12] = jnp.sum(gb[...].astype(f32), axis=0, keepdims=True)

    hid_t = dot_t(turn[...], hidden[...]).astype(low)
    tile = dot(hid_t, gb[...]).astype(low)
    for q in range(4):
        d_shrink[:, q * D : (q + 1) * D] = tile[q * 192 : (q + 1) * 192]
    ghp = (dot_t(gb[...], ws[...]) * dgate[...].astype(f32)).astype(low)
    sums[pl.ds(7 + j, 1)] = jnp.sum(ghp.astype(f32), axis=0, keepdims=True)
    d_expand[...] = dot(st[...], ghp).astype(low)
    gsec[...] += dot_t(ghp, we[...])

    @pl.when(j == 3)
    def _():
        gain = vec[R_SG : R_SG + 1]
        total = [jnp.zeros((1, D), f32) for _ in range(3)]
        for c in range(CLIPS_HERE):
            rows = pl.ds(c * ROWS, ROWS)
            u, inv = stats(resid[rows])
            g = gsec[rows]
            out = gl[rows] + norm_back(g, u, inv, gain)
            after[rows] = out
            total[0] += jnp.sum(g * u, axis=0, keepdims=True)
            total[1] += jnp.sum(g, axis=0, keepdims=True)
            total[2] += jnp.sum(out.astype(low).astype(f32), axis=0, keepdims=True)
        sums[5:6] = total[0]
        sums[6:7] = total[1]
        sums[4:5] = total[2]


def mlp_back(cot, gpool, vec, hidden, dgate, second_low, we, ws, resid):
    tile = pl.BlockSpec((ALL, D), lambda j: (0, j))
    turn = jnp.asarray(unit_order(), low)
    return pl.pallas_call(
        mlp_back_kernel,
        grid=(4,),
        in_specs=[const((CLIPS_HERE, 1, PATCH, D)), const((8, D)), const((24, D)), tile, tile, const((ALL, D)),
                  pl.BlockSpec((D, D), lambda j: (0, j)), pl.BlockSpec((D, D), lambda j: (j, 0)), const((ALL, D)),
                  const((D, D))],
        out_specs=[pl.BlockSpec((192, FF), lambda j: (j, 0)), pl.BlockSpec((D, D), lambda j: (0, j)), const((ALL, D)),
                   const((24, D))],
        out_shape=[jax.ShapeDtypeStruct((D, FF), low), jax.ShapeDtypeStruct((D, FF), low),
                   jax.ShapeDtypeStruct((ALL, D), f32), jax.ShapeDtypeStruct((24, D), f32)],
        scratch_shapes=[pltpu.VMEM((ALL, D), f32), pltpu.VMEM((ALL, D), low), pltpu.VMEM((D, ALL), low),
                        pltpu.VMEM((ALL, D), f32)],
        compiler_params=pltpu.CompilerParams(vmem_limit_bytes=BIG),
        name="mlp_back",
    )(cot, gpool, vec, hidden, dgate, second_low, we, ws, resid, turn)


def attend_back_kernel(after, proj, probs, frames, message, vec, wp, wo, sums_in,
                       gproj, tokens, cls, gmsg, sums, xs):
    clip = pl.program_id(0)

    @pl.when(clip == 0)
    def _():
        sums[...] = sums_in[...]
        cls[...] = jnp.zeros((8, D), f32)
        gmsg[...] = jnp.zeros((8, D), f32)

    xs[pl.ds(192, 16)] = jnp.zeros((16, D), f32)
    xs[pl.ds(0, PATCH)] = frames[0, 0].astype(f32)
    xs[pl.ds(PATCH, 1)] = message[pl.ds(clip, 1)]
    u, inv = stats(xs[...])
    gm_all = dot_t(after[...].astype(low), wo[...]).astype(low)
    lane = lax.broadcasted_iota(jnp.int32, (ROWS, 128), 1)
    zero = jnp.zeros((), low)
    for pair in range(6):
        cols = slice(pair * 128, pair * 128 + 128)
        q = proj[:, pair * 128 : pair * 128 + 128]
        k = proj[:, D + pair * 128 : D + pair * 128 + 128]
        v = proj[:, 2 * D + pair * 128 : 2 * D + pair * 128 + 128]
        gm = gm_all[:, cols]
        outs = []
        for half in range(2):
            mine = (lane < 64) if half == 0 else (lane >= 64)
            dp = dot_t(jnp.where(mine, gm, zero), v)
            p_low = probs[0, 2 * pair + half]
            p = p_low.astype(f32)
            gs = (p * (dp - jnp.sum(dp * p, axis=-1, keepdims=True))).astype(low)
            outs.append((dot(gs, k), dot_tl(gs, q), dot_tl(p_low, gm)))
        for n, scale in ((0, 0.125), (1, 0.125), (2, 1.0)):
            both = jnp.where(lane < 64, outs[0][n], outs[1][n]) * scale
            gproj[:, n * D + pair * 128 : n * D + pair * 128 + 128] = both.astype(low)
    grad = jnp.zeros((ROWS, D), f32)
    for n in range(3):
        part = gproj[:, n * D : (n + 1) * D]
        grad += dot_t(part, wp[:, n * D : (n + 1) * D])
        if n != 1:
            at = 2 if n == 0 else 3
            sums[at : at + 1] += jnp.sum(part.astype(f32), axis=0, keepdims=True)
    sums[0:1] += jnp.sum(grad * u, axis=0, keepdims=True)
    sums[1:2] += jnp.sum(grad, axis=0, keepdims=True)
    xs[...] = after[...] + norm_back(grad, u, inv, vec[R_FG : R_FG + 1])
    tokens[0, 0] = xs[pl.ds(0, PATCH)].astype(low)
    cls[pl.ds(clip, 1)] = xs[pl.ds(0, 1)]
    gmsg[pl.ds(clip, 1)] = xs[pl.ds(PATCH, 1)]


def attend_back(after, proj, probs, frames, message, vec, wp, wo, sums):
    row = lambda w: pl.BlockSpec((ROWS, w), lambda c: (c, 0))
    item = pl.BlockSpec((1, 1, PATCH, D), lambda c: (c, 0, 0, 0))
    return pl.pallas_call(
        attend_back_kernel,
        grid=(CLIPS_HERE,),
        in_specs=[row(D), row(3 * D), pl.BlockSpec((1, 12, ROWS, ROWS), lambda c: (c, 0, 0, 0)), item, const((8, D)),
                  const((24, D)), const((D, 3 * D)), const((D, D)), const((24, D))],
        out_specs=[row(3 * D), item, const((8, D)), const((8, D)), const((24, D))],
        out_shape=[jax.ShapeDtypeStruct((ALL, 3 * D), low), jax.ShapeDtypeStruct((CLIPS_HERE, 1, PATCH, D), low),
                   jax.ShapeDtypeStruct((8, D), f32), jax.ShapeDtypeStruct((8, D), f32),
                   jax.ShapeDtypeStruct((24, D), f32)],
        scratch_shapes=[pltpu.VMEM((ROWS, D), f32)],
        compiler_params=pltpu.CompilerParams(vmem_limit_bytes=BIG),
        name="attend_back",
    )(after, proj, probs, frames, message, vec, wp, wo, sums)


def attend_weights_kernel(first_low, gproj, mixed, after, d_first, d_second, turned):
    j = pl.program_id(0)
    rows = lax.broadcasted_iota(jnp.int32, (D, D), 0)
    cols = lax.broadcasted_iota(jnp.int32, (D, D), 1)
    eye = (rows == cols).astype(low)

    @pl.when(j == 0)
    def _():
        turned[...] = dot_t(eye, first_low[...]).astype(low)

    @pl.when(j < 2)
    def _():
        d_first[...] = dot(turned[...], gproj[...]).astype(low)

    @pl.when(j == 2)
    def _():
        d_second[...] = dot(turned[...], gproj[...]).astype(low)

    @pl.when(j == 3)
    def _():
        turned[...] = dot_t(eye, mixed[...]).astype(low)
        d_second[...] = dot(turned[...], after[...].astype(low)).astype(low)


def attend_weights(first_low, gproj, mixed, after):
    return pl.pallas_call(
        attend_weights_kernel,
        grid=(4,),
        in_specs=[const((ALL, D)), pl.BlockSpec((ALL, D), lambda j: (0, jnp.minimum(j, 2))), const((ALL, D)),
                  const((ALL, D))],
        out_specs=[pl.BlockSpec((D, D), lambda j: (0, jnp.minimum(j, 1))),
                   pl.BlockSpec((D, D), lambda j: (0, jnp.maximum(j - 2, 0)))],
        out_shape=[jax.ShapeDtypeStruct((D, 2 * D), low), jax.ShapeDtypeStruct((D, 2 * D), low)],
        scratch_shapes=[pltpu.VMEM((D, ALL), low)],
        compiler_params=pltpu.CompilerParams(vmem_limit_bytes=BIG),
        name="attend_weights",
    )(first_low, gproj, mixed, after)


MESH = pl.DeviceIdType.MESH


def flip_low(index):
    return index + 1 - 2 * (index % 2)


def flip_pair(index, high, low):
    index = 3 - index if high else index
    return flip_low(index) if low else index


def place():
    dp, fr = lax.axis_index("dp"), lax.axis_index("frame")
    return dict(y=dp // 4, x=(dp // 2 % 2) * 2 + fr // 4, z=fr % 4, c=dp % 2)


def moved(at, bits):
    return dict(
        y=flip_pair(at["y"], bits.get("yu"), bits.get("yv")),
        x=flip_pair(at["x"], bits.get("xu"), bits.get("xv")),
        z=flip_pair(at["z"], bits.get("zu"), bits.get("zv")),
        c=1 - at["c"] if bits.get("c") else at["c"],
    )


def dp_of(at):
    return at["y"] * 4 + (at["x"] // 2) * 2 + at["c"]


def frame_of(at):
    return (at["x"] % 2) * 4 + at["z"]


def device_of(at):
    return (dp_of(at), frame_of(at))


CLIP_DIMS = ("yu", "yv", "xu")
FRAME_DIMS = ("xv", "zu", "zv")


def rotated(dims, turn):
    return dims[turn:] + dims[:turn]


def bits_at(dims, position):
    return {dims[k]: (position >> (2 - k)) & 1 for k in range(3)}


def spread_matrices():
    at = place()
    rows = lax.broadcasted_iota(jnp.int32, (128, 48), 0)
    cols = lax.broadcasted_iota(jnp.int32, (128, 48), 1)
    out = {}
    for name, dims in (("a", FRAME_DIMS), ("b", CLIP_DIMS)):
        mats = []
        for turn in range(3):
            block = jnp.zeros((128, 48), jnp.int32)
            for position in range(8):
                to = moved(at, bits_at(rotated(dims, turn), position))
                value = frame_of(to) if name == "a" else dp_of(to) // 2
                block = jnp.where(rows // 16 == position, value, block)
            for half in range(2):
                inner = rows % 16 - 8 * half
                hit = (cols == block * 6 + inner) & (inner >= 0) & (inner < 6)
                mats.append(hit.astype(jnp.bfloat16))
        out[name] = jnp.stack(mats)
    rows = lax.broadcasted_iota(jnp.int32, (3, 384, 384), 1)
    cols = lax.broadcasted_iota(jnp.int32, (3, 384, 384), 2)
    turns = lax.broadcasted_iota(jnp.int32, (3, 384, 384), 0)
    position, chunk, inner = rows // 48, rows % 48 // 6, rows % 6
    source = jnp.zeros((3, 384, 384), jnp.int32)
    skew = (chunk + at["x"] // 2) % 2
    for turn in range(3):
        for p in range(8):
            to = moved(at, bits_at(rotated(FRAME_DIMS, turn), p))
            xl, z = to["x"] % 2, to["z"]
            frame = ((xl + skew) % 2) * 4 + z
            source = jnp.where((position == p) & (turns == turn), frame, source)
    out["mix"] = (cols == chunk * 48 + source * 6 + inner).astype(jnp.bfloat16)
    return out


def to_units(full):
    return full.reshape(8, 2, 48, full.shape[-1])


FRAMES = 8
SLOT = 8
MROWS = FRAMES * SLOT
SUMS = 24


def greet(partners):
    barrier = pltpu.get_barrier_semaphore()
    for partner in partners:
        pl.semaphore_signal(barrier, inc=1, device_id=partner, device_id_type=MESH)
    pl.semaphore_wait(barrier, len(partners))


def frame_partners():
    dp, fr = lax.axis_index("dp"), lax.axis_index("frame")
    return [(dp, lax.rem(fr + k, FRAMES)) for k in range(1, FRAMES)]


def remote(src, dst, send_sem, recv_sem, device):
    copy = pltpu.make_async_remote_copy(
        src_ref=src, dst_ref=dst, send_sem=send_sem, recv_sem=recv_sem, device_id=device, device_id_type=MESH)
    copy.start()
    return copy


def same_clip():
    rows = lax.broadcasted_iota(jnp.int32, (MROWS, MROWS), 0)
    cols = lax.broadcasted_iota(jnp.int32, (MROWS, MROWS), 1)
    return rows % SLOT == cols % SLOT


def soft(s):
    e = jnp.exp(s - jnp.max(s, axis=-1, keepdims=True))
    return e / jnp.sum(e, axis=-1, keepdims=True)


def message_kernel(cls, vec, mw, mp, mo, message, all_cls, pre_out, normed_out, qkv, mixed,
                   vw, vp, vo, load_sem, send_sem, recv_sem):
    fr = lax.axis_index("frame")
    loads = [pltpu.make_async_copy(s, d, load_sem.at[n]) for n, (s, d) in enumerate(((mw, vw), (mp, vp), (mo, vo)))]
    for load in loads:
        load.start()
    partners = frame_partners()
    greet(partners)
    copies = [remote(cls, all_cls.at[fr], send_sem.at[k], recv_sem.at[k], partner)
              for k, partner in enumerate(partners)]
    all_cls[fr] = cls[...]
    loads[0].wait()
    for copy in copies:
        copy.wait_recv()
    x = all_cls[...].reshape(MROWS, D).astype(low)
    pre = dot(x, vw[...]) + vec[R_MB : R_MB + 1]
    pre_out[...] = pre
    u, _ = stats(pre)
    normed = (u * vec[R_MG : R_MG + 1] + vec[R_MS : R_MS + 1]).astype(low)
    normed_out[...] = normed
    loads[1].wait()
    for j in range(3):
        qkv[:, j * D : (j + 1) * D] = (dot(normed, vp[:, j * D : (j + 1) * D]) + vec[R_MPB + j : R_MPB + j + 1]).astype(low)
    keep = same_clip()
    lane = lax.broadcasted_iota(jnp.int32, (MROWS, 128), 1)
    zero = jnp.zeros((), low)
    for pair in range(6):
        q = qkv[:, pair * 128 : pair * 128 + 128]
        k = qkv[:, D + pair * 128 : D + pair * 128 + 128]
        v = qkv[:, 2 * D + pair * 128 : 2 * D + pair * 128 + 128]
        outs = []
        for half in range(2):
            mine = (lane < 64) if half == 0 else (lane >= 64)
            s = jnp.where(keep, dot_t(jnp.where(mine, q, zero), k) * 0.125, -1e30)
            outs.append(dot(soft(s).astype(low), v))
        mixed[:, pair * 128 : pair * 128 + 128] = jnp.where(lane < 64, outs[0], outs[1]).astype(low)
    loads[2].wait()
    every = pre + dot(mixed[...], vo[...]) + vec[R_MOB : R_MOB + 1]
    rows = lax.broadcasted_iota(jnp.int32, (MROWS, 1), 0) // SLOT
    every = jnp.where(rows == fr, every, 0.0)
    message[...] = jnp.sum(every.reshape(FRAMES, SLOT, D), axis=0)
    for copy in copies:
        copy.wait_send()


def message_forward(cls, vec, mw, mp, mo):
    vmem = pl.BlockSpec(memory_space=pltpu.VMEM)
    any_spec = pl.BlockSpec(memory_space=pl.ANY)
    S = jax.ShapeDtypeStruct
    return pl.pallas_call(
        message_kernel,
        in_specs=[vmem, vmem, any_spec, any_spec, any_spec],
        out_specs=[vmem] * 6,
        out_shape=[S((SLOT, D), f32), S((FRAMES, SLOT, D), f32), S((MROWS, D), f32), S((MROWS, D), low),
                   S((MROWS, 3 * D), low), S((MROWS, D), low)],
        scratch_shapes=[pltpu.VMEM((D, D), low), pltpu.VMEM((D, 3 * D), low), pltpu.VMEM((D, D), low),
                        pltpu.SemaphoreType.DMA((3,)), pltpu.SemaphoreType.DMA((7,)), pltpu.SemaphoreType.DMA((7,))],
        compiler_params=pltpu.CompilerParams(collective_id=0, has_side_effects=True, vmem_limit_bytes=BIG),
        name="message_forward",
    )(cls, vec, mw, mp, mo)


PRECISE = lax.Precision.HIGHEST


def loss_kernel(cls, gid_col, gid_row, loss, pooled_out, gpool, cur, got, every, natural, grads, send_sem, recv_sem):
    at = place()
    order = FRAME_DIMS + ("c",) + CLIP_DIMS
    partner = {d: device_of(moved(at, {d: 1})) for d in order}
    greet([partner[d] for d in order])
    s = cls[...]
    copies = []
    for k, d in enumerate(FRAME_DIMS):
        cur[k] = s
        copy = remote(cur.at[k], got.at[k], send_sem.at[k], recv_sem.at[k], partner[d])
        copies.append(copy)
        copy.wait_recv()
        s = s + got[k]
    pooled = s * 0.125
    pooled_out[...] = pooled
    inv_len = lax.rsqrt(jnp.sum(pooled * pooled, axis=-1, keepdims=True) + 1e-06)
    every[0] = pooled * inv_len
    for k, d in enumerate(order[3:]):
        copy = remote(every.at[pl.ds(0, 2**k)], every.at[pl.ds(2**k, 2**k)], send_sem.at[3 + k], recv_sem.at[3 + k],
                      partner[d])
        copies.append(copy)
        copy.wait_recv()
    for p in range(16):
        to = moved(at, {d: (p >> k) & 1 for k, d in enumerate(order[3:])})
        natural[dp_of(to)] = every[p]
    n = natural[...].reshape(128, D)
    sims = 50.0 * lax.dot_general(n, n, (((1,), (1,)), ((), ())), precision=PRECISE, preferred_element_type=f32)
    rows = lax.broadcasted_iota(jnp.int32, (128, 128), 0)
    cols = lax.broadcasted_iota(jnp.int32, (128, 128), 1)
    here = cols % SLOT < CLIPS_HERE
    other = here & (rows != cols)
    same = other & (gid_col[...] == gid_row[...])
    valid = lax.broadcasted_iota(jnp.int32, (128, 1), 0) % SLOT < CLIPS_HERE

    def log_soft(logits):
        top = jnp.max(logits, axis=-1, keepdims=True)
        e = jnp.exp(logits - top)
        total = jnp.sum(e, axis=-1, keepdims=True)
        return top + jnp.log(total), e / total

    all_log, all_p = log_soft(jnp.where(other, sims, -1e30))
    pos_log, pos_p = log_soft(jnp.where(same, sims, -1e30))
    terms = jnp.where(valid, all_log - pos_log, 0.0)
    loss[...] = jnp.broadcast_to(jnp.sum(terms, axis=0, keepdims=True) * (1.0 / 64.0), (8, 128))
    gs = jnp.where(valid & here, all_p - pos_p, 0.0)
    grad_all = 50.0 * jnp.dot(gs + gs.T, n, precision=PRECISE, preferred_element_type=f32)
    grads[...] = grad_all.reshape(16, SLOT, D)
    g = grads[lax.axis_index("dp")]
    back = inv_len * g - inv_len * inv_len * inv_len * pooled * jnp.sum(pooled * g, axis=-1, keepdims=True)
    gpool[...] = back * 0.125
    for copy in copies:
        copy.wait_send()


def loss_step(cls, gid_col, gid_row):
    vmem = pl.BlockSpec(memory_space=pltpu.VMEM)
    S = jax.ShapeDtypeStruct
    return pl.pallas_call(
        loss_kernel,
        in_specs=[vmem] * 3,
        out_specs=[vmem] * 3,
        out_shape=[S((8, 128), f32), S((SLOT, D), f32), S((SLOT, D), f32)],
        scratch_shapes=[pltpu.VMEM((3, SLOT, D), f32), pltpu.VMEM((3, SLOT, D), f32), pltpu.VMEM((16, SLOT, D), f32),
                        pltpu.VMEM((16, SLOT, D), f32), pltpu.VMEM((16, SLOT, D), f32),
                        pltpu.SemaphoreType.DMA((7,)), pltpu.SemaphoreType.DMA((7,))],
        compiler_params=pltpu.CompilerParams(collective_id=1, has_side_effects=True, vmem_limit_bytes=BIG),
        name="loss_step",
    )(cls, gid_col, gid_row)


def pick_table():
    at = place()
    row = jnp.arange(96)
    c, chunk, i = row // 48, row % 48 // 6, row % 6
    y, xh = chunk // 2, chunk % 2
    x_low = (at["x"] % 2 + at["x"] // 2 + xh) % 2
    block = (y * 4 + xh * 2 + c) * 8 + x_low * 4 + at["z"]
    picks = [block * 6 + i]
    picks += [block % 32 * 24 + q * 6 + i for q in range(4)]
    picks += [block % 64 * 12 + q * 6 + i for q in range(2)]
    part = jnp.stack([block // 32, block // 64] * 4, axis=1)
    return jnp.concatenate(picks)[:, None], part


def message_back(at, cls_all, pre, normed, qkv, mixed, vec, vw, vp, vo, gall, sums, pick, part, mgrad, gcls):
    fr = lax.axis_index("frame")
    g = gall[...].reshape(MROWS, D)
    g_low = g.astype(low)
    gmm = dot_t(g_low, vo[...]).astype(low)
    keep = same_clip()
    lane = lax.broadcasted_iota(jnp.int32, (MROWS, 128), 1)
    zero = jnp.zeros((), low)
    parts = ([], [], [])
    for pair in range(6):
        q = qkv[:, pair * 128 : pair * 128 + 128]
        k = qkv[:, D + pair * 128 : D + pair * 128 + 128]
        v = qkv[:, 2 * D + pair * 128 : 2 * D + pair * 128 + 128]
        gm = gmm[:, pair * 128 : pair * 128 + 128]
        outs = []
        for half in range(2):
            mine = (lane < 64) if half == 0 else (lane >= 64)
            p = soft(jnp.where(keep, dot_t(jnp.where(mine, q, zero), k) * 0.125, -1e30))
            dp = dot_t(jnp.where(mine, gm, zero), v)
            gs = (p * (dp - jnp.sum(dp * p, axis=-1, keepdims=True))).astype(low)
            outs.append((dot(gs, k), dot_tl(gs, q), dot_tl(p.astype(low), gm)))
        for n, scale in ((0, 0.125), (1, 0.125), (2, 1.0)):
            parts[n].append((jnp.where(lane < 64, outs[0][n], outs[1][n]) * scale).astype(low))
    gq, gk, gv = (jnp.concatenate(part, axis=1) for part in parts)
    gnorm = dot_t(gq, vp[:, :D]) + dot_t(gk, vp[:, D : 2 * D]) + dot_t(gv, vp[:, 2 * D :])
    u, inv = stats(pre[...])
    gpre = (g + norm_back(gnorm, u, inv, vec[R_MG : R_MG + 1])).astype(low)

    def total(value):
        return jnp.sum(value.astype(f32), axis=0, keepdims=True)

    table = jnp.concatenate(
        [sums[0:12], total(gpre), total(gnorm * u), total(gnorm), total(gq), total(gv), total(g_low),
         jnp.zeros((SUMS - 18, D), f32)], axis=0).astype(low)
    column = lax.broadcasted_iota(jnp.int32, (672, D), 1)
    choose = (column == pick[...]).astype(low)
    mine = choose[:96]
    x = cls_all[...].reshape(MROWS, D).astype(low)
    for unit, (left, right) in enumerate(((x, gpre), (normed[...], gq), (normed[...], gk), (normed[...], gv),
                                          (mixed[...], g_low))):
        turned = dot_t(mine, left).astype(low)
        mgrad[:, :, unit * D : (unit + 1) * D] = dot(turned, right).astype(low).reshape(2, 48, D)
    z = dot_t(choose, table)
    wide = lax.broadcasted_iota(jnp.int32, (96, 128), 1)
    narrow = lax.broadcasted_iota(jnp.int32, (96, SUMS), 1)
    out = jnp.zeros((96, 128), f32)
    out += jnp.concatenate([z[:96], jnp.zeros((96, 128 - SUMS), f32)], axis=1)
    for q in range(4):
        hit = narrow == 7 + part[:, 0:1]
        value = jnp.sum(jnp.where(hit, z[96 * (1 + q) : 96 * (2 + q)], 0.0), axis=-1, keepdims=True)
        out = jnp.where(wide == 24 + q, value, out)
    for q in range(2):
        for n, first in enumerate((2, 15)):
            hit = narrow == first + part[:, 1:2]
            value = jnp.sum(jnp.where(hit, z[96 * (5 + q) : 96 * (6 + q)], 0.0), axis=-1, keepdims=True)
            out = jnp.where(wide == 28 + 2 * n + q, value, out)
    mgrad[:, :, 5 * D : 5 * D + 128] = out.astype(low).reshape(2, 48, 128)
    mgrad[:, :, 5 * D + 128 :] = jnp.zeros((2, 48, D - 128), low)
    back = dot_t(gpre, vw[...])
    rows = lax.broadcasted_iota(jnp.int32, (MROWS, 1), 0) // SLOT
    gcls[...] = jnp.sum(jnp.where(rows == fr, back, 0.0).reshape(FRAMES, SLOT, D), axis=0)


PARTS = (("a", 0, 0), ("b", 1, 0), ("a", 0, 1), ("b", 1, 1), ("a", 2, 0), ("b", 3, 0), ("m", 4, 0), ("m", 4, 1), ("m", 4, 2))


def sums_kernel(*refs):
    (e_ref, s_ref, p_ref, o_ref, sa, sb, mix, gmsg, sums, cls_all, pre, normed, qkv, mixed, vec, pick, part,
     mw, mp, mo, tok_cls, out, new_cls, own, got, acc, r1, r2, r3, t, u1, u2, u3, mgrad, mgot, vw, vp, vo,
     gall, sall, stot, load_sem, local_sem, send_sem, recv_sem, near_send, near_recv) = refs
    at = place()
    fr = lax.axis_index("frame")
    loads = [pltpu.make_async_copy(s, d, load_sem.at[n]) for n, (s, d) in enumerate(((mo, vo), (mp, vp), (mw, vw)))]
    for load in loads:
        load.start()
    around = frame_partners()
    partners = {d: device_of(moved(at, {d: 1})) for d in ("c",) + CLIP_DIMS + FRAME_DIMS}
    far = [partners[d] for d in ("c", "yu", "yv", "xu")]
    greet(around + far)
    near = []
    for k, partner in enumerate(around):
        near.append(remote(gmsg, gall.at[fr], near_send.at[0, k], near_recv.at[0, k], partner))
        near.append(remote(sums, sall.at[fr], near_send.at[1, k], near_recv.at[1, k], partner))
    gall[fr] = gmsg[...]
    sall[fr] = sums[...]
    arrays = (e_ref, s_ref, p_ref, o_ref)
    dims1 = {"a": CLIP_DIMS, "b": FRAME_DIMS}
    dims2 = {"a": FRAME_DIMS, "b": CLIP_DIMS, "m": CLIP_DIMS}
    turn = (0, 0, 1, 1, 2, 2, 0, 1, 2)
    copies, local = {}, {}

    def send(n, step, src, dst, dim):
        copies[n, step] = remote(src, dst, send_sem.at[n, step], recv_sem.at[n, step], partners[dim])

    for n in range(6):
        g, a, k = PARTS[n]
        src = arrays[a]
        cols = pl.ds(k * 1536, 1536)
        send(n, 0, src.at[:, 1 - at["c"], :, cols], got.at[n], "c")
        local[n] = pltpu.make_async_copy(src.at[:, at["c"], :, cols], own.at[n], local_sem.at[n])
        local[n].start()

    def first(n):
        g, a, k = PARTS[n]
        order = rotated(dims1[g], turn[n])
        local[n].wait()
        copies[n, 0].wait_recv()
        if g == "a":
            for p in range(8):
                chunk = dp_of(moved(at, bits_at(order, p))) // 2
                acc[n, p] = own[n, chunk] + got[n, chunk]
        else:
            full = (own[n] + got[n]).reshape(384, 1536)
            for q in range(2):
                acc[n, :, :, pl.ds(q * D, D)] = dot(mix[turn[n]], full[:, q * D : (q + 1) * D]).astype(low).reshape(8, 48, D)
        send(n, 1, acc.at[n, pl.ds(4, 4)], r1.at[n], order[0])

    def spread(n, last):
        g = PARTS[n][0]
        table = sa if g == "a" else sb
        wide = dot(table[2 * turn[n]], last[:, :D]) + dot(table[2 * turn[n] + 1], last[:, D:])
        t[n] = wide.astype(low).reshape(8, 16, D)
        send(n, 4, t.at[n, pl.ds(4, 4)], u1.at[n], rotated(dims2[g], turn[n])[0])

    def middle(n, s):
        g = PARTS[n][0]
        order = rotated(dims1[g], turn[n])
        copies[n, s].wait_recv()
        if s == 1:
            acc[n, pl.ds(0, 4)] += r1[n]
            send(n, 2, acc.at[n, pl.ds(2, 2)], r2.at[n], order[1])
        elif s == 2:
            acc[n, pl.ds(0, 2)] += r2[n]
            send(n, 3, acc.at[n, pl.ds(1, 1)], r3.at[n], order[2])
        else:
            spread(n, acc[n, 0] + r3[n, 0])

    def tail(n, s):
        order = rotated(dims2[PARTS[n][0]], turn[n])
        copies[n, 3 + s].wait_recv()
        if s == 1:
            t[n, pl.ds(0, 4)] += u1[n]
            send(n, 5, t.at[n, pl.ds(2, 2)], u2.at[n], order[1])
        elif s == 2:
            t[n, pl.ds(0, 2)] += u2[n]
            send(n, 6, t.at[n, pl.ds(1, 1)], u3.at[n], order[2])
        else:
            out[n] = t[n, 0].astype(f32) + u3[n, 0].astype(f32)

    for n in range(6):
        first(n)
    for copy in near:
        copy.wait_recv()
    for load in loads:
        load.wait()
    total = sall[0]
    for k in range(1, FRAMES):
        total = total + sall[k]
    stot[...] = total
    message_back(at, cls_all, pre, normed, qkv, mixed, vec, vw, vp, vo, gall, stot, pick, part, mgrad, new_cls)
    new_cls[...] += tok_cls[...]
    send(6, 0, mgrad.at[1 - at["c"]], mgot, "c")
    for s in (1, 2, 3):
        for n in range(6):
            middle(n, s)
        if s == 1:
            copies[6, 0].wait_recv()
            both = mgrad[at["c"]] + mgot[...]
            for n in range(6, 9):
                spread(n, both[:, (n - 6) * 1536 : (n - 5) * 1536])
    for s in (1, 2, 3):
        for n in range(9):
            tail(n, s)
    for copy in near:
        copy.wait_send()
    for key in copies:
        copies[key].wait_send()


def all_sums(d_expand, d_shrink, d_first, d_second, gmsg, sums, saved, vec, mw, mp, mo, tok_cls):
    all_cls, pre, normed, qkv, mixed = saved
    mats = spread_matrices()
    pick, part = pick_table()
    vmem = pl.BlockSpec(memory_space=pltpu.VMEM)
    any_spec = pl.BlockSpec(memory_space=pl.ANY)
    S, V, SEM = jax.ShapeDtypeStruct, pltpu.VMEM, pltpu.SemaphoreType.DMA
    scratch = [V((6, 8, 48, 1536), low), V((6, 8, 48, 1536), low), V((6, 8, 48, 1536), low),
               V((6, 4, 48, 1536), low), V((6, 2, 48, 1536), low), V((6, 1, 48, 1536), low),
               V((9, 8, 16, D), low), V((9, 4, 16, D), low), V((9, 2, 16, D), low), V((9, 1, 16, D), low),
               V((2, 48, 6 * D), low), V((48, 6 * D), low), V((D, D), low), V((D, 3 * D), low), V((D, D), low),
               V((FRAMES, SLOT, D), f32), V((FRAMES, SUMS, D), f32), V((SUMS, D), f32),
               SEM((3,)), SEM((6,)), SEM((9, 7)), SEM((9, 7)), SEM((2, 7)), SEM((2, 7))]
    return pl.pallas_call(
        sums_kernel,
        in_specs=[any_spec] * 4 + [vmem] * 13 + [any_spec] * 3 + [vmem],
        out_specs=[vmem, vmem],
        out_shape=[S((9, 16, D), f32), S((SLOT, D), f32)],
        scratch_shapes=scratch,
        compiler_params=pltpu.CompilerParams(collective_id=2, has_side_effects=True, vmem_limit_bytes=BIG),
        name="all_sums",
    )(to_units(d_expand), to_units(d_shrink), to_units(d_first), to_units(d_second), mats["a"], mats["b"], mats["mix"],
      gmsg, sums, all_cls, pre, normed, qkv, mixed, vec, pick, part, mw, mp, mo, tok_cls)


def on_device(
    frames, cotangent, group_ids, message_weight, message_bias, message_gain, message_shift, message_project,
    message_project_bias, message_output, message_output_bias, first_gain, first_shift, attend_project,
    attend_project_bias, attend_output, attend_output_bias, second_gain, second_shift, expand_weight, expand_bias,
    shrink_weight, shrink_bias,
):
    blank = jnp.zeros((D,), low)
    vec = jnp.concatenate([
        message_bias, message_gain, message_shift, message_project_bias[:D], blank, message_project_bias[D:],
        message_output_bias, first_gain, first_shift, attend_project_bias[:D], blank, attend_project_bias[D:],
        attend_output_bias, second_gain, second_shift, expand_bias, shrink_bias, blank, blank, blank, blank,
    ]).astype(f32).reshape(24, D)
    cls = jnp.pad(frames[:, 0, 0].astype(f32), ((0, SLOT - CLIPS_HERE), (0, 0)))
    gids = jnp.pad(group_ids.reshape(16, CLIPS_HERE), ((0, 0), (0, SLOT - CLIPS_HERE)), constant_values=-1)
    message, *saved = message_forward(cls, vec, message_weight, message_project, message_output)
    first_low, proj, probs, mixed, resid, second_low = attend_forward(frames, message, vec, attend_project, attend_output)
    hidden, dgate, result, cls_out = mlp_forward(second_low, resid, vec, expand_weight, shrink_weight)
    loss, pooled, gpool = loss_step(cls_out, gids.reshape(128, 1), gids.reshape(1, 128))
    d_shrink, d_expand, after, sums = mlp_back(
        cotangent, gpool, vec, hidden, dgate, second_low, expand_weight, shrink_weight, resid)
    gproj, tokens, tok_cls, gmsg, sums = attend_back(
        after, proj, probs, frames, message, vec, attend_project, attend_output, sums)
    d_first, d_second = attend_weights(first_low, gproj, mixed, after)
    out, new_cls = all_sums(
        d_expand, d_shrink, d_first, d_second, gmsg, sums, saved, vec, message_weight, message_project,
        message_output, tok_cls)
    delta_frames = tokens.at[:, 0, 0].set(new_cls[:CLIPS_HERE].astype(low))

    def unit(part, half):
        return out[part, 8 * half : 8 * half + 6]

    tail = unit(8, 1)

    def lanes(first, count=1):
        return tail[:, first : first + count].T.reshape(6 * count)

    return (
        result, loss[0, 0], pooled[:CLIPS_HERE], delta_frames,
        unit(6, 0), lanes(12), lanes(13), lanes(14),
        jnp.concatenate([unit(6, 1), unit(7, 0), unit(7, 1)], axis=1), lanes(30, 2),
        unit(8, 0), lanes(17), lanes(0), lanes(1),
        jnp.concatenate([unit(4, 0), unit(4, 1), unit(5, 0)], axis=1), lanes(28, 2),
        unit(5, 1), lanes(4), lanes(5), lanes(6),
        jnp.concatenate([unit(0, 0), unit(0, 1), unit(2, 0), unit(2, 1)], axis=1), lanes(24, 4),
        jnp.concatenate([unit(1, 0), unit(1, 1), unit(3, 0), unit(3, 1)], axis=0), lanes(11),
    )


def solution(mesh):
    placed = (
        P("dp", "frame", None, None),
        P("dp", "frame", None, None),
        P(),
        P(),
        P(),
        P(),
        P(),
        P(),
        P(),
        P(),
        P(),
        P(),
        P(),
        P(),
        P(),
        P(),
        P(),
        P(),
        P(),
        P(),
        P(),
        P(),
        P(),
    )
    return jax.shard_map(
        on_device,
        mesh=mesh,
        in_specs=placed,
        out_specs=(
            P("dp", "frame", None, None),
            P(),
            P("dp", None),
            P("dp", "frame", None, None),
            P(("dp", "frame"), None),
            P(("dp", "frame")),
            P(("dp", "frame")),
            P(("dp", "frame")),
            P(("dp", "frame"), None),
            P(("dp", "frame")),
            P(("dp", "frame"), None),
            P(("dp", "frame")),
            P(("dp", "frame")),
            P(("dp", "frame")),
            P(("dp", "frame"), None),
            P(("dp", "frame")),
            P(("dp", "frame"), None),
            P(("dp", "frame")),
            P(("dp", "frame")),
            P(("dp", "frame")),
            P(("dp", "frame"), None),
            P(("dp", "frame")),
            P(("dp", "frame"), None),
            P(("dp", "frame")),
        ),
        check_vma=False,
    )
```

```python
import functools

import jax
import jax.numpy as jnp
import numpy as np
from jax import lax
from jax.experimental import pallas as pl
from jax.experimental.pallas import tpu as pltpu
from jax.sharding import PartitionSpec as P

f32, low = jnp.float32, jnp.bfloat16
CLIPS_HERE, PATCH, ROWS, D, FF = 4, 197, 208, 768, 3072
ALL = CLIPS_HERE * ROWS
BIG = 58 * 2**20
(R_MB, R_MG, R_MS, R_MPB, R_MOB, R_FG, R_FS, R_APB, R_AOB, R_SG, R_SS, R_EB, R_SB) = (
    0, 1, 2, 3, 6, 7, 8, 9, 12, 13, 14, 15, 19)


def dot(a, b):
    return jnp.dot(a, b, preferred_element_type=f32)


def dot_t(a, b):
    return lax.dot_general(a, b, (((1,), (1,)), ((), ())), preferred_element_type=f32)


def dot_tl(a, b):
    return lax.dot_general(a, b, (((0,), (0,)), ((), ())), preferred_element_type=f32)


def stats(x):
    mean = jnp.mean(x, axis=-1, keepdims=True)
    centered = x - mean
    inv = lax.rsqrt(jnp.mean(centered * centered, axis=-1, keepdims=True) + 1e-05)
    return centered * inv, inv


def norm_back(grad, u, inv, gain):
    h = grad * gain
    return (h - jnp.mean(h, axis=-1, keepdims=True) - u * jnp.mean(h * u, axis=-1, keepdims=True)) * inv


def attend_kernel(frames, message, vec, wp, wo, first_low, proj, probs, mixed, resid, second_low, xs):
    clip = pl.program_id(0)
    xs[pl.ds(192, 16)] = jnp.zeros((16, D), f32)
    xs[pl.ds(0, PATCH)] = frames[0, 0].astype(f32)
    xs[pl.ds(PATCH, 1)] = message[pl.ds(clip, 1)]
    x = xs[...]
    u, _ = stats(x)
    normed = (u * vec[R_FG : R_FG + 1] + vec[R_FS : R_FS + 1]).astype(low)
    first_low[...] = normed
    for j in range(3):
        part = dot(normed, wp[:, j * D : (j + 1) * D]) + vec[R_APB + j : R_APB + j + 1]
        proj[:, j * D : (j + 1) * D] = part.astype(low)
    lane = lax.broadcasted_iota(jnp.int32, (ROWS, 128), 1)
    keep = lax.broadcasted_iota(jnp.int32, (ROWS, ROWS), 1) < PATCH + 1
    zero = jnp.zeros((), low)
    for pair in range(6):
        q = proj[:, pair * 128 : pair * 128 + 128]
        k = proj[:, D + pair * 128 : D + pair * 128 + 128]
        v = proj[:, 2 * D + pair * 128 : 2 * D + pair * 128 + 128]
        outs = []
        for half in range(2):
            mine = (lane < 64) if half == 0 else (lane >= 64)
            s = dot_t(jnp.where(mine, q, zero), k) * 0.125
            s = jnp.where(keep, s, -1e30)
            e = jnp.exp(s - jnp.max(s, axis=-1, keepdims=True))
            p = (e * (1.0 / jnp.sum(e, axis=-1, keepdims=True))).astype(low)
            probs[0, 2 * pair + half] = p
            outs.append(dot(p, v))
        mixed[:, pair * 128 : pair * 128 + 128] = jnp.where(lane < 64, outs[0], outs[1]).astype(low)
    after = x + (dot(mixed[...], wo[...]) + vec[R_AOB : R_AOB + 1])
    resid[...] = after
    u2, _ = stats(after)
    second_low[...] = (u2 * vec[R_SG : R_SG + 1] + vec[R_SS : R_SS + 1]).astype(low)


def const(shape):
    return pl.BlockSpec(shape, lambda *i: (0,) * len(shape))


def attend_forward(frames, message, vec, wp, wo):
    row = lambda w: pl.BlockSpec((ROWS, w), lambda c: (c, 0))
    return pl.pallas_call(
        attend_kernel,
        grid=(CLIPS_HERE,),
        in_specs=[pl.BlockSpec((1, 1, PATCH, D), lambda c: (c, 0, 0, 0)), const((8, D)), const((24, D)),
                  const((D, 3 * D)), const((D, D))],
        out_specs=[row(D), row(3 * D), pl.BlockSpec((1, 12, ROWS, ROWS), lambda c: (c, 0, 0, 0)), row(D), row(D), row(D)],
        out_shape=[jax.ShapeDtypeStruct((ALL, D), low), jax.ShapeDtypeStruct((ALL, 3 * D), low),
                   jax.ShapeDtypeStruct((CLIPS_HERE, 12, ROWS, ROWS), low), jax.ShapeDtypeStruct((ALL, D), low),
                   jax.ShapeDtypeStruct((ALL, D), f32), jax.ShapeDtypeStruct((ALL, D), low)],
        scratch_shapes=[pltpu.VMEM((ROWS, D), f32)],
        compiler_params=pltpu.CompilerParams(vmem_limit_bytes=BIG),
        name="attend_forward",
    )(frames, message, vec, wp, wo)


def mlp_back_kernel(cot, gpool, vec, hidden, dgate, second_low, we, ws, resid,
                    d_shrink, d_expand, after, sums, gl, gb, gsec):
    j = pl.program_id(0)

    @pl.when(j == 0)
    def _():
        gl[...] = jnp.zeros((ALL, D), f32)
        for c in range(CLIPS_HERE):
            gl[pl.ds(c * ROWS, PATCH)] = cot[c, 0].astype(f32)
            gl[pl.ds(c * ROWS, 1)] += gpool[pl.ds(c, 1)]
        gb[...] = gl[...].astype(low)
        gsec[...] = jnp.zeros((ALL, D), f32)
        sums[...] = jnp.zeros((24, D), f32)
        sums[11:12] = jnp.sum(gb[...].astype(f32), axis=0, keepdims=True)

    d_shrink[...] = dot_tl(hidden[...], gb[...]).astype(low)
    ghp = (dot_t(gb[...], ws[...]) * dgate[...].astype(f32)).astype(low)
    sums[pl.ds(7 + j, 1)] = jnp.sum(ghp.astype(f32), axis=0, keepdims=True)
    d_expand[...] = dot_tl(second_low[...], ghp).astype(low)
    gsec[...] += dot_t(ghp, we[...])

    @pl.when(j == 3)
    def _():
        gain = vec[R_SG : R_SG + 1]
        total = [jnp.zeros((1, D), f32) for _ in range(3)]
        for c in range(CLIPS_HERE):
            rows = pl.ds(c * ROWS, ROWS)
            u, inv = stats(resid[rows])
            g = gsec[rows]
            out = gl[rows] + norm_back(g, u, inv, gain)
            after[rows] = out
            total[0] += jnp.sum(g * u, axis=0, keepdims=True)
            total[1] += jnp.sum(g, axis=0, keepdims=True)
            total[2] += jnp.sum(out.astype(low).astype(f32), axis=0, keepdims=True)
        sums[5:6] = total[0]
        sums[6:7] = total[1]
        sums[4:5] = total[2]


def mlp_back(cot, gpool, vec, hidden, dgate, second_low, we, ws, resid):
    tile = pl.BlockSpec((ALL, D), lambda j: (0, j))
    return pl.pallas_call(
        mlp_back_kernel,
        grid=(4,),
        in_specs=[const((CLIPS_HERE, 1, PATCH, D)), const((8, D)), const((24, D)), tile, tile, const((ALL, D)),
                  pl.BlockSpec((D, D), lambda j: (0, j)), pl.BlockSpec((D, D), lambda j: (j, 0)), const((ALL, D))],
        out_specs=[pl.BlockSpec((D, D), lambda j: (j, 0)), pl.BlockSpec((D, D), lambda j: (0, j)), const((ALL, D)),
                   const((24, D))],
        out_shape=[jax.ShapeDtypeStruct((FF, D), low), jax.ShapeDtypeStruct((D, FF), low),
                   jax.ShapeDtypeStruct((ALL, D), f32), jax.ShapeDtypeStruct((24, D), f32)],
        scratch_shapes=[pltpu.VMEM((ALL, D), f32), pltpu.VMEM((ALL, D), low), pltpu.VMEM((ALL, D), f32)],
        compiler_params=pltpu.CompilerParams(vmem_limit_bytes=BIG),
        name="mlp_back",
    )(cot, gpool, vec, hidden, dgate, second_low, we, ws, resid)


MESH = pl.DeviceIdType.MESH


def flip_low(index):
    return index + 1 - 2 * (index % 2)


def flip_pair(index, high, low):
    index = 3 - index if high else index
    return flip_low(index) if low else index


def place():
    dp, fr = lax.axis_index("dp"), lax.axis_index("frame")
    return dict(y=dp // 4, x=(dp // 2 % 2) * 2 + fr // 4, z=fr % 4, c=dp % 2)


def moved(at, bits):
    return dict(
        y=flip_pair(at["y"], bits.get("yu"), bits.get("yv")),
        x=flip_pair(at["x"], bits.get("xu"), bits.get("xv")),
        z=flip_pair(at["z"], bits.get("zu"), bits.get("zv")),
        c=1 - at["c"] if bits.get("c") else at["c"],
    )


def dp_of(at):
    return at["y"] * 4 + (at["x"] // 2) * 2 + at["c"]


def frame_of(at):
    return (at["x"] % 2) * 4 + at["z"]


def device_of(at):
    return (dp_of(at), frame_of(at))


CLIP_DIMS = ("yu", "yv", "xu")
FRAME_DIMS = ("xv", "zu", "zv")


def rotated(dims, turn):
    return dims[turn:] + dims[:turn]


def bits_at(dims, position):
    return {dims[k]: (position >> (2 - k)) & 1 for k in range(3)}


def to_units(full):
    return full.reshape(8, 2, 48, full.shape[-1])


FRAMES = 8
SLOT = 8
MROWS = FRAMES * SLOT
SUMS = 24


def greet(partners):
    barrier = pltpu.get_barrier_semaphore()
    for partner in partners:
        pl.semaphore_signal(barrier, inc=1, device_id=partner, device_id_type=MESH)
    pl.semaphore_wait(barrier, len(partners))


def frame_partners():
    dp, fr = lax.axis_index("dp"), lax.axis_index("frame")
    return [(dp, lax.rem(fr + k, FRAMES)) for k in range(1, FRAMES)]


def remote(src, dst, send_sem, recv_sem, device):
    copy = pltpu.make_async_remote_copy(
        src_ref=src, dst_ref=dst, send_sem=send_sem, recv_sem=recv_sem, device_id=device, device_id_type=MESH)
    copy.start()
    return copy


def same_clip():
    rows = lax.broadcasted_iota(jnp.int32, (MROWS, MROWS), 0)
    cols = lax.broadcasted_iota(jnp.int32, (MROWS, MROWS), 1)
    return rows % SLOT == cols % SLOT


def soft(s):
    e = jnp.exp(s - jnp.max(s, axis=-1, keepdims=True))
    return e / jnp.sum(e, axis=-1, keepdims=True)


VECTORS = ((R_MB,), (R_MG,), (R_MS,), (R_MPB, R_MPB + 2), (R_MOB,), (R_FG,), (R_FS,), (R_APB, R_APB + 2), (R_AOB,), (R_SG,),
           (R_SS,), (R_EB, R_EB + 1, R_EB + 2, R_EB + 3), (R_SB,))


def message_kernel(*refs):
    vectors, refs = refs[: len(VECTORS)], refs[len(VECTORS) :]
    (frames, mw, mp, mo, vec, message, all_cls, pre_out, normed_out, qkv, mixed,
     vw, vp, vo, cls, tops, load_sem, tops_sem, send_sem, recv_sem) = refs
    fr = lax.axis_index("frame")
    get_tops = pltpu.make_async_copy(frames.at[:, 0, pl.ds(0, 16)], tops, tops_sem.at[0])
    get_tops.start()
    loads = [pltpu.make_async_copy(s, d, load_sem.at[n]) for n, (s, d) in enumerate(((mw, vw), (mp, vp), (mo, vo)))]
    for load in loads:
        load.start()
    vec[...] = jnp.zeros((24, D), f32)
    for ref, rows in zip(vectors, VECTORS):
        for k, row in enumerate(rows):
            vec[row : row + 1] = ref[pl.ds(k * D, D)].astype(f32).reshape(1, D)
    cls[...] = jnp.zeros((SLOT, D), f32)
    get_tops.wait()
    for c in range(CLIPS_HERE):
        cls[c : c + 1] = tops[c].astype(f32)[0:1]
    partners = frame_partners()
    greet(partners)
    copies = [remote(cls, all_cls.at[fr], send_sem.at[k], recv_sem.at[k], partner)
              for k, partner in enumerate(partners)]
    all_cls[fr] = cls[...]
    loads[0].wait()
    for copy in copies:
        copy.wait_recv()
    x = all_cls[...].reshape(MROWS, D).astype(low)
    pre = dot(x, vw[...]) + vec[R_MB : R_MB + 1]
    pre_out[...] = pre
    u, _ = stats(pre)
    normed = (u * vec[R_MG : R_MG + 1] + vec[R_MS : R_MS + 1]).astype(low)
    normed_out[...] = normed
    loads[1].wait()
    for j in range(3):
        qkv[:, j * D : (j + 1) * D] = (dot(normed, vp[:, j * D : (j + 1) * D]) + vec[R_MPB + j : R_MPB + j + 1]).astype(low)
    keep = same_clip()
    lane = lax.broadcasted_iota(jnp.int32, (MROWS, 128), 1)
    zero = jnp.zeros((), low)
    for pair in range(6):
        q = qkv[:, pair * 128 : pair * 128 + 128]
        k = qkv[:, D + pair * 128 : D + pair * 128 + 128]
        v = qkv[:, 2 * D + pair * 128 : 2 * D + pair * 128 + 128]
        outs = []
        for half in range(2):
            mine = (lane < 64) if half == 0 else (lane >= 64)
            s = jnp.where(keep, dot_t(jnp.where(mine, q, zero), k) * 0.125, -1e30)
            outs.append(dot(soft(s).astype(low), v))
        mixed[:, pair * 128 : pair * 128 + 128] = jnp.where(lane < 64, outs[0], outs[1]).astype(low)
    loads[2].wait()
    every = pre + dot(mixed[...], vo[...]) + vec[R_MOB : R_MOB + 1]
    rows = lax.broadcasted_iota(jnp.int32, (MROWS, 1), 0) // SLOT
    every = jnp.where(rows == fr, every, 0.0)
    message[...] = jnp.sum(every.reshape(FRAMES, SLOT, D), axis=0)
    for copy in copies:
        copy.wait_send()


def message_forward(vectors, frames, mw, mp, mo):
    vmem = pl.BlockSpec(memory_space=pltpu.VMEM)
    any_spec = pl.BlockSpec(memory_space=pl.ANY)
    S = jax.ShapeDtypeStruct
    return pl.pallas_call(
        message_kernel,
        in_specs=[vmem] * len(VECTORS) + [any_spec] * 4,
        out_specs=[vmem] * 7,
        out_shape=[S((24, D), f32), S((SLOT, D), f32), S((FRAMES, SLOT, D), f32), S((MROWS, D), f32), S((MROWS, D), low),
                   S((MROWS, 3 * D), low), S((MROWS, D), low)],
        scratch_shapes=[pltpu.VMEM((D, D), low), pltpu.VMEM((D, 3 * D), low), pltpu.VMEM((D, D), low),
                        pltpu.VMEM((SLOT, D), f32), pltpu.VMEM((CLIPS_HERE, 16, D), low),
                        pltpu.SemaphoreType.DMA((3,)), pltpu.SemaphoreType.DMA((1,)), pltpu.SemaphoreType.DMA((7,)), pltpu.SemaphoreType.DMA((7,))],
        compiler_params=pltpu.CompilerParams(collective_id=0, has_side_effects=True, vmem_limit_bytes=BIG),
        name="message_forward",
    )(*vectors, frames, mw, mp, mo)


PRECISE = lax.Precision.HIGHEST


def message_back(at, cls_all, pre, normed, qkv, mixed, vec, vw, vp, vo, gall, pick, mgrad, gcls, between):
    fr = lax.axis_index("frame")
    g = gall[...].reshape(MROWS, D)
    g_low = g.astype(low)
    gmm = dot_t(g_low, vo[...]).astype(low)
    keep = same_clip()
    lane = lax.broadcasted_iota(jnp.int32, (MROWS, 128), 1)
    zero = jnp.zeros((), low)
    parts = ([], [], [])
    for pair in range(6):
        q = qkv[:, pair * 128 : pair * 128 + 128]
        k = qkv[:, D + pair * 128 : D + pair * 128 + 128]
        v = qkv[:, 2 * D + pair * 128 : 2 * D + pair * 128 + 128]
        gm = gmm[:, pair * 128 : pair * 128 + 128]
        outs = []
        for half in range(2):
            mine = (lane < 64) if half == 0 else (lane >= 64)
            p = soft(jnp.where(keep, dot_t(jnp.where(mine, q, zero), k) * 0.125, -1e30))
            dp = dot_t(jnp.where(mine, gm, zero), v)
            gs = (p * (dp - jnp.sum(dp * p, axis=-1, keepdims=True))).astype(low)
            outs.append((dot(gs, k), dot_tl(gs, q), dot_tl(p.astype(low), gm)))
        for n, scale in ((0, 0.125), (1, 0.125), (2, 1.0)):
            parts[n].append((jnp.where(lane < 64, outs[0][n], outs[1][n]) * scale).astype(low))
    gq, gk, gv = (jnp.concatenate(part, axis=1) for part in parts)
    between()
    gnorm = dot_t(gq, vp[:, :D]) + dot_t(gk, vp[:, D : 2 * D]) + dot_t(gv, vp[:, 2 * D :])
    u, inv = stats(pre[...])
    gpre = (g + norm_back(gnorm, u, inv, vec[R_MG : R_MG + 1])).astype(low)

    def total(value):
        return jnp.sum(value.astype(f32), axis=0, keepdims=True)

    mine = (lax.broadcasted_iota(jnp.int32, (96, D), 1) == pick[0:96]).astype(low)
    x = cls_all[...].reshape(MROWS, D).astype(low)
    for unit, (left, right) in enumerate(((x, gpre), (normed[...], gq), (normed[...], gk), (normed[...], gv),
                                          (mixed[...], g_low))):
        turned = dot_t(mine, left).astype(low)
        mgrad[:, :, unit * D : (unit + 1) * D] = dot(turned, right).astype(low).reshape(2, 48, D)
    back = dot_t(gpre, vw[...])
    rows = lax.broadcasted_iota(jnp.int32, (MROWS, 1), 0) // SLOT
    gcls[...] = jnp.sum(jnp.where(rows == fr, back, 0.0).reshape(FRAMES, SLOT, D), axis=0)
    return [total(gpre), total(gnorm * u), total(gnorm), total(gq), total(gv), total(g_low)]


def message_vectors(sums, message_sums, pick, part, mgrad):
    table = jnp.concatenate([sums[0:12], *message_sums, jnp.zeros((SUMS - 18, D), f32)], axis=0).astype(low)
    choose = (lax.broadcasted_iota(jnp.int32, (672, D), 1) == pick[...]).astype(low)
    z = dot_t(choose, table)
    wide = lax.broadcasted_iota(jnp.int32, (96, 128), 1)
    narrow = lax.broadcasted_iota(jnp.int32, (96, SUMS), 1)
    out = jnp.zeros((96, 128), f32)
    out += jnp.concatenate([z[:96], jnp.zeros((96, 128 - SUMS), f32)], axis=1)
    for q in range(4):
        hit = narrow == 7 + part[384:480, 3:4]
        value = jnp.sum(jnp.where(hit, z[96 * (1 + q) : 96 * (2 + q)], 0.0), axis=-1, keepdims=True)
        out = jnp.where(wide == 24 + q, value, out)
    for q in range(2):
        for n, first in enumerate((2, 15)):
            hit = narrow == first + part[384:480, 4:5]
            value = jnp.sum(jnp.where(hit, z[96 * (5 + q) : 96 * (6 + q)], 0.0), axis=-1, keepdims=True)
            out = jnp.where(wide == 28 + 2 * n + q, value, out)
    mgrad[:, :, 5 * D : 5 * D + 128] = out.astype(low).reshape(2, 48, 128)
    mgrad[:, :, 5 * D + 128 :] = jnp.zeros((2, 48, D - 128), low)


def index_table():
    table = np.zeros((384 + 672, 8), np.int32)
    r = np.arange(384)
    table[:384, 0] = r // 48
    table[:384, 1] = r % 48 // 6 * 48 + r % 6
    table[:384, 2] = r % 48 // 6 % 2
    r = np.arange(96)
    c, y, xh, i = r // 48, r % 48 // 12, r % 12 // 6, r % 6
    high = y * 4 + xh * 2 + c
    picks = [(high * 48 + i, 6)]
    picks += [(high % 4 * 192 + q * 6 + i, 24) for q in range(4)]
    picks += [(high % 8 * 96 + q * 6 + i, 12) for q in range(2)]
    for n, (base, step) in enumerate(picks):
        rows = slice(384 + 96 * n, 384 + 96 * (n + 1))
        table[rows, 0], table[rows, 1], table[rows, 2] = base, step, xh
        table[rows, 3], table[rows, 4] = y, y // 2
    return jnp.asarray(table)


def fill_orders(at, table, sa, sb, mix, pick):
    xh, xl = at["x"] // 2, at["x"] % 2
    rows = lax.broadcasted_iota(jnp.int32, (128, 48), 0)
    cols = lax.broadcasted_iota(jnp.int32, (128, 48), 1)
    for ref, dims in ((sa, FRAME_DIMS), (sb, CLIP_DIMS)):
        for turn in range(3):
            block = jnp.zeros((128, 48), jnp.int32)
            for p in range(8):
                to = moved(at, bits_at(rotated(dims, turn), p))
                value = frame_of(to) if dims == FRAME_DIMS else dp_of(to) // 2
                block = jnp.where((rows >> 4) == p, value, block)
            for half in range(2):
                inner = (rows & 15) - 8 * half
                hit = (cols == block * 6 + inner) & (inner >= 0) & (inner < 6)
                ref[2 * turn + half] = hit.astype(f32).astype(low)
    lanes = lax.broadcasted_iota(jnp.int32, (384, 384), 1)
    p_col, base, same = table[0:384, 0:1], table[0:384, 1:2], table[0:384, 2:3] == xh
    for turn in range(3):
        frame = jnp.zeros((384, 1), jnp.int32)
        for p in range(8):
            to = moved(at, bits_at(rotated(FRAME_DIMS, turn), p))
            side = to["x"] % 2
            frame = jnp.where(p_col == p, jnp.where(same, 4 * side + to["z"], 4 * (1 - side) + to["z"]), frame)
        mix[turn] = (lanes == base + 6 * frame).astype(f32).astype(low)
    base, step, same = table[384:, 0:1], table[384:, 1:2], table[384:, 2:3] == xh
    pick[...] = base + step * jnp.where(same, 4 * xl + at["z"], 4 * (1 - xl) + at["z"])


CORE, S1, S2, S3, S4, S5, S6 = 0, 1, 5, 7, 8, 9, 10
KEEP = (4, 2, 1)
KIND = ("a", "s") * 3 + ("a", "b") * 3 + ("m",) * 3
TURN = (0, 0, 1, 1, 2, 2) * 2 + (0, 1, 2)
N_PARTS = 15


def order_of(n, phase):
    clips_first = (KIND[n] == "a") == (phase == 1)
    if KIND[n] == "m":
        clips_first = True
    return rotated(CLIP_DIMS if clips_first else FRAME_DIMS, TURN[n])


def back_kernel(
    e_ref, s_ref, after_ref, proj_ref, probs_ref, frames_ref, first_ref, mixed_ref, wp_ref, wo_ref, mw_ref, mp_ref, mo_ref,
    vec, message, sums_in, cls_all, pre, normed, qkv, msg_mixed, table,
    tokens, out, out_s,
    wp, wo, mw, mo, after, proj, probs, frames, first_low, mixed, xs, gm_all, heads, sums, gmsg, gcls, mgrad, mgot,
    gall, sall, sa, sb, mix, pick, wide_s,
    own_a, got_a, ra1, ra2, ra3, own_s, got_s, rs1, rs2, rs3, late, got_l, rl1, rl2, rl3,
    ta, ua1, ua2, ua3, ts, us1, us2, us3, tl, ul1, ul2, ul3, tm, um1, um2, um3,
    load_sem, probs_sem, local_sem, send_sem, recv_sem, near_send, near_recv,
):
    at = place()
    fr = lax.axis_index("frame")
    core = at["c"]
    around = frame_partners()
    partners = {d: device_of(moved(at, {d: 1})) for d in ("c",) + CLIP_DIMS + FRAME_DIMS}

    def load(n, src, dst):
        copy = pltpu.make_async_copy(src, dst, load_sem.at[n])
        copy.start()
        return copy

    def probs_copy(clip):
        return pltpu.make_async_copy(probs_ref.at[clip], probs.at[clip % 2], probs_sem.at[clip % 2])

    probs_copy(0).start()
    get_wo, get_after, get_proj = load(0, wo_ref, wo), load(1, after_ref, after), load(2, proj_ref, proj)
    greet(around + [partners[d] for d in ("c", "yu", "yv", "xu")])

    def mine(n, lead):
        if n < 6:
            return (own_a if n % 2 == 0 else own_s).at[n // 2, lead]
        return late.at[n % 2, lead, core, :, pl.ds((n - 6) // 2 * 512, 512)]

    def got(n):
        if n < 6:
            return (got_a if n % 2 == 0 else got_s).at[n // 2]
        return got_l.at[n - 6]

    def half(n, s):
        if n < 6:
            return ((ra1, ra2, ra3) if n % 2 == 0 else (rs1, rs2, rs3))[s - 1].at[n // 2]
        return (rl1, rl2, rl3)[s - 1].at[n - 6]

    def width(n):
        return 512 if n < 6 else 256 if n < 12 else D

    def small(n, s):
        if KIND[n] == "s":
            return (ts, us1, us2, us3)[s].at[n // 2]
        if n < 6:
            return (ta, ua1, ua2, ua3)[s].at[n // 2]
        if n < 12:
            return (tl, ul1, ul2, ul3)[s].at[n - 6]
        return (tm, um1, um2, um3)[s].at[n - 12]

    def chunk_at(n, p):
        return dp_of(moved(at, bits_at(order_of(n, 1), p))) // 2

    def source(n, which):
        if n < 6:
            step = 1024 if n % 2 == 0 else 256
            return (e_ref if n % 2 == 0 else s_ref).at[:, which, :, pl.ds(n // 2 * step, step)]
        return late.at[n % 2, :, which, :, pl.ds((n - 6) // 2 * 512, 512)]

    def local(n):
        return pltpu.make_async_copy(source(n, core), mine(n, pl.ds(0, 8)), local_sem.at[n])

    registry = {}

    def define(n, step, src, dst, dim):
        def make():
            return pltpu.make_async_remote_copy(
                src_ref=src(), dst_ref=dst(), send_sem=send_sem.at[n, step], recv_sem=recv_sem.at[n, step],
                device_id=partners[dim], device_id_type=MESH)
        registry[n, step] = make

    def define_part(n):
        if KIND[n] != "m":
            define(n, CORE, lambda: source(n, 1 - core), lambda: got(n), "c")
            for s, first in ((1, S1), (2, S2), (3, S3)):
                keep, dim = KEEP[s - 1], order_of(n, 1)[s - 1]
                if KIND[n] == "a":
                    for p in range(keep):
                        define(n, first + p, lambda p=p, keep=keep: mine(n, chunk_at(n, keep + p)),
                               lambda p=p, s=s: half(n, s).at[p], dim)
                else:
                    define(n, first, lambda keep=keep: mine(n, pl.ds(keep, keep)), lambda s=s: half(n, s), dim)
        for s, step in ((1, S4), (2, S5), (3, S6)):
            keep, dim = KEEP[s - 1], order_of(n, 2)[s - 1]
            define(n, step, lambda keep=keep: small(n, 0).at[pl.ds(keep, keep)], lambda s=s: small(n, s), dim)

    for n in range(N_PARTS):
        define_part(n)

    def start(n, step):
        registry[n, step]().start()

    def arrived(n, step):
        registry[n, step]().wait_recv()

    fill_orders(at, table, sa, sb, mix, pick)
    sums[...] = sums_in[...]
    gmsg[...] = jnp.zeros((SLOT, D), f32)

    def steps_of(n, s):
        first = (S1, S2, S3)[s - 1]
        return range(first, first + KEEP[s - 1]) if KIND[n] == "a" else (first,)

    def frame_at(n, p, chunk):
        to = moved(at, bits_at(order_of(n, 1), p))
        side = lax.rem(to["x"] % 2 + at["x"] // 2 + chunk % 2, 2)
        return side * 4 + to["z"]

    def begin(n):
        if n < 6:
            local(n).wait()
        arrived(n, CORE)
        if KIND[n] == "a":
            for chunk in range(8):
                ref = mine(n, chunk)
                ref[...] = ref[...] + got(n)[chunk]
        elif KIND[n] == "b":
            ref = mine(n, pl.ds(0, 8))
            full = (ref[...] + got(n)[...]).reshape(384, 512)
            ref[...] = dot(mix[TURN[n]], full).astype(low).reshape(8, 48, 512)
        else:
            for chunk in range(8):
                wide_s[chunk] = (mine(n, chunk)[...] + got(n)[chunk]).astype(f32).reshape(8, 24, 256)
            for p in range(8):
                for two in range(0, 8, 2):
                    rows = [wide_s[two + k, frame_at(n, p, two + k)] for k in range(2)]
                    mine(n, p)[pl.ds(24 * two, 48)] = jnp.concatenate(rows, axis=0).astype(low)
        for step in steps_of(n, 1):
            start(n, step)

    def spread(n, last):
        w = width(n)
        if KIND[n] == "s":
            wide_s[0] = last.astype(f32).reshape(8, 24, 256)
            for p in range(8):
                chunk = dp_of(moved(at, bits_at(order_of(n, 2), p))) // 2
                rows = jnp.concatenate([wide_s[0, chunk], jnp.zeros((8, 256), f32)], axis=0)
                small(n, 0)[p] = rows.astype(low)
        else:
            orders = sa if KIND[n] == "a" else sb
            wide = dot(orders[2 * TURN[n]], last[:, :w]) + dot(orders[2 * TURN[n] + 1], last[:, w:])
            small(n, 0)[...] = wide.astype(low).reshape(8, 16, w)
        start(n, S4)

    def middle(n, s):
        keep = KEEP[s - 1]
        for step in steps_of(n, s):
            arrived(n, step)
        if s == 3:
            lead = chunk_at(n, 0) if KIND[n] == "a" else 0
            spread(n, mine(n, lead)[...] + half(n, 3)[0])
            return
        if KIND[n] == "a":
            for p in range(keep):
                kept = mine(n, chunk_at(n, p))
                kept[...] = kept[...] + half(n, s)[p]
        else:
            kept = mine(n, pl.ds(0, keep))
            kept[...] = kept[...] + half(n, s)[...]
        for step in steps_of(n, s + 1):
            start(n, step)

    def tail(n, s):
        arrived(n, (S4, S5, S6)[s - 1])
        if s == 3:
            total = small(n, 0)[0].astype(f32) + small(n, 3)[0].astype(f32)
            if KIND[n] == "s":
                out_s[n // 2] = total
            else:
                out[n, :, pl.ds(0, width(n))] = total
        else:
            kept = small(n, 0).at[pl.ds(0, KEEP[s - 1])]
            kept[...] = kept[...] + small(n, s)[...]
            start(n, (S5, S6)[s - 1])

    def every(action, parts, *args):
        for n in parts:
            action(n, *args)

    lane = lax.broadcasted_iota(jnp.int32, (ROWS, 128), 1)
    zero = jnp.zeros((), low)
    get_wo.wait()
    get_after.wait()
    gm_all[...] = dot_t(after[...].astype(low), wo[...]).astype(low)
    get_proj.wait()
    for n in range(6):
        start(n, CORE)
        local(n).start()
    get_wp, get_first, get_mixed = load(4, wp_ref, wp), load(5, first_ref, first_low), load(6, mixed_ref, mixed)
    get_frames, get_mw, get_mo = load(3, frames_ref, frames), load(7, mw_ref, mw), load(8, mo_ref, mo)

    def one_clip(clip, carry):
        @pl.when(clip < CLIPS_HERE - 1)
        def _():
            probs_copy(clip + 1).start()

        rows = pl.ds(pl.multiple_of(clip * ROWS, 16), ROWS)
        probs_copy(clip).wait()
        for pair in range(6):
            cols = [pl.ds(n * D + pair * 128, 128) for n in range(3)]
            q, k, v = (proj[rows, c] for c in cols)
            gm = gm_all[rows, pair * 128 : pair * 128 + 128]
            outs = []
            for side in range(2):
                here = (lane < 64) if side == 0 else (lane >= 64)
                dp = dot_t(jnp.where(here, gm, zero), v)
                p_low = probs[clip % 2, 2 * pair + side]
                p = p_low.astype(f32)
                gs = (p * (dp - jnp.sum(dp * p, axis=-1, keepdims=True))).astype(low)
                outs.append((dot(gs, k), dot_tl(gs, q), dot_tl(p_low, gm)))
            for n, scale in ((0, 0.125), (1, 0.125), (2, 1.0)):
                proj[rows, cols[n]] = (jnp.where(lane < 64, outs[0][n], outs[1][n]) * scale).astype(low)

        @pl.when(clip == 1)
        def _():
            every(begin, range(3))

        @pl.when(clip == 2)
        def _():
            every(begin, range(3, 6))

        return carry

    lax.fori_loop(0, CLIPS_HERE, one_clip, 0)

    get_wp.wait()
    ends = jnp.concatenate([proj[pl.ds(c * ROWS + 192, 16)] for c in range(CLIPS_HERE)], axis=0)
    grad = jnp.zeros((16 * CLIPS_HERE, D), f32)
    for n in range(3):
        grad += dot_t(ends[:, n * D : (n + 1) * D], wp[:, n * D : (n + 1) * D])
    for c in range(CLIPS_HERE):
        gmsg[c : c + 1] = grad[16 * c + 5 : 16 * c + 6]
    u, inv = stats(message[...])
    gmsg[...] = norm_back(gmsg[...], u, inv, vec[R_FG : R_FG + 1])
    near = []
    for k, partner in enumerate(around):
        near.append(remote(gmsg, gall.at[fr], near_send.at[0, k], near_recv.at[0, k], partner))
    gall[fr] = gmsg[...]
    get_first.wait()
    get_mixed.wait()

    def late_grad(side, first, stop, left, right):
        grad = dot_tl(left[...], right)
        late[side, :, :, :, pl.ds(first, stop - first)] = grad.astype(low).reshape(8, 2, 48, stop - first)

    late_grad(0, 0, 512, first_low, proj[:, 0:512])
    start(6, CORE)
    late_grad(0, 512, 1024, first_low, proj[:, 512:1024])
    start(8, CORE)
    late_grad(0, 1024, 1536, first_low, proj[:, 1024:1536])
    start(10, CORE)
    begin(6)
    late_grad(1, 0, 768, first_low, proj[:, 1536:2304])
    start(7, CORE)
    begin(8)
    late_grad(1, 768, 1536, mixed, after[...].astype(low))
    start(9, CORE)
    start(11, CORE)
    begin(10)
    begin(7)
    begin(9)
    begin(11)
    every(middle, range(6), 1)
    for n in (0, 2):
        total = jnp.zeros((1, D), f32)
        for c in range(CLIPS_HERE):
            total += jnp.sum(proj[pl.ds(c * ROWS, ROWS), n * D : (n + 1) * D].astype(f32), axis=0, keepdims=True)
        to = 2 if n == 0 else 3
        sums[to : to + 1] = total
    get_frames.wait()

    def token_grads(first):
        two = pl.ds(first * ROWS, 2 * ROWS)
        grad_two = jnp.zeros((2 * ROWS, D), f32)
        for n in range(3):
            grad_two += dot_t(proj[two, n * D : (n + 1) * D], wp[:, n * D : (n + 1) * D])
        for clip in (first, first + 1):
            grad = grad_two[(clip - first) * ROWS : (clip - first + 1) * ROWS]
            xs[pl.ds(192, 16)] = jnp.zeros((16, D), f32)
            xs[pl.ds(0, PATCH)] = frames[clip, 0].astype(f32)
            xs[pl.ds(PATCH, 1)] = message[clip : clip + 1]
            u, inv = stats(xs[...])
            sums[0:1] += jnp.sum(grad * u, axis=0, keepdims=True)
            sums[1:2] += jnp.sum(grad, axis=0, keepdims=True)
            xs[...] = after[pl.ds(clip * ROWS, ROWS)] + norm_back(grad, u, inv, vec[R_FG : R_FG + 1])
            tokens[clip, 0] = xs[pl.ds(0, PATCH)].astype(low)
            heads[clip] = xs[pl.ds(0, 16)]

    sums[0:2] = jnp.zeros((2, D), f32)
    token_grads(0)
    every(middle, range(6), 2)
    token_grads(2)
    get_mp = load(4, mp_ref, wp)
    for k, partner in enumerate(around):
        near.append(remote(sums, sall.at[fr], near_send.at[1, k], near_recv.at[1, k], partner))
    sall[fr] = sums[...]
    every(middle, range(6, 12), 1)
    every(middle, range(6), 3)
    for copy in near[:7]:
        copy.wait_recv()
    get_mw.wait()
    get_mo.wait()
    get_mp.wait()
    def between():
        every(middle, range(6, 12), 2)
        every(tail, range(6), 1)

    vectors = message_back(
        at, cls_all, pre, normed, qkv, msg_mixed, vec, mw, wp, mo, gall, pick, mgrad, gcls, between)
    core_m = []

    def send_message(k):
        cols = pl.ds(1536 * k, 1536)
        core_m.append(remote(mgrad.at[1 - core, :, cols], mgot.at[:, cols], send_sem.at[12 + k, CORE],
                             recv_sem.at[12 + k, CORE], partners["c"]))

    def spread_message(k):
        core_m[k].wait_recv()
        cols = pl.ds(1536 * k, 1536)
        spread(12 + k, mgrad[core, :, cols] + mgot[:, cols])

    send_message(0)
    send_message(1)
    every(middle, range(6, 12), 3)
    for copy in near[7:]:
        copy.wait_recv()
    total = sall[0]
    for k in range(1, FRAMES):
        total = total + sall[k]
    message_vectors(total, vectors, pick, table, mgrad)
    send_message(2)
    spread_message(0)
    spread_message(1)
    every(tail, range(6), 2)
    spread_message(2)
    every(tail, range(6, 12), 1)
    top = lax.broadcasted_iota(jnp.int32, (16, 1), 0) == 0
    for clip in range(CLIPS_HERE):
        tokens[clip, 0, pl.ds(0, 16)] = (heads[clip] + jnp.where(top, gcls[clip : clip + 1], 0.0)).astype(low)
    every(tail, range(12, 15), 1)
    every(tail, range(6, 12), 2)
    every(tail, range(6), 3)
    every(tail, range(12, 15), 2)
    every(tail, range(6, 12), 3)
    every(tail, range(12, 15), 3)
    for copy in core_m:
        copy.wait_send()
    for copy in near:
        copy.wait_send()
    for key in registry:
        registry[key]().wait_send()


def back_and_sums(d_expand, d_shrink, after, proj, probs, frames, first_low, mixed, wp, wo, mw, mp, mo, vec, message, sums,
                  saved):
    vmem = pl.BlockSpec(memory_space=pltpu.VMEM)
    any_spec = pl.BlockSpec(memory_space=pl.ANY)
    S, V, SEM = jax.ShapeDtypeStruct, pltpu.VMEM, pltpu.SemaphoreType.DMA

    def phase_one(count, rows, cols, own=True):
        leads = ([8] if own else []) + [8, 4, 2, 1]
        return [V((count, lead, rows, cols), low) for lead in leads]

    scratch = [
        V((D, 3 * D), low), V((D, D), low), V((D, D), low), V((D, D), low), V((ALL, D), f32), V((ALL, 3 * D), low),
        V((2, 12, ROWS, ROWS), low), V((CLIPS_HERE, 1, PATCH, D), low), V((ALL, D), low), V((ALL, D), low),
        V((ROWS, D), f32), V((ALL, D), low), V((CLIPS_HERE, 16, D), f32), V((SUMS, D), f32), V((SLOT, D), f32), V((SLOT, D), f32),
        V((2, 48, 6 * D), low), V((48, 6 * D), low), V((FRAMES, SLOT, D), f32), V((FRAMES, SUMS, D), f32),
        V((6, 128, 48), low), V((6, 128, 48), low), V((3, 384, 384), low), V((672, 1), jnp.int32), V((8, 8, 24, 256), f32),
        *phase_one(3, 48, 1024), *phase_one(3, 192, 256), V((2, 8, 2, 48, 1536), low), *phase_one(6, 48, 512, own=False),
        *[V((n, lead, rows, cols), low) for n, rows, cols in ((3, 16, 512), (3, 32, 256), (6, 16, 256), (3, 16, D))
          for lead in (8, 4, 2, 1)],
        SEM((9,)), SEM((2,)), SEM((6,)), SEM((N_PARTS, 11)), SEM((N_PARTS, 11)), SEM((2, 7)), SEM((2, 7))]
    return pl.pallas_call(
        back_kernel,
        in_specs=[any_spec] * 13 + [vmem] * 9,
        out_specs=[vmem, vmem, vmem],
        out_shape=[S((CLIPS_HERE, 1, PATCH, D), low), S((N_PARTS, 16, D), f32), S((3, 32, 256), f32)],
        scratch_shapes=scratch,
        compiler_params=pltpu.CompilerParams(collective_id=2, has_side_effects=True, vmem_limit_bytes=62 * 2**20),
        name="back_and_sums",
    )(to_units(d_expand), d_shrink.reshape(8, 2, 192, D), after, proj, probs, frames, first_low, mixed, wp, wo, mw, mp, mo,
      vec, message, sums, *saved, index_table())


def unpack_kernel(out, out_s, mw, mp, mo, ap, ao, ew, sw, small):
    def piece(n, side, w):
        return out[n, 8 * side : 8 * side + 6, 0:w]

    mw[...] = piece(12, 0, D)
    for k, (n, side) in enumerate(((12, 1), (13, 0), (13, 1))):
        mp[:, k * D : (k + 1) * D] = piece(n, side, D)
    mo[...] = piece(14, 0, D)
    for k in range(3):
        for side in range(2):
            ap[:, 512 * k + 256 * side : 512 * k + 256 * side + 256] = piece(6 + 2 * k, side, 256)
            ew[:, 1024 * k + 512 * side : 1024 * k + 512 * side + 512] = piece(2 * k, side, 512)
            x = 512 * k + 256 * side
            target, x = (ap, x + 1536) if x < D else (ao, x - D)
            target[:, x : x + 256] = piece(7 + 2 * k, side, 256)
        sw[:, 256 * k : 256 * (k + 1)] = out_s[k, 0:24]
    lanes = lax.broadcasted_iota(jnp.int32, (6, 128), 1)
    rows = lax.broadcasted_iota(jnp.int32, (6, 128), 0)
    values = out[14, 8:14, 0:128]
    flat = jnp.zeros((128, 128), f32)
    for shift in range(4):
        place_at = (lanes == rows + 6 * shift).astype(f32)
        owner = jnp.where((lanes < 24) | (lanes >= 32), 0, jnp.where(lanes < 28, lanes - 24, (lanes - 28) & 1))
        part = jnp.where(owner == shift, values, 0.0)
        flat += lax.dot_general(part, place_at, (((0,), (0,)), ((), ())), precision=PRECISE, preferred_element_type=f32)
    small[...] = flat[0:32]
    small[24:25] = jnp.sum(flat[24:28], axis=0, keepdims=True)
    small[28:29] = jnp.sum(flat[28:30], axis=0, keepdims=True)
    small[30:31] = jnp.sum(flat[30:32], axis=0, keepdims=True)


def unpack(out, out_s):
    S = jax.ShapeDtypeStruct
    vmem = pl.BlockSpec(memory_space=pltpu.VMEM)
    shapes = [(6, D), (6, 3 * D), (6, D), (6, 3 * D), (6, D), (6, FF), (24, D), (32, 128)]
    return pl.pallas_call(
        unpack_kernel,
        in_specs=[vmem, vmem],
        out_specs=[vmem] * 8,
        out_shape=[S(shape, f32) for shape in shapes],
        compiler_params=pltpu.CompilerParams(vmem_limit_bytes=BIG),
        name="unpack",
    )(out, out_s)


def mlp_loss_kernel(second_low, resid, vec, gids, we_ref, ws_ref, hidden_ref, dgate_ref, result, loss, pooled_out, gpool,
                    we, ws, hid, dg, acc, cls, all_cls, every, natural, grads,
                    load_sem, store_sem, send_sem, recv_sem, near_send, near_recv):
    at = place()
    fr = lax.axis_index("frame")
    loads = []
    for j in range(4):
        for n, (src, dst) in enumerate(((we_ref.at[:, pl.ds(j * D, D)], we.at[j]), (ws_ref.at[pl.ds(j * D, D)], ws.at[j]))):
            copy = pltpu.make_async_copy(src, dst, load_sem.at[n, j])
            copy.start()
            loads.append(copy)
    around = frame_partners()
    order = ("c",) + CLIP_DIMS
    partner = {d: device_of(moved(at, {d: 1})) for d in order}
    greet(around + [partner[d] for d in order])

    def gate(h):
        sg = 1.0 / (1.0 + jnp.exp(-1.702 * h))
        hs = h * sg
        return sg, hs

    tops = jnp.concatenate([second_low[pl.ds(c * ROWS, 16)] for c in range(CLIPS_HERE)], axis=0)
    total = jnp.zeros((16 * CLIPS_HERE, D), f32)
    for j in range(4):
        loads[2 * j].wait()
        _, hs = gate(dot(tops, we[j]) + vec[R_EB + j : R_EB + j + 1])
        loads[2 * j + 1].wait()
        total += dot(hs.astype(low), ws[j])
    cls[...] = jnp.zeros((SLOT, D), f32)
    for c in range(CLIPS_HERE):
        cls[c : c + 1] = resid[c * ROWS : c * ROWS + 1] + vec[R_SB : R_SB + 1] + total[16 * c : 16 * c + 1]
    near = [remote(cls, all_cls.at[fr], near_send.at[k], near_recv.at[k], p) for k, p in enumerate(around)]
    all_cls[fr] = cls[...]

    copies, state = [], {}

    def exchange(k):
        copy = remote(every.at[pl.ds(0, 2**k)], every.at[pl.ds(2**k, 2**k)], send_sem.at[k], recv_sem.at[k],
                      partner[order[k]])
        copies.append(copy)

    def step(k):
        if k == 0:
            for copy in near:
                copy.wait_recv()
            s = all_cls[0]
            for f in range(1, FRAMES):
                s = s + all_cls[f]
            pooled = s * 0.125
            pooled_out[...] = pooled[:CLIPS_HERE]
            inv_len = lax.rsqrt(jnp.sum(pooled * pooled, axis=-1, keepdims=True) + 1e-06)
            state.update(pooled=pooled, inv_len=inv_len)
            every[0] = pooled * inv_len
        else:
            copies[k - 1].wait_recv()
        if k < 4:
            exchange(k)

    stores = []
    for j in range(4):
        if j >= 2:
            for copy in stores[2 * (j - 2) : 2 * (j - 1)]:
                copy.wait()
        for part in range(2):
            rows = pl.ds(part * 2 * ROWS, 2 * ROWS)
            h = dot(second_low[rows], we[j]) + vec[R_EB + j : R_EB + j + 1]
            sg, hs = gate(h)
            hidden = hs.astype(low)
            hid[j % 2, rows] = hidden
            dg[j % 2, rows] = (sg + 1.702 * hs * (1.0 - sg)).astype(low)
            out = dot(hidden, ws[j])
            acc[rows] = (resid[rows] + vec[R_SB : R_SB + 1] if j == 0 else acc[rows]) + out
            k = 2 * j + part - 2
            if 0 <= k <= 4:
                step(k)
        for n, (src, dst) in enumerate(((hid, hidden_ref), (dg, dgate_ref))):
            copy = pltpu.make_async_copy(src.at[j % 2], dst.at[:, pl.ds(j * D, D)], store_sem.at[n, j])
            copy.start()
            stores.append(copy)
    for c in range(CLIPS_HERE):
        result[c, 0] = acc[pl.ds(c * ROWS, PATCH)].astype(low)
    for p in range(16):
        to = moved(at, {d: (p >> k) & 1 for k, d in enumerate(order)})
        natural[dp_of(to)] = every[p]
    n = natural[...].reshape(128, D)
    sims = 50.0 * lax.dot_general(n, n, (((1,), (1,)), ((), ())), precision=PRECISE, preferred_element_type=f32)
    rows = lax.broadcasted_iota(jnp.int32, (128, 128), 0)
    cols = lax.broadcasted_iota(jnp.int32, (128, 128), 1)
    here = (cols & 7) < CLIPS_HERE
    other = here & (rows != cols)
    slot = lax.broadcasted_iota(jnp.int32, (128, 64), 0)
    clip = lax.broadcasted_iota(jnp.int32, (128, 64), 1)
    spot = (((slot >> 3) * CLIPS_HERE + (slot & 7)) == clip) & ((slot & 7) < CLIPS_HERE)
    wide = jnp.broadcast_to(gids[...].astype(f32), (128, 64))
    mine = jnp.where(spot, wide, 0.0)
    gid_col = jnp.sum(mine, axis=-1, keepdims=True)
    gid_row = lax.dot_general(wide, spot.astype(f32), (((1,), (1,)), ((), ())), precision=PRECISE, preferred_element_type=f32)
    same = other & (gid_col == gid_row)
    valid = (lax.broadcasted_iota(jnp.int32, (128, 1), 0) & 7) < CLIPS_HERE

    def log_soft(logits):
        top = jnp.max(logits, axis=-1, keepdims=True)
        e = jnp.exp(logits - top)
        total = jnp.sum(e, axis=-1, keepdims=True)
        return top + jnp.log(total), e / total

    all_log, all_p = log_soft(jnp.where(other, sims, -1e30))
    pos_log, pos_p = log_soft(jnp.where(same, sims, -1e30))
    terms = jnp.where(valid, all_log - pos_log, 0.0)
    loss[...] = jnp.sum(terms, axis=0, keepdims=True) * (1.0 / 64.0)
    gs = jnp.where(valid & here, all_p - pos_p, 0.0)
    grad_all = 50.0 * jnp.dot(gs + gs.T, n, precision=PRECISE, preferred_element_type=f32)
    grads[...] = grad_all.reshape(16, SLOT, D)
    g = grads[lax.axis_index("dp")]
    pooled, inv_len = state["pooled"], state["inv_len"]
    back = inv_len * g - inv_len * inv_len * inv_len * pooled * jnp.sum(pooled * g, axis=-1, keepdims=True)
    gpool[...] = back * 0.125
    for copy in stores[4:]:
        copy.wait()
    for copy in near + copies:
        copy.wait_send()


def mlp_loss(second_low, resid, vec, gids, we, ws):
    vmem = pl.BlockSpec(memory_space=pltpu.VMEM)
    any_spec = pl.BlockSpec(memory_space=pl.ANY)
    S, V, SEM = jax.ShapeDtypeStruct, pltpu.VMEM, pltpu.SemaphoreType.DMA
    return pl.pallas_call(
        mlp_loss_kernel,
        in_specs=[vmem] * 4 + [any_spec] * 2,
        out_specs=[any_spec] * 2 + [vmem] * 4,
        out_shape=[S((ALL, FF), low), S((ALL, FF), low), S((CLIPS_HERE, 1, PATCH, D), low), S((1, 1), f32),
                   S((CLIPS_HERE, D), f32), S((SLOT, D), f32)],
        scratch_shapes=[
            V((4, D, D), low), V((4, D, D), low), V((2, ALL, D), low), V((2, ALL, D), low), V((ALL, D), f32),
            V((SLOT, D), f32), V((FRAMES, SLOT, D), f32), V((16, SLOT, D), f32), V((16, SLOT, D), f32),
            V((16, SLOT, D), f32), SEM((2, 4)), SEM((2, 4)), SEM((4,)), SEM((4,)), SEM((7,)), SEM((7,))],
        compiler_params=pltpu.CompilerParams(collective_id=1, has_side_effects=True, vmem_limit_bytes=BIG),
        name="mlp_loss",
    )(second_low, resid, vec, gids, we, ws)


def on_device(
    frames, cotangent, group_ids, message_weight, message_bias, message_gain, message_shift, message_project,
    message_project_bias, message_output, message_output_bias, first_gain, first_shift, attend_project,
    attend_project_bias, attend_output, attend_output_bias, second_gain, second_shift, expand_weight, expand_bias,
    shrink_weight, shrink_bias,
):
    vectors = (
        message_bias, message_gain, message_shift, message_project_bias, message_output_bias, first_gain, first_shift,
        attend_project_bias, attend_output_bias, second_gain, second_shift, expand_bias, shrink_bias,
    )
    vec, message, *saved = message_forward(vectors, frames, message_weight, message_project, message_output)
    first_low, proj, probs, mixed, resid, second_low = attend_forward(frames, message, vec, attend_project, attend_output)
    hidden, dgate, result, loss, pooled, gpool = mlp_loss(
        second_low, resid, vec, group_ids.reshape(1, 64), expand_weight, shrink_weight)
    d_shrink, d_expand, after, sums = mlp_back(
        cotangent, gpool, vec, hidden, dgate, second_low, expand_weight, shrink_weight, resid)
    delta_frames, out, out_s = back_and_sums(
        d_expand, d_shrink, after, proj, probs, frames, first_low, mixed, attend_project, attend_output, message_weight,
        message_project, message_output, vec, message, sums, saved)
    mw, mp, mo, ap, ao, ew, sw, small = unpack(out, out_s)

    def lanes(row, count=1):
        return small[row, : 6 * count]

    return (
        result, loss.reshape(()), pooled, delta_frames,
        mw, lanes(12), lanes(13), lanes(14), mp, lanes(30, 2), mo, lanes(17),
        lanes(0), lanes(1), ap, lanes(28, 2), ao, lanes(4), lanes(5), lanes(6), ew, lanes(24, 4), sw, lanes(11),
    )


def solution(mesh):
    placed = (
        P("dp", "frame", None, None),
        P("dp", "frame", None, None),
        P(),
        P(),
        P(),
        P(),
        P(),
        P(),
        P(),
        P(),
        P(),
        P(),
        P(),
        P(),
        P(),
        P(),
        P(),
        P(),
        P(),
        P(),
        P(),
        P(),
        P(),
    )
    return jax.shard_map(
        on_device,
        mesh=mesh,
        in_specs=placed,
        out_specs=(
            P("dp", "frame", None, None),
            P(),
            P("dp", None),
            P("dp", "frame", None, None),
            P(("dp", "frame"), None),
            P(("dp", "frame")),
            P(("dp", "frame")),
            P(("dp", "frame")),
            P(("dp", "frame"), None),
            P(("dp", "frame")),
            P(("dp", "frame"), None),
            P(("dp", "frame")),
            P(("dp", "frame")),
            P(("dp", "frame")),
            P(("dp", "frame"), None),
            P(("dp", "frame")),
            P(("dp", "frame"), None),
            P(("dp", "frame")),
            P(("dp", "frame")),
            P(("dp", "frame")),
            P(("dp", "frame"), None),
            P(("dp", "frame")),
            P(("dp", "frame"), None),
            P(("dp", "frame")),
        ),
        check_vma=False,
    )
```

```python
import functools

import jax
import jax.numpy as jnp
import numpy as np
from jax import lax
from jax.experimental import pallas as pl
from jax.experimental.pallas import tpu as pltpu
from jax.sharding import PartitionSpec as P

f32, low = jnp.float32, jnp.bfloat16
CLIPS_HERE, PATCH, ROWS, D, FF = 4, 197, 208, 768, 3072
ALL = CLIPS_HERE * ROWS
BIG = 58 * 2**20
(R_MB, R_MG, R_MS, R_MPB, R_MOB, R_FG, R_FS, R_APB, R_AOB, R_SG, R_SS, R_EB, R_SB) = (
    0, 1, 2, 3, 6, 7, 8, 9, 12, 13, 14, 15, 19)


def dot(a, b):
    return jnp.dot(a, b, preferred_element_type=f32)


def dot_t(a, b):
    return lax.dot_general(a, b, (((1,), (1,)), ((), ())), preferred_element_type=f32)


def dot_tl(a, b):
    return lax.dot_general(a, b, (((0,), (0,)), ((), ())), preferred_element_type=f32)


def stats(x):
    mean = jnp.mean(x, axis=-1, keepdims=True)
    centered = x - mean
    inv = lax.rsqrt(jnp.mean(centered * centered, axis=-1, keepdims=True) + 1e-05)
    return centered * inv, inv


def norm_back(grad, u, inv, gain):
    h = grad * gain
    return (h - jnp.mean(h, axis=-1, keepdims=True) - u * jnp.mean(h * u, axis=-1, keepdims=True)) * inv


def const(shape):
    return pl.BlockSpec(shape, lambda *i: (0,) * len(shape))


def mlp_back_kernel(cot, gpool, vec, hidden, dgate, second_low, we, ws, resid,
                    d_shrink, d_expand, after, sums, gl, gb, gsec):
    j = pl.program_id(0)

    @pl.when(j == 0)
    def _():
        gl[...] = jnp.zeros((ALL, D), f32)
        for c in range(CLIPS_HERE):
            gl[pl.ds(c * ROWS, PATCH)] = cot[c, 0].astype(f32)
            gl[pl.ds(c * ROWS, 1)] += gpool[pl.ds(c, 1)]
        gb[...] = gl[...].astype(low)
        gsec[...] = jnp.zeros((ALL, D), f32)
        sums[...] = jnp.zeros((24, D), f32)
        sums[11:12] = jnp.sum(gb[...].astype(f32), axis=0, keepdims=True)

    d_shrink[...] = dot_tl(hidden[...], gb[...]).astype(low)
    ghp = (dot_t(gb[...], ws[...]) * dgate[...].astype(f32)).astype(low)
    sums[pl.ds(7 + j, 1)] = jnp.sum(ghp.astype(f32), axis=0, keepdims=True)
    d_expand[...] = dot_tl(second_low[...], ghp).astype(low)
    gsec[...] += dot_t(ghp, we[...])

    @pl.when(j == 3)
    def _():
        gain = vec[R_SG : R_SG + 1]
        total = [jnp.zeros((1, D), f32) for _ in range(3)]
        for c in range(CLIPS_HERE):
            rows = pl.ds(c * ROWS, ROWS)
            u, inv = stats(resid[rows])
            g = gsec[rows]
            out = gl[rows] + norm_back(g, u, inv, gain)
            after[rows] = out
            total[0] += jnp.sum(g * u, axis=0, keepdims=True)
            total[1] += jnp.sum(g, axis=0, keepdims=True)
            total[2] += jnp.sum(out.astype(low).astype(f32), axis=0, keepdims=True)
        sums[5:6] = total[0]
        sums[6:7] = total[1]
        sums[4:5] = total[2]


def mlp_back(cot, gpool, vec, hidden, dgate, second_low, we, ws, resid):
    tile = pl.BlockSpec((ALL, D), lambda j: (0, j))
    return pl.pallas_call(
        mlp_back_kernel,
        grid=(4,),
        in_specs=[const((CLIPS_HERE, 1, PATCH, D)), const((8, D)), const((24, D)), tile, tile, const((ALL, D)),
                  pl.BlockSpec((D, D), lambda j: (0, j)), pl.BlockSpec((D, D), lambda j: (j, 0)), const((ALL, D))],
        out_specs=[pl.BlockSpec((D, D), lambda j: (j, 0)), pl.BlockSpec((D, D), lambda j: (0, j)), const((ALL, D)),
                   const((24, D))],
        out_shape=[jax.ShapeDtypeStruct((FF, D), low), jax.ShapeDtypeStruct((D, FF), low),
                   jax.ShapeDtypeStruct((ALL, D), f32), jax.ShapeDtypeStruct((24, D), f32)],
        scratch_shapes=[pltpu.VMEM((ALL, D), f32), pltpu.VMEM((ALL, D), low), pltpu.VMEM((ALL, D), f32)],
        compiler_params=pltpu.CompilerParams(vmem_limit_bytes=BIG),
        name="mlp_back",
    )(cot, gpool, vec, hidden, dgate, second_low, we, ws, resid)


MESH = pl.DeviceIdType.MESH


def flip_low(index):
    return index + 1 - 2 * (index % 2)


def flip_pair(index, high, low):
    index = 3 - index if high else index
    return flip_low(index) if low else index


def place():
    dp, fr = lax.axis_index("dp"), lax.axis_index("frame")
    return dict(y=dp // 4, x=(dp // 2 % 2) * 2 + fr // 4, z=fr % 4, c=dp % 2)


def moved(at, bits):
    return dict(
        y=flip_pair(at["y"], bits.get("yu"), bits.get("yv")),
        x=flip_pair(at["x"], bits.get("xu"), bits.get("xv")),
        z=flip_pair(at["z"], bits.get("zu"), bits.get("zv")),
        c=1 - at["c"] if bits.get("c") else at["c"],
    )


def dp_of(at):
    return at["y"] * 4 + (at["x"] // 2) * 2 + at["c"]


def frame_of(at):
    return (at["x"] % 2) * 4 + at["z"]


def device_of(at):
    return (dp_of(at), frame_of(at))


CLIP_DIMS = ("yu", "yv", "xu")
FRAME_DIMS = ("xv", "zu", "zv")


def rotated(dims, turn):
    return dims[turn:] + dims[:turn]


def bits_at(dims, position):
    return {dims[k]: (position >> (2 - k)) & 1 for k in range(3)}


def to_units(full):
    return full.reshape(8, 2, 48, full.shape[-1])


FRAMES = 8
SLOT = 8
MROWS = FRAMES * SLOT
SUMS = 24


def greet(partners):
    barrier = pltpu.get_barrier_semaphore()
    for partner in partners:
        pl.semaphore_signal(barrier, inc=1, device_id=partner, device_id_type=MESH)
    pl.semaphore_wait(barrier, len(partners))


def frame_partners():
    dp, fr = lax.axis_index("dp"), lax.axis_index("frame")
    return [(dp, lax.rem(fr + k, FRAMES)) for k in range(1, FRAMES)]


def remote(src, dst, send_sem, recv_sem, device):
    copy = pltpu.make_async_remote_copy(
        src_ref=src, dst_ref=dst, send_sem=send_sem, recv_sem=recv_sem, device_id=device, device_id_type=MESH)
    copy.start()
    return copy


def same_clip():
    rows = lax.broadcasted_iota(jnp.int32, (MROWS, MROWS), 0)
    cols = lax.broadcasted_iota(jnp.int32, (MROWS, MROWS), 1)
    return rows % SLOT == cols % SLOT


def soft(s):
    e = jnp.exp(s - jnp.max(s, axis=-1, keepdims=True))
    return e / jnp.sum(e, axis=-1, keepdims=True)


VECTORS = ((R_MB,), (R_MG,), (R_MS,), (R_MPB, R_MPB + 2), (R_MOB,), (R_FG,), (R_FS,), (R_APB, R_APB + 2), (R_AOB,), (R_SG,),
           (R_SS,), (R_EB, R_EB + 1, R_EB + 2, R_EB + 3), (R_SB,))


PRECISE = lax.Precision.HIGHEST


def message_back(at, cls_all, pre, normed, qkv, mixed, vec, vw, vp, vo, gall, pick, mgrad, gcls, between):
    fr = lax.axis_index("frame")
    g = gall[...].reshape(MROWS, D)
    g_low = g.astype(low)
    gmm = dot_t(g_low, vo[...]).astype(low)
    keep = same_clip()
    lane = lax.broadcasted_iota(jnp.int32, (MROWS, 128), 1)
    zero = jnp.zeros((), low)
    parts = ([], [], [])
    for pair in range(6):
        q = qkv[:, pair * 128 : pair * 128 + 128]
        k = qkv[:, D + pair * 128 : D + pair * 128 + 128]
        v = qkv[:, 2 * D + pair * 128 : 2 * D + pair * 128 + 128]
        gm = gmm[:, pair * 128 : pair * 128 + 128]
        outs = []
        for half in range(2):
            mine = (lane < 64) if half == 0 else (lane >= 64)
            p = soft(jnp.where(keep, dot_t(jnp.where(mine, q, zero), k) * 0.125, -1e30))
            dp = dot_t(jnp.where(mine, gm, zero), v)
            gs = (p * (dp - jnp.sum(dp * p, axis=-1, keepdims=True))).astype(low)
            outs.append((dot(gs, k), dot_tl(gs, q), dot_tl(p.astype(low), gm)))
        for n, scale in ((0, 0.125), (1, 0.125), (2, 1.0)):
            parts[n].append((jnp.where(lane < 64, outs[0][n], outs[1][n]) * scale).astype(low))
    gq, gk, gv = (jnp.concatenate(part, axis=1) for part in parts)
    between()
    gnorm = dot_t(gq, vp[:, :D]) + dot_t(gk, vp[:, D : 2 * D]) + dot_t(gv, vp[:, 2 * D :])
    u, inv = stats(pre[...])
    gpre = (g + norm_back(gnorm, u, inv, vec[R_MG : R_MG + 1])).astype(low)

    def total(value):
        return jnp.sum(value.astype(f32), axis=0, keepdims=True)

    mine = (lax.broadcasted_iota(jnp.int32, (96, D), 1) == pick[0:96]).astype(low)
    x = cls_all[...].reshape(MROWS, D).astype(low)
    for unit, (left, right) in enumerate(((x, gpre), (normed[...], gq), (normed[...], gk), (normed[...], gv),
                                          (mixed[...], g_low))):
        turned = dot_t(mine, left).astype(low)
        mgrad[:, :, unit * D : (unit + 1) * D] = dot(turned, right).astype(low).reshape(2, 48, D)
    back = dot_t(gpre, vw[...])
    rows = lax.broadcasted_iota(jnp.int32, (MROWS, 1), 0) // SLOT
    gcls[...] = jnp.sum(jnp.where(rows == fr, back, 0.0).reshape(FRAMES, SLOT, D), axis=0)
    return [total(gpre), total(gnorm * u), total(gnorm), total(gq), total(gv), total(g_low)]


def message_vectors(sums, message_sums, pick, part, mgrad):
    table = jnp.concatenate([sums[0:12], *message_sums, jnp.zeros((SUMS - 18, D), f32)], axis=0).astype(low)
    choose = (lax.broadcasted_iota(jnp.int32, (672, D), 1) == pick[...]).astype(low)
    z = dot_t(choose, table)
    wide = lax.broadcasted_iota(jnp.int32, (96, 128), 1)
    narrow = lax.broadcasted_iota(jnp.int32, (96, SUMS), 1)
    out = jnp.zeros((96, 128), f32)
    out += jnp.concatenate([z[:96], jnp.zeros((96, 128 - SUMS), f32)], axis=1)
    for q in range(4):
        hit = narrow == 7 + part[384:480, 3:4]
        value = jnp.sum(jnp.where(hit, z[96 * (1 + q) : 96 * (2 + q)], 0.0), axis=-1, keepdims=True)
        out = jnp.where(wide == 24 + q, value, out)
    for q in range(2):
        for n, first in enumerate((2, 15)):
            hit = narrow == first + part[384:480, 4:5]
            value = jnp.sum(jnp.where(hit, z[96 * (5 + q) : 96 * (6 + q)], 0.0), axis=-1, keepdims=True)
            out = jnp.where(wide == 28 + 2 * n + q, value, out)
    mgrad[:, :, 5 * D : 5 * D + 128] = out.astype(low).reshape(2, 48, 128)
    mgrad[:, :, 5 * D + 128 :] = jnp.zeros((2, 48, D - 128), low)


def index_table():
    table = np.zeros((384 + 672, 8), np.int32)
    r = np.arange(384)
    table[:384, 0] = r // 48
    table[:384, 1] = r % 48 // 6 * 48 + r % 6
    table[:384, 2] = r % 48 // 6 % 2
    r = np.arange(96)
    c, y, xh, i = r // 48, r % 48 // 12, r % 12 // 6, r % 6
    high = y * 4 + xh * 2 + c
    picks = [(high * 48 + i, 6)]
    picks += [(high % 4 * 192 + q * 6 + i, 24) for q in range(4)]
    picks += [(high % 8 * 96 + q * 6 + i, 12) for q in range(2)]
    for n, (base, step) in enumerate(picks):
        rows = slice(384 + 96 * n, 384 + 96 * (n + 1))
        table[rows, 0], table[rows, 1], table[rows, 2] = base, step, xh
        table[rows, 3], table[rows, 4] = y, y // 2
    return jnp.asarray(table)


def fill_orders(at, table, sa, sb, mix, pick):
    xh, xl = at["x"] // 2, at["x"] % 2
    rows = lax.broadcasted_iota(jnp.int32, (128, 48), 0)
    cols = lax.broadcasted_iota(jnp.int32, (128, 48), 1)
    for ref, dims in ((sa, FRAME_DIMS), (sb, CLIP_DIMS)):
        block = jnp.zeros((128, 48), jnp.int32)
        for p in range(8):
            to = moved(at, bits_at(dims, p))
            value = frame_of(to) if dims == FRAME_DIMS else dp_of(to) // 2
            block = jnp.where((rows >> 4) == p, value, block)
        for half in range(2):
            inner = (rows & 15) - 8 * half
            hit = (cols == block * 6 + inner) & (inner >= 0) & (inner < 6)
            ref[half] = hit.astype(f32).astype(low)
    lanes = lax.broadcasted_iota(jnp.int32, (384, 384), 1)
    p_col, base, same = table[0:384, 0:1], table[0:384, 1:2], table[0:384, 2:3] == xh
    for turn in range(3):
        frame = jnp.zeros((384, 1), jnp.int32)
        for p in range(8):
            to = moved(at, bits_at(rotated(FRAME_DIMS, turn), p))
            side = to["x"] % 2
            frame = jnp.where(p_col == p, jnp.where(same, 4 * side + to["z"], 4 * (1 - side) + to["z"]), frame)
        mix[turn] = (lanes == base + 6 * frame).astype(f32).astype(low)
    base, step, same = table[384:, 0:1], table[384:, 1:2], table[384:, 2:3] == xh
    pick[...] = base + step * jnp.where(same, 4 * xl + at["z"], 4 * (1 - xl) + at["z"])


CORE, S1, S2, S3 = 0, 1, 5, 7
KEEP = (4, 2, 1)
KIND = ("a", "s") * 3 + ("a", "b") * 3 + ("m",) * 3
TURN = (0, 0, 1, 1, 2, 2) * 2 + (0, 1, 2)
N_PARTS = 15


GROUPS = (
    ((0, 2, 4), 16, 512, FRAME_DIMS), ((1, 3, 5), 32, 256, CLIP_DIMS), ((6, 8, 10), 16, 256, FRAME_DIMS),
    ((7, 9, 11), 16, 256, CLIP_DIMS), ((12, 13, 14), 16, 768, CLIP_DIMS),
)
FEED_A, FEED_S, LATE_A, LATE_B, MESSAGE = range(5)


def order_of(n):
    return rotated(CLIP_DIMS if KIND[n] == "a" else FRAME_DIMS, TURN[n])


def back_kernel(
    e_ref, s_ref, after_ref, proj_ref, probs_ref, frames_ref, first_ref, mixed_ref, wp_ref, wo_ref, mw_ref, mp_ref, mo_ref,
    vec, message, sums_in, cls_all, pre, normed, qkv, msg_mixed, table,
    tokens, out, out_s,
    wp, wo, mw, mo, after, proj, probs, frames, first_low, mixed, xs, gm_all, heads, sums, gmsg, gcls, mgrad, mgot,
    gall, sums_low, sall, sa, sb, mix, pick, wide_s,
    own_a, got_a, ra1, ra2, ra3, own_s, got_s, rs1, rs2, rs3, late, got_l, rl1, rl2, rl3,
    t0, t1, t2, t3, t4, v0, v1, v2, v3, v4,
    load_sem, probs_sem, local_sem, send_sem, recv_sem, near_send, near_recv, last_send, last_recv,
):
    at = place()
    fr = lax.axis_index("frame")
    core = at["c"]
    around = frame_partners()
    partners = {d: device_of(moved(at, {d: 1})) for d in ("c",) + CLIP_DIMS + FRAME_DIMS}

    def load(n, src, dst):
        copy = pltpu.make_async_copy(src, dst, load_sem.at[n])
        copy.start()
        return copy

    def probs_copy(clip):
        return pltpu.make_async_copy(probs_ref.at[clip], probs.at[clip % 2], probs_sem.at[clip % 2])

    probs_copy(0).start()
    get_wo, get_after, get_proj = load(0, wo_ref, wo), load(1, after_ref, after), load(2, proj_ref, proj)
    clip_cube = [device_of(moved(at, bits_at(CLIP_DIMS, p))) for p in range(1, 8)]
    greet(around + clip_cube + [partners["c"]])

    def mine(n, lead):
        if n < 6:
            return (own_a if n % 2 == 0 else own_s).at[n // 2, lead]
        return late.at[n % 2, lead, core, :, pl.ds((n - 6) // 2 * 512, 512)]

    def got(n):
        if n < 6:
            return (got_a if n % 2 == 0 else got_s).at[n // 2]
        return got_l.at[n - 6]

    def half(n, s):
        if n < 6:
            return ((ra1, ra2, ra3) if n % 2 == 0 else (rs1, rs2, rs3))[s - 1].at[n // 2]
        return (rl1, rl2, rl3)[s - 1].at[n - 6]

    kept_blocks, sent_blocks = (t0, t1, t2, t3, t4), (v0, v1, v2, v3, v4)

    def group_of(n):
        return next((g, group[0].index(n), group) for g, group in enumerate(GROUPS) if n in group[0])

    def chunk_at(n, p):
        return dp_of(moved(at, bits_at(order_of(n), p))) // 2

    def source(n, which):
        if n < 6:
            step = 1024 if n % 2 == 0 else 256
            return (e_ref if n % 2 == 0 else s_ref).at[:, which, :, pl.ds(n // 2 * step, step)]
        return late.at[n % 2, :, which, :, pl.ds((n - 6) // 2 * 512, 512)]

    def local(n):
        return pltpu.make_async_copy(source(n, core), mine(n, pl.ds(0, 8)), local_sem.at[n])

    registry = {}

    def define(n, step, src, dst, dim):
        def make():
            return pltpu.make_async_remote_copy(
                src_ref=src(), dst_ref=dst(), send_sem=send_sem.at[n, step], recv_sem=recv_sem.at[n, step],
                device_id=partners[dim], device_id_type=MESH)
        registry[n, step] = make

    def define_part(n):
        if KIND[n] != "m":
            define(n, CORE, lambda: source(n, 1 - core), lambda: got(n), "c")
            for s, first in ((1, S1), (2, S2), (3, S3)):
                keep, dim = KEEP[s - 1], order_of(n)[s - 1]
                if KIND[n] == "a":
                    for p in range(keep):
                        define(n, first + p, lambda p=p, keep=keep: mine(n, chunk_at(n, keep + p)),
                               lambda p=p, s=s: half(n, s).at[p], dim)
                else:
                    define(n, first, lambda keep=keep: mine(n, pl.ds(keep, keep)), lambda s=s: half(n, s), dim)

    def last_copy(g, p):
        return pltpu.make_async_remote_copy(
            src_ref=kept_blocks[g].at[p], dst_ref=sent_blocks[g].at[p - 1], send_sem=last_send.at[g, p - 1],
            recv_sem=last_recv.at[g, p - 1], device_id=device_of(moved(at, bits_at(GROUPS[g][3], p))),
            device_id_type=MESH)

    for n in range(N_PARTS):
        define_part(n)

    def start(n, step):
        registry[n, step]().start()

    def arrived(n, step):
        registry[n, step]().wait_recv()

    fill_orders(at, table, sa, sb, mix, pick)
    sums[...] = sums_in[...]
    gmsg[...] = jnp.zeros((SLOT, D), f32)

    def steps_of(n, s):
        first = (S1, S2, S3)[s - 1]
        return range(first, first + KEEP[s - 1]) if KIND[n] == "a" else (first,)

    def frame_at(n, p, chunk):
        to = moved(at, bits_at(order_of(n), p))
        side = lax.rem(to["x"] % 2 + at["x"] // 2 + chunk % 2, 2)
        return side * 4 + to["z"]

    def begin(n):
        if n < 6:
            local(n).wait()
        arrived(n, CORE)
        if KIND[n] == "a":
            for chunk in range(8):
                ref = mine(n, chunk)
                ref[...] = ref[...] + got(n)[chunk]
        elif KIND[n] == "b":
            ref = mine(n, pl.ds(0, 8))
            full = (ref[...] + got(n)[...]).reshape(384, 512)
            ref[...] = dot(mix[TURN[n]], full).astype(low).reshape(8, 48, 512)
        else:
            for chunk in range(8):
                wide_s[chunk] = (mine(n, chunk)[...] + got(n)[chunk]).astype(f32).reshape(8, 24, 256)
            for p in range(8):
                for two in range(0, 8, 2):
                    rows = [wide_s[two + k, frame_at(n, p, two + k)] for k in range(2)]
                    mine(n, p)[pl.ds(24 * two, 48)] = jnp.concatenate(rows, axis=0).astype(low)
        for step in steps_of(n, 1):
            start(n, step)

    def spread(n, last):
        g, k, (_, _, w, dims) = group_of(n)
        blocks, cols = kept_blocks[g], pl.ds(k * w, w)
        if KIND[n] == "s":
            wide_s[0] = last.astype(f32).reshape(8, 24, 256)
            for p in range(8):
                chunk = dp_of(moved(at, bits_at(dims, p))) // 2
                rows = jnp.concatenate([wide_s[0, chunk], jnp.zeros((8, 256), f32)], axis=0)
                blocks[p, :, cols] = rows.astype(low)
        else:
            orders = sa if dims == FRAME_DIMS else sb
            wide = dot(orders[0], last[:, :w]) + dot(orders[1], last[:, w:])
            blocks[:, :, cols] = wide.astype(low).reshape(8, 16, w)

    def send_last(g):
        for p in range(1, 8):
            last_copy(g, p).start()

    def finish(g):
        parts, _, w, _ = GROUPS[g]
        total = kept_blocks[g][0].astype(f32)
        for p in range(1, 8):
            last_copy(g, p).wait_recv()
            total = total + sent_blocks[g][p - 1].astype(f32)
        for k, n in enumerate(parts):
            if KIND[n] == "s":
                out_s[k] = total[:, k * w : (k + 1) * w]
            else:
                out[n, :, 0:w] = total[:, k * w : (k + 1) * w]

    def middle(n, s):
        keep = KEEP[s - 1]
        for step in steps_of(n, s):
            arrived(n, step)
        if s == 3:
            lead = chunk_at(n, 0) if KIND[n] == "a" else 0
            spread(n, mine(n, lead)[...] + half(n, 3)[0])
            return
        if KIND[n] == "a":
            for p in range(keep):
                kept = mine(n, chunk_at(n, p))
                kept[...] = kept[...] + half(n, s)[p]
        else:
            kept = mine(n, pl.ds(0, keep))
            kept[...] = kept[...] + half(n, s)[...]
        for step in steps_of(n, s + 1):
            start(n, step)

    def every(action, parts, *args):
        for n in parts:
            action(n, *args)

    lane = lax.broadcasted_iota(jnp.int32, (ROWS, 128), 1)
    zero = jnp.zeros((), low)
    get_wo.wait()
    get_after.wait()
    gm_all[...] = dot_t(after[...].astype(low), wo[...]).astype(low)
    get_proj.wait()
    for n in range(6):
        start(n, CORE)
        local(n).start()
    get_wp, get_first, get_mixed = load(4, wp_ref, wp), load(5, first_ref, first_low), load(6, mixed_ref, mixed)
    get_frames, get_mw, get_mo = load(3, frames_ref, frames), load(7, mw_ref, mw), load(8, mo_ref, mo)

    def one_clip(clip, carry):
        @pl.when(clip < CLIPS_HERE - 1)
        def _():
            probs_copy(clip + 1).start()

        rows = pl.ds(pl.multiple_of(clip * ROWS, 16), ROWS)
        probs_copy(clip).wait()
        for pair in range(6):
            cols = [pl.ds(n * D + pair * 128, 128) for n in range(3)]
            q, k, v = (proj[rows, c] for c in cols)
            gm = gm_all[rows, pair * 128 : pair * 128 + 128]
            outs = []
            for side in range(2):
                here = (lane < 64) if side == 0 else (lane >= 64)
                dp = dot_t(jnp.where(here, gm, zero), v)
                p_low = probs[clip % 2, 2 * pair + side]
                p = p_low.astype(f32)
                gs = (p * (dp - jnp.sum(dp * p, axis=-1, keepdims=True))).astype(low)
                outs.append((dot(gs, k), dot_tl(gs, q), dot_tl(p_low, gm)))
            for n, scale in ((0, 0.125), (1, 0.125), (2, 1.0)):
                proj[rows, cols[n]] = (jnp.where(lane < 64, outs[0][n], outs[1][n]) * scale).astype(low)

        @pl.when(clip == 1)
        def _():
            every(begin, range(3))

        @pl.when(clip == 2)
        def _():
            every(begin, range(3, 6))

        return carry

    lax.fori_loop(0, CLIPS_HERE, one_clip, 0)

    get_wp.wait()
    ends = jnp.concatenate([proj[pl.ds(c * ROWS + 192, 16)] for c in range(CLIPS_HERE)], axis=0)
    grad = jnp.zeros((16 * CLIPS_HERE, D), f32)
    for n in range(3):
        grad += dot_t(ends[:, n * D : (n + 1) * D], wp[:, n * D : (n + 1) * D])
    for c in range(CLIPS_HERE):
        gmsg[c : c + 1] = grad[16 * c + 5 : 16 * c + 6]
    u, inv = stats(message[...])
    gmsg[...] = norm_back(gmsg[...], u, inv, vec[R_FG : R_FG + 1])
    near = []
    for k, partner in enumerate(around):
        near.append(remote(gmsg, gall.at[fr], near_send.at[0, k], near_recv.at[0, k], partner))
    gall[fr] = gmsg[...]
    get_first.wait()
    get_mixed.wait()

    def late_grad(side, first, stop, left, right):
        grad = dot_tl(left[...], right)
        late[side, :, :, :, pl.ds(first, stop - first)] = grad.astype(low).reshape(8, 2, 48, stop - first)

    late_grad(0, 0, 512, first_low, proj[:, 0:512])
    start(6, CORE)
    late_grad(0, 512, 1024, first_low, proj[:, 512:1024])
    start(8, CORE)
    late_grad(0, 1024, 1536, first_low, proj[:, 1024:1536])
    start(10, CORE)
    begin(6)
    late_grad(1, 0, 768, first_low, proj[:, 1536:2304])
    start(7, CORE)
    begin(8)
    late_grad(1, 768, 1536, mixed, after[...].astype(low))
    start(9, CORE)
    start(11, CORE)
    begin(10)
    begin(7)
    begin(9)
    begin(11)
    every(middle, range(6), 1)
    for n in (0, 2):
        total = jnp.zeros((1, D), f32)
        for c in range(CLIPS_HERE):
            total += jnp.sum(proj[pl.ds(c * ROWS, ROWS), n * D : (n + 1) * D].astype(f32), axis=0, keepdims=True)
        to = 2 if n == 0 else 3
        sums[to : to + 1] = total
    get_frames.wait()

    def token_grads(first):
        two = pl.ds(first * ROWS, 2 * ROWS)
        grad_two = jnp.zeros((2 * ROWS, D), f32)
        for n in range(3):
            grad_two += dot_t(proj[two, n * D : (n + 1) * D], wp[:, n * D : (n + 1) * D])
        for clip in (first, first + 1):
            grad = grad_two[(clip - first) * ROWS : (clip - first + 1) * ROWS]
            xs[pl.ds(192, 16)] = jnp.zeros((16, D), f32)
            xs[pl.ds(0, PATCH)] = frames[clip, 0].astype(f32)
            xs[pl.ds(PATCH, 1)] = message[clip : clip + 1]
            u, inv = stats(xs[...])
            sums[0:1] += jnp.sum(grad * u, axis=0, keepdims=True)
            sums[1:2] += jnp.sum(grad, axis=0, keepdims=True)
            xs[...] = after[pl.ds(clip * ROWS, ROWS)] + norm_back(grad, u, inv, vec[R_FG : R_FG + 1])
            tokens[clip, 0] = xs[pl.ds(0, PATCH)].astype(low)
            heads[clip] = xs[pl.ds(0, 16)]

    sums[0:2] = jnp.zeros((2, D), f32)
    token_grads(0)
    every(middle, range(6), 2)
    token_grads(2)
    get_mp = load(4, mp_ref, wp)
    sums_low[...] = sums[0:16].astype(low)
    for k, partner in enumerate(around):
        near.append(remote(sums_low, sall.at[fr], near_send.at[1, k], near_recv.at[1, k], partner))
    sall[fr] = sums_low[...]
    every(middle, range(6, 12), 1)
    every(middle, range(6), 3)
    send_last(FEED_A)
    send_last(FEED_S)
    for copy in near[:7]:
        copy.wait_recv()
    get_mw.wait()
    get_mo.wait()
    get_mp.wait()
    def between():
        every(middle, range(6, 12), 2)

    vectors = message_back(
        at, cls_all, pre, normed, qkv, msg_mixed, vec, mw, wp, mo, gall, pick, mgrad, gcls, between)
    core_m = []

    def send_message(k):
        cols = pl.ds(1536 * k, 1536)
        core_m.append(remote(mgrad.at[1 - core, :, cols], mgot.at[:, cols], send_sem.at[12 + k, CORE],
                             recv_sem.at[12 + k, CORE], partners["c"]))

    def spread_message(k):
        core_m[k].wait_recv()
        cols = pl.ds(1536 * k, 1536)
        spread(12 + k, mgrad[core, :, cols] + mgot[:, cols])

    send_message(0)
    send_message(1)
    every(middle, range(6, 12), 3)
    send_last(LATE_A)
    send_last(LATE_B)
    for copy in near[7:]:
        copy.wait_recv()
    total = sall[0].astype(f32)
    for k in range(1, FRAMES):
        total = total + sall[k].astype(f32)
    message_vectors(total, vectors, pick, table, mgrad)
    send_message(2)
    spread_message(0)
    spread_message(1)
    finish(FEED_A)
    finish(FEED_S)
    spread_message(2)
    send_last(MESSAGE)
    top = lax.broadcasted_iota(jnp.int32, (16, 1), 0) == 0
    for clip in range(CLIPS_HERE):
        tokens[clip, 0, pl.ds(0, 16)] = (heads[clip] + jnp.where(top, gcls[clip : clip + 1], 0.0)).astype(low)
    for g in (LATE_A, LATE_B, MESSAGE):
        finish(g)
    for copy in core_m:
        copy.wait_send()
    for copy in near:
        copy.wait_send()
    for key in registry:
        registry[key]().wait_send()
    for g in range(len(GROUPS)):
        for p in range(1, 8):
            last_copy(g, p).wait_send()


def back_and_sums(d_expand, d_shrink, after, proj, probs, frames, first_low, mixed, wp, wo, mw, mp, mo, vec, message, sums,
                  saved):
    vmem = pl.BlockSpec(memory_space=pltpu.VMEM)
    any_spec = pl.BlockSpec(memory_space=pl.ANY)
    S, V, SEM = jax.ShapeDtypeStruct, pltpu.VMEM, pltpu.SemaphoreType.DMA

    def phase_one(count, rows, cols, own=True):
        leads = ([8] if own else []) + [8, 4, 2, 1]
        return [V((count, lead, rows, cols), low) for lead in leads]

    scratch = [
        V((D, 3 * D), low), V((D, D), low), V((D, D), low), V((D, D), low), V((ALL, D), f32), V((ALL, 3 * D), low),
        V((2, 12, ROWS, ROWS), low), V((CLIPS_HERE, 1, PATCH, D), low), V((ALL, D), low), V((ALL, D), low),
        V((ROWS, D), f32), V((ALL, D), low), V((CLIPS_HERE, 16, D), f32), V((SUMS, D), f32), V((SLOT, D), f32), V((SLOT, D), f32),
        V((2, 48, 6 * D), low), V((48, 6 * D), low), V((FRAMES, SLOT, D), f32), V((16, D), low), V((FRAMES, 16, D), low),
        V((2, 128, 48), low), V((2, 128, 48), low), V((3, 384, 384), low), V((672, 1), jnp.int32), V((8, 8, 24, 256), f32),
        *phase_one(3, 48, 1024), *phase_one(3, 192, 256), V((2, 8, 2, 48, 1536), low), *phase_one(6, 48, 512, own=False),
        *[V((lead, rows, 3 * cols), low) for lead in (8, 7) for _, rows, cols, _ in GROUPS],
        SEM((9,)), SEM((2,)), SEM((6,)), SEM((N_PARTS, 8)), SEM((N_PARTS, 8)), SEM((2, 7)), SEM((2, 7)), SEM((5, 7)), SEM((5, 7))]
    return pl.pallas_call(
        back_kernel,
        in_specs=[any_spec] * 13 + [vmem] * 9,
        out_specs=[vmem, vmem, vmem],
        out_shape=[S((CLIPS_HERE, 1, PATCH, D), low), S((N_PARTS, 16, D), f32), S((3, 32, 256), f32)],
        scratch_shapes=scratch,
        compiler_params=pltpu.CompilerParams(collective_id=2, has_side_effects=True, vmem_limit_bytes=62 * 2**20),
        name="back_and_sums",
    )(to_units(d_expand), d_shrink.reshape(8, 2, 192, D), after, proj, probs, frames, first_low, mixed, wp, wo, mw, mp, mo,
      vec, message, sums, *saved, index_table())


def unpack_kernel(out, out_s, mw, mp, mo, ap, ao, ew, sw, *vectors):
    def piece(n, side, w):
        return out[n, 8 * side : 8 * side + 6, 0:w]

    mw[...] = piece(12, 0, D)
    for k, (n, side) in enumerate(((12, 1), (13, 0), (13, 1))):
        mp[:, k * D : (k + 1) * D] = piece(n, side, D)
    mo[...] = piece(14, 0, D)
    for k in range(3):
        for side in range(2):
            ap[:, 512 * k + 256 * side : 512 * k + 256 * side + 256] = piece(6 + 2 * k, side, 256)
            ew[:, 1024 * k + 512 * side : 1024 * k + 512 * side + 512] = piece(2 * k, side, 512)
            x = 512 * k + 256 * side
            target, x = (ap, x + 1536) if x < D else (ao, x - D)
            target[:, x : x + 256] = piece(7 + 2 * k, side, 256)
        sw[:, 256 * k : 256 * (k + 1)] = out_s[k, 0:24]
    lanes = lax.broadcasted_iota(jnp.int32, (6, 128), 1)
    rows = lax.broadcasted_iota(jnp.int32, (6, 128), 0)
    values = out[14, 8:14, 0:128]
    flat = jnp.zeros((128, 128), f32)
    for shift in range(4):
        place_at = (lanes == rows + 6 * shift).astype(f32)
        owner = jnp.where((lanes < 24) | (lanes >= 32), 0, jnp.where(lanes < 28, lanes - 24, (lanes - 28) & 1))
        part = jnp.where(owner == shift, values, 0.0)
        flat += lax.dot_general(part, place_at, (((0,), (0,)), ((), ())), precision=PRECISE, preferred_element_type=f32)
    for ref, (row, count) in zip(vectors, LANES):
        ref[...] = jnp.sum(flat[row : row + count], axis=0)[0 : 6 * count]


LANES = ((12, 1), (13, 1), (14, 1), (30, 2), (17, 1), (0, 1), (1, 1), (28, 2), (4, 1), (5, 1), (6, 1), (24, 4), (11, 1))


def unpack(out, out_s):
    S = jax.ShapeDtypeStruct
    vmem = pl.BlockSpec(memory_space=pltpu.VMEM)
    shapes = [(6, D), (6, 3 * D), (6, D), (6, 3 * D), (6, D), (6, FF), (24, D)] + [(6 * count,) for _, count in LANES]
    return pl.pallas_call(
        unpack_kernel,
        in_specs=[vmem, vmem],
        out_specs=[vmem] * len(shapes),
        out_shape=[S(shape, f32) for shape in shapes],
        compiler_params=pltpu.CompilerParams(vmem_limit_bytes=BIG),
        name="unpack",
    )(out, out_s)


def forward_kernel(*refs):
    vectors, refs = refs[: len(VECTORS)], refs[len(VECTORS) :]
    (gids, frames_ref, mw_ref, mp_ref, mo_ref, wp_ref, wo_ref, we_ref, ws_ref,
     vec, message, all_cls, pre_out, normed_out, qkv, msg_mixed,
     first_ref, proj_ref, probs_ref, mixed_ref, resid_ref, second_ref, hidden_ref, dgate_ref,
     result, loss, pooled_out, gpool,
     vw, vp, vo, wp, wo, we, ws, frames, cls, tops, first_low, proj, probs, mixed, resid, second_low, xs,
     hid, dg, acc, pool_all, every, natural, grads,
     load_sem, store_sem, probs_sem, send_sem, recv_sem, near_send, near_recv) = refs
    at = place()
    fr = lax.axis_index("frame")

    def load(n, src, dst):
        copy = pltpu.make_async_copy(src, dst, load_sem.at[n])
        copy.start()
        return copy

    def store(n, src, dst):
        copy = pltpu.make_async_copy(src, dst, store_sem.at[n])
        copy.start()
        return copy

    get_frames = load(0, frames_ref, frames)
    get_wp = [load(1 + j, wp_ref.at[:, pl.ds(j * D, D)], wp.at[j]) for j in range(3)]
    get_mw, get_mp, get_mo = load(4, mw_ref, vw), load(5, mp_ref, vp), load(6, mo_ref, vo)
    vec[...] = jnp.zeros((24, D), f32)
    for ref, rows in zip(vectors, VECTORS):
        for k, row in enumerate(rows):
            vec[row : row + 1] = ref[pl.ds(k * D, D)].astype(f32).reshape(1, D)
    cls[...] = jnp.zeros((SLOT, D), f32)
    around = frame_partners()
    order = ("c",) + CLIP_DIMS
    partner = {d: device_of(moved(at, {d: 1})) for d in order}
    greet(around + [partner[d] for d in order])
    get_frames.wait()
    for c in range(CLIPS_HERE):
        cls[c : c + 1] = frames[c, 0, 0:16].astype(f32)[0:1]
    first_near = [remote(cls, all_cls.at[fr], near_send.at[0, k], near_recv.at[0, k], p) for k, p in enumerate(around)]
    all_cls[fr] = cls[...]

    gain, shift = vec[R_FG : R_FG + 1], vec[R_FS : R_FS + 1]
    xs[pl.ds(192, 16)] = jnp.zeros((16, D), f32)
    for c in range(CLIPS_HERE):
        xs[pl.ds(0, PATCH)] = frames[c, 0].astype(f32)
        u, _ = stats(xs[...])
        first_low[pl.ds(c * ROWS, ROWS)] = (u * gain + shift).astype(low)
    for j in range(3):
        get_wp[j].wait()
        for part in range(2):
            rows = pl.ds(part * 2 * ROWS, 2 * ROWS)
            value = dot(first_low[rows], wp[j]) + vec[R_APB + j : R_APB + j + 1]
            proj[rows, j * D : (j + 1) * D] = value.astype(low)
    get_wo = load(7, wo_ref, wo)
    get_we = [load(8 + j, we_ref.at[:, pl.ds(j * D, D)], we.at[j]) for j in range(4)]
    get_ws = [load(12 + j, ws_ref.at[pl.ds(j * D, D)], ws.at[j]) for j in range(4)]

    get_mw.wait()
    for copy in first_near:
        copy.wait_recv()
    x = all_cls[...].reshape(MROWS, D).astype(low)
    pre = dot(x, vw[...]) + vec[R_MB : R_MB + 1]
    pre_out[...] = pre
    u, _ = stats(pre)
    normed = (u * vec[R_MG : R_MG + 1] + vec[R_MS : R_MS + 1]).astype(low)
    normed_out[...] = normed
    get_mp.wait()
    for j in range(3):
        qkv[:, j * D : (j + 1) * D] = (dot(normed, vp[:, j * D : (j + 1) * D]) + vec[R_MPB + j : R_MPB + j + 1]).astype(low)
    keep = same_clip()
    lane = lax.broadcasted_iota(jnp.int32, (MROWS, 128), 1)
    zero = jnp.zeros((), low)
    for pair in range(6):
        q = qkv[:, pair * 128 : pair * 128 + 128]
        k = qkv[:, D + pair * 128 : D + pair * 128 + 128]
        v = qkv[:, 2 * D + pair * 128 : 2 * D + pair * 128 + 128]
        outs = []
        for half in range(2):
            mine = (lane < 64) if half == 0 else (lane >= 64)
            s = jnp.where(keep, dot_t(jnp.where(mine, q, zero), k) * 0.125, -1e30)
            outs.append(dot(soft(s).astype(low), v))
        msg_mixed[:, pair * 128 : pair * 128 + 128] = jnp.where(lane < 64, outs[0], outs[1]).astype(low)
    get_mo.wait()
    branch = pre + dot(msg_mixed[...], vo[...]) + vec[R_MOB : R_MOB + 1]
    rows = lax.broadcasted_iota(jnp.int32, (MROWS, 1), 0) // SLOT
    message[...] = jnp.sum(jnp.where(rows == fr, branch, 0.0).reshape(FRAMES, SLOT, D), axis=0)

    u, _ = stats(message[...])
    ends = (u * gain + shift).astype(low)
    spot = lax.broadcasted_iota(jnp.int32, (16, 1), 0) == PATCH - 192
    for c in range(CLIPS_HERE):
        window = pl.ds(c * ROWS + 192, 16)
        row = ends[c : c + 1].astype(f32)
        first_low[window] = jnp.where(spot, row, first_low[window].astype(f32)).astype(low)
    for j in range(3):
        row = dot(ends, wp[j]) + vec[R_APB + j : R_APB + j + 1]
        for c in range(CLIPS_HERE):
            window = pl.ds(c * ROWS + 192, 16)
            old = proj[window, j * D : (j + 1) * D].astype(f32)
            proj[window, j * D : (j + 1) * D] = jnp.where(spot, row[c : c + 1], old).astype(low)
    stores = [store(0, first_low, first_ref), store(1, proj, proj_ref)]

    lane = lax.broadcasted_iota(jnp.int32, (ROWS, 128), 1)
    seen = lax.broadcasted_iota(jnp.int32, (ROWS, ROWS), 1) < PATCH + 1

    def probs_out(clip):
        return pltpu.make_async_copy(probs.at[clip % 2], probs_ref.at[clip], probs_sem.at[clip % 2])

    def one_clip(clip, carry):
        @pl.when(clip >= 2)
        def _():
            probs_out(clip - 2).wait()

        rows = pl.ds(pl.multiple_of(clip * ROWS, 16), ROWS)
        for pair in range(6):
            q, k, v = (proj[rows, n * D + pair * 128 : n * D + pair * 128 + 128] for n in range(3))
            outs = []
            for half in range(2):
                mine = (lane < 64) if half == 0 else (lane >= 64)
                s = dot_t(jnp.where(mine, q, zero), k) * 0.125
                s = jnp.where(seen, s, -1e30)
                e = jnp.exp(s - jnp.max(s, axis=-1, keepdims=True))
                p = (e * (1.0 / jnp.sum(e, axis=-1, keepdims=True))).astype(low)
                probs[clip % 2, 2 * pair + half] = p
                outs.append(dot(p, v))
            mixed[rows, pair * 128 : pair * 128 + 128] = jnp.where(lane < 64, outs[0], outs[1]).astype(low)
        probs_out(clip).start()
        return carry

    lax.fori_loop(0, CLIPS_HERE, one_clip, 0)
    stores.append(store(2, mixed, mixed_ref))
    get_wo.wait()
    for part in range(2):
        branch = dot(mixed[pl.ds(part * 2 * ROWS, 2 * ROWS)], wo[...]) + vec[R_AOB : R_AOB + 1]
        for c in (2 * part, 2 * part + 1):
            xs[pl.ds(192, 16)] = jnp.zeros((16, D), f32)
            xs[pl.ds(0, PATCH)] = frames[c, 0].astype(f32)
            after = xs[...] + branch[(c - 2 * part) * ROWS : (c - 2 * part + 1) * ROWS]
            rows = pl.ds(c * ROWS, ROWS)
            resid[rows] = after
            u2, _ = stats(after)
            second_low[rows] = (u2 * vec[R_SG : R_SG + 1] + vec[R_SS : R_SS + 1]).astype(low)
    stores += [store(3, resid, resid_ref), store(4, second_low, second_ref)]

    def gate(h):
        sg = 1.0 / (1.0 + jnp.exp(-1.702 * h))
        hs = h * sg
        return sg, hs

    heads = jnp.concatenate([second_low[pl.ds(c * ROWS, 16)] for c in range(CLIPS_HERE)], axis=0)
    total = jnp.zeros((16 * CLIPS_HERE, D), f32)
    for j in range(4):
        get_we[j].wait()
        _, hs = gate(dot(heads, we[j]) + vec[R_EB + j : R_EB + j + 1])
        get_ws[j].wait()
        total += dot(hs.astype(low), ws[j])
    tops[...] = jnp.zeros((SLOT, D), f32)
    for c in range(CLIPS_HERE):
        tops[c : c + 1] = resid[c * ROWS : c * ROWS + 1] + vec[R_SB : R_SB + 1] + total[16 * c : 16 * c + 1]
    near = [remote(tops, pool_all.at[fr], near_send.at[1, k], near_recv.at[1, k], p) for k, p in enumerate(around)]
    pool_all[fr] = tops[...]

    copies, state = [], {}

    def exchange(k):
        copy = remote(every.at[pl.ds(0, 2**k)], every.at[pl.ds(2**k, 2**k)], send_sem.at[k], recv_sem.at[k],
                      partner[order[k]])
        copies.append(copy)

    def step(k):
        if k == 0:
            for copy in near:
                copy.wait_recv()
            s = pool_all[0]
            for f in range(1, FRAMES):
                s = s + pool_all[f]
            pooled = s * 0.125
            pooled_out[...] = pooled[:CLIPS_HERE]
            inv_len = lax.rsqrt(jnp.sum(pooled * pooled, axis=-1, keepdims=True) + 1e-06)
            state.update(pooled=pooled, inv_len=inv_len)
            every[0] = pooled * inv_len
        else:
            copies[k - 1].wait_recv()
        if k < 4:
            exchange(k)

    tile_stores = []
    for j in range(4):
        if j >= 2:
            for copy in tile_stores[2 * (j - 2) : 2 * (j - 1)]:
                copy.wait()
        for part in range(2):
            rows = pl.ds(part * 2 * ROWS, 2 * ROWS)
            h = dot(second_low[rows], we[j]) + vec[R_EB + j : R_EB + j + 1]
            sg, hs = gate(h)
            hidden = hs.astype(low)
            hid[j % 2, rows] = hidden
            dg[j % 2, rows] = (sg + 1.702 * hs * (1.0 - sg)).astype(low)
            out = dot(hidden, ws[j])
            acc[rows] = (resid[rows] + vec[R_SB : R_SB + 1] if j == 0 else acc[rows]) + out
            k = 2 * j + part - 2
            if 0 <= k <= 4:
                step(k)
        for n, (src, dst) in enumerate(((hid, hidden_ref), (dg, dgate_ref))):
            copy = pltpu.make_async_copy(src.at[j % 2], dst.at[:, pl.ds(j * D, D)], store_sem.at[5 + 4 * n + j])
            copy.start()
            tile_stores.append(copy)
    for c in range(CLIPS_HERE):
        result[c, 0] = acc[pl.ds(c * ROWS, PATCH)].astype(low)
    for p in range(16):
        to = moved(at, {d: (p >> k) & 1 for k, d in enumerate(order)})
        natural[dp_of(to)] = every[p]
    n = natural[...].reshape(128, D)
    sims = 50.0 * lax.dot_general(n, n, (((1,), (1,)), ((), ())), precision=PRECISE, preferred_element_type=f32)
    rows = lax.broadcasted_iota(jnp.int32, (128, 128), 0)
    cols = lax.broadcasted_iota(jnp.int32, (128, 128), 1)
    here = (cols & 7) < CLIPS_HERE
    other = here & (rows != cols)
    slot = lax.broadcasted_iota(jnp.int32, (128, 64), 0)
    clip = lax.broadcasted_iota(jnp.int32, (128, 64), 1)
    spot = (((slot >> 3) * CLIPS_HERE + (slot & 7)) == clip) & ((slot & 7) < CLIPS_HERE)
    wide = jnp.broadcast_to(gids[...].astype(f32), (128, 64))
    mine = jnp.where(spot, wide, 0.0)
    gid_col = jnp.sum(mine, axis=-1, keepdims=True)
    gid_row = lax.dot_general(wide, spot.astype(f32), (((1,), (1,)), ((), ())), precision=PRECISE, preferred_element_type=f32)
    same = other & (gid_col == gid_row)
    valid = (lax.broadcasted_iota(jnp.int32, (128, 1), 0) & 7) < CLIPS_HERE

    def log_soft(logits):
        top = jnp.max(logits, axis=-1, keepdims=True)
        e = jnp.exp(logits - top)
        total = jnp.sum(e, axis=-1, keepdims=True)
        return top + jnp.log(total), e / total

    all_log, all_p = log_soft(jnp.where(other, sims, -1e30))
    pos_log, pos_p = log_soft(jnp.where(same, sims, -1e30))
    terms = jnp.where(valid, all_log - pos_log, 0.0)
    loss[...] = jnp.sum(terms, axis=0, keepdims=True) * (1.0 / 64.0)
    gs = jnp.where(valid & here, all_p - pos_p, 0.0)
    grad_all = 50.0 * jnp.dot(gs + gs.T, n, precision=PRECISE, preferred_element_type=f32)
    grads[...] = grad_all.reshape(16, SLOT, D)
    g = grads[lax.axis_index("dp")]
    pooled, inv_len = state["pooled"], state["inv_len"]
    back = inv_len * g - inv_len * inv_len * inv_len * pooled * jnp.sum(pooled * g, axis=-1, keepdims=True)
    gpool[...] = back * 0.125
    for copy in tile_stores[4:] + stores:
        copy.wait()
    for clip in (CLIPS_HERE - 2, CLIPS_HERE - 1):
        probs_out(clip).wait()
    for copy in first_near + near + copies:
        copy.wait_send()


def forward(vectors, gids, frames, mw, mp, mo, wp, wo, we, ws):
    vmem = pl.BlockSpec(memory_space=pltpu.VMEM)
    any_spec = pl.BlockSpec(memory_space=pl.ANY)
    S, V, SEM = jax.ShapeDtypeStruct, pltpu.VMEM, pltpu.SemaphoreType.DMA
    return pl.pallas_call(
        forward_kernel,
        in_specs=[vmem] * (len(VECTORS) + 1) + [any_spec] * 8,
        out_specs=[vmem] * 7 + [any_spec] * 8 + [vmem] * 4,
        out_shape=[
            S((24, D), f32), S((SLOT, D), f32), S((FRAMES, SLOT, D), f32), S((MROWS, D), f32), S((MROWS, D), low),
            S((MROWS, 3 * D), low), S((MROWS, D), low),
            S((ALL, D), low), S((ALL, 3 * D), low), S((CLIPS_HERE, 12, ROWS, ROWS), low), S((ALL, D), low), S((ALL, D), f32),
            S((ALL, D), low), S((ALL, FF), low), S((ALL, FF), low),
            S((CLIPS_HERE, 1, PATCH, D), low), S((1, 1), f32), S((CLIPS_HERE, D), f32), S((SLOT, D), f32)],
        scratch_shapes=[
            V((D, D), low), V((D, 3 * D), low), V((D, D), low), V((3, D, D), low), V((D, D), low), V((4, D, D), low),
            V((4, D, D), low), V((CLIPS_HERE, 1, PATCH, D), low), V((SLOT, D), f32), V((SLOT, D), f32), V((ALL, D), low),
            V((ALL, 3 * D), low), V((2, 12, ROWS, ROWS), low), V((ALL, D), low), V((ALL, D), f32), V((ALL, D), low),
            V((ROWS, D), f32), V((2, ALL, D), low), V((2, ALL, D), low), V((ALL, D), f32), V((FRAMES, SLOT, D), f32),
            V((16, SLOT, D), f32), V((16, SLOT, D), f32), V((16, SLOT, D), f32),
            SEM((16,)), SEM((13,)), SEM((2,)), SEM((4,)), SEM((4,)), SEM((2, 7)), SEM((2, 7))],
        compiler_params=pltpu.CompilerParams(collective_id=0, has_side_effects=True, vmem_limit_bytes=62 * 2**20),
        name="forward",
    )(*vectors, gids, frames, mw, mp, mo, wp, wo, we, ws)


def on_device(
    frames, cotangent, group_ids, message_weight, message_bias, message_gain, message_shift, message_project,
    message_project_bias, message_output, message_output_bias, first_gain, first_shift, attend_project,
    attend_project_bias, attend_output, attend_output_bias, second_gain, second_shift, expand_weight, expand_bias,
    shrink_weight, shrink_bias,
):
    vectors = (
        message_bias, message_gain, message_shift, message_project_bias, message_output_bias, first_gain, first_shift,
        attend_project_bias, attend_output_bias, second_gain, second_shift, expand_bias, shrink_bias,
    )
    (vec, message, *saved, first_low, proj, probs, mixed, resid, second_low, hidden, dgate, result, loss, pooled,
     gpool) = forward(
        vectors, group_ids.reshape(1, 64), frames, message_weight, message_project, message_output, attend_project,
        attend_output, expand_weight, shrink_weight)
    d_shrink, d_expand, after, sums = mlp_back(
        cotangent, gpool, vec, hidden, dgate, second_low, expand_weight, shrink_weight, resid)
    delta_frames, out, out_s = back_and_sums(
        d_expand, d_shrink, after, proj, probs, frames, first_low, mixed, attend_project, attend_output, message_weight,
        message_project, message_output, vec, message, sums, saved)
    mw, mp, mo, ap, ao, ew, sw, mb, mg, ms, mpb, mob, fg, fs, apb, aob, sg, ss, eb, sb = unpack(out, out_s)
    return (
        result, loss.reshape(()), pooled, delta_frames, mw, mb, mg, ms, mp, mpb, mo, mob, fg, fs, ap, apb, ao, aob, sg, ss,
        ew, eb, sw, sb,
    )


def solution(mesh):
    placed = (
        P("dp", "frame", None, None),
        P("dp", "frame", None, None),
        P(),
        P(),
        P(),
        P(),
        P(),
        P(),
        P(),
        P(),
        P(),
        P(),
        P(),
        P(),
        P(),
        P(),
        P(),
        P(),
        P(),
        P(),
        P(),
        P(),
        P(),
    )
    return jax.shard_map(
        on_device,
        mesh=mesh,
        in_specs=placed,
        out_specs=(
            P("dp", "frame", None, None),
            P(),
            P("dp", None),
            P("dp", "frame", None, None),
            P(("dp", "frame"), None),
            P(("dp", "frame")),
            P(("dp", "frame")),
            P(("dp", "frame")),
            P(("dp", "frame"), None),
            P(("dp", "frame")),
            P(("dp", "frame"), None),
            P(("dp", "frame")),
            P(("dp", "frame")),
            P(("dp", "frame")),
            P(("dp", "frame"), None),
            P(("dp", "frame")),
            P(("dp", "frame"), None),
            P(("dp", "frame")),
            P(("dp", "frame")),
            P(("dp", "frame")),
            P(("dp", "frame"), None),
            P(("dp", "frame")),
            P(("dp", "frame"), None),
            P(("dp", "frame")),
        ),
        check_vma=False,
    )
```

```python
import functools

import jax
import jax.numpy as jnp
import numpy as np
from jax import lax
from jax.experimental import pallas as pl
from jax.experimental.pallas import tpu as pltpu
from jax.sharding import PartitionSpec as P

f32, low = jnp.float32, jnp.bfloat16
CLIPS_HERE, PATCH, ROWS, D, FF = 4, 197, 208, 768, 3072
ALL = CLIPS_HERE * ROWS
BIG = 58 * 2**20
(R_MB, R_MG, R_MS, R_MPB, R_MOB, R_FG, R_FS, R_APB, R_AOB, R_SG, R_SS, R_EB, R_SB) = (
    0, 1, 2, 3, 6, 7, 8, 9, 12, 13, 14, 15, 19)


def dot(a, b):
    return jnp.dot(a, b, preferred_element_type=f32)


def dot_t(a, b):
    return lax.dot_general(a, b, (((1,), (1,)), ((), ())), preferred_element_type=f32)


def dot_tl(a, b):
    return lax.dot_general(a, b, (((0,), (0,)), ((), ())), preferred_element_type=f32)


def stats(x):
    mean = jnp.mean(x, axis=-1, keepdims=True)
    centered = x - mean
    inv = lax.rsqrt(jnp.mean(centered * centered, axis=-1, keepdims=True) + 1e-05)
    return centered * inv, inv


def norm_back(grad, u, inv, gain):
    h = grad * gain
    return (h - jnp.mean(h, axis=-1, keepdims=True) - u * jnp.mean(h * u, axis=-1, keepdims=True)) * inv


def const(shape):
    return pl.BlockSpec(shape, lambda *i: (0,) * len(shape))


MESH = pl.DeviceIdType.MESH


def flip_low(index):
    return index + 1 - 2 * (index % 2)


def flip_pair(index, high, low):
    index = 3 - index if high else index
    return flip_low(index) if low else index


def place():
    dp, fr = lax.axis_index("dp"), lax.axis_index("frame")
    return dict(y=dp // 4, x=(dp // 2 % 2) * 2 + fr // 4, z=fr % 4, c=dp % 2)


def moved(at, bits):
    return dict(
        y=flip_pair(at["y"], bits.get("yu"), bits.get("yv")),
        x=flip_pair(at["x"], bits.get("xu"), bits.get("xv")),
        z=flip_pair(at["z"], bits.get("zu"), bits.get("zv")),
        c=1 - at["c"] if bits.get("c") else at["c"],
    )


def dp_of(at):
    return at["y"] * 4 + (at["x"] // 2) * 2 + at["c"]


def frame_of(at):
    return (at["x"] % 2) * 4 + at["z"]


def device_of(at):
    return (dp_of(at), frame_of(at))


CLIP_DIMS = ("yu", "yv", "xu")
FRAME_DIMS = ("xv", "zu", "zv")


def rotated(dims, turn):
    return dims[turn:] + dims[:turn]


def bits_at(dims, position):
    return {dims[k]: (position >> (2 - k)) & 1 for k in range(3)}


def to_units(full):
    return full.reshape(8, 2, 48, full.shape[-1])


FRAMES = 8
SLOT = 8
MROWS = FRAMES * SLOT
SUMS = 24


def greet(partners):
    barrier = pltpu.get_barrier_semaphore()
    for partner in partners:
        pl.semaphore_signal(barrier, inc=1, device_id=partner, device_id_type=MESH)
    pl.semaphore_wait(barrier, len(partners))


def frame_partners():
    dp, fr = lax.axis_index("dp"), lax.axis_index("frame")
    return [(dp, lax.rem(fr + k, FRAMES)) for k in range(1, FRAMES)]


def remote(src, dst, send_sem, recv_sem, device):
    copy = pltpu.make_async_remote_copy(
        src_ref=src, dst_ref=dst, send_sem=send_sem, recv_sem=recv_sem, device_id=device, device_id_type=MESH)
    copy.start()
    return copy


def same_clip():
    rows = lax.broadcasted_iota(jnp.int32, (MROWS, MROWS), 0)
    cols = lax.broadcasted_iota(jnp.int32, (MROWS, MROWS), 1)
    return rows % SLOT == cols % SLOT


def soft(s):
    e = jnp.exp(s - jnp.max(s, axis=-1, keepdims=True))
    return e / jnp.sum(e, axis=-1, keepdims=True)


VECTORS = ((R_MB,), (R_MG,), (R_MS,), (R_MPB, R_MPB + 2), (R_MOB,), (R_FG,), (R_FS,), (R_APB, R_APB + 2), (R_AOB,), (R_SG,),
           (R_SS,), (R_EB, R_EB + 1, R_EB + 2, R_EB + 3), (R_SB,))


PRECISE = lax.Precision.HIGHEST


def message_back(at, cls_all, pre, normed, qkv, mixed, vec, vw, vp, vo, gall, pick, mgrad, gcls, between):
    fr = lax.axis_index("frame")
    g = gall[...].reshape(MROWS, D)
    g_low = g.astype(low)
    gmm = dot_t(g_low, vo[...]).astype(low)
    keep = same_clip()
    lane = lax.broadcasted_iota(jnp.int32, (MROWS, 128), 1)
    zero = jnp.zeros((), low)
    parts = ([], [], [])
    for pair in range(6):
        q = qkv[:, pair * 128 : pair * 128 + 128]
        k = qkv[:, D + pair * 128 : D + pair * 128 + 128]
        v = qkv[:, 2 * D + pair * 128 : 2 * D + pair * 128 + 128]
        gm = gmm[:, pair * 128 : pair * 128 + 128]
        totals = [0.0, 0.0, 0.0]
        for half in range(2):
            mine = (lane < 64) if half == 0 else (lane >= 64)
            q_here, k_here, gm_here = (jnp.where(mine, value, zero) for value in (q, k, gm))
            s = jnp.where(keep, dot_t(k_here, q) * 0.125, -1e30)
            e = jnp.exp(s - jnp.max(s, axis=0, keepdims=True))
            p = e / jnp.sum(e, axis=0, keepdims=True)
            dp = dot_t(v, gm_here)
            gs = (p * (dp - jnp.sum(dp * p, axis=0, keepdims=True))).astype(low)
            products = (dot_tl(gs, k_here), dot(gs, q_here), dot(p.astype(low), gm_here))
            totals = [total + product for total, product in zip(totals, products)]
        for n, scale in ((0, 0.125), (1, 0.125), (2, 1.0)):
            parts[n].append((totals[n] * scale).astype(low))
    gq, gk, gv = (jnp.concatenate(part, axis=1) for part in parts)
    between()
    gnorm = dot_t(gq, vp[:, :D]) + dot_t(gk, vp[:, D : 2 * D]) + dot_t(gv, vp[:, 2 * D :])
    u, inv = stats(pre[...])
    gpre = (g + norm_back(gnorm, u, inv, vec[R_MG : R_MG + 1])).astype(low)

    def total(value):
        return jnp.sum(value.astype(f32), axis=0, keepdims=True)

    mine = (lax.broadcasted_iota(jnp.int32, (96, D), 1) == pick[0:96]).astype(low)
    x = cls_all[...].reshape(MROWS, D).astype(low)
    for unit, (left, right) in enumerate(((x, gpre), (normed[...], gq), (normed[...], gk), (normed[...], gv),
                                          (mixed[...], g_low))):
        turned = dot_t(mine, left).astype(low)
        mgrad[:, :, unit * D : (unit + 1) * D] = dot(turned, right).astype(low).reshape(2, 48, D)
    back = dot_t(gpre, vw[...])
    rows = lax.broadcasted_iota(jnp.int32, (MROWS, 1), 0) // SLOT
    gcls[...] = jnp.sum(jnp.where(rows == fr, back, 0.0).reshape(FRAMES, SLOT, D), axis=0)
    return [total(gpre), total(gnorm * u), total(gnorm), total(gq), total(gv), total(g_low)]


def message_vectors(sums, message_sums, pick, part, mgrad):
    table = jnp.concatenate([sums[0:12], *message_sums, jnp.zeros((SUMS - 18, D), f32)], axis=0).astype(low)
    choose = (lax.broadcasted_iota(jnp.int32, (672, D), 1) == pick[...]).astype(low)
    z = dot_t(choose, table)
    wide = lax.broadcasted_iota(jnp.int32, (96, 128), 1)
    narrow = lax.broadcasted_iota(jnp.int32, (96, SUMS), 1)
    out = jnp.zeros((96, 128), f32)
    out += jnp.concatenate([z[:96], jnp.zeros((96, 128 - SUMS), f32)], axis=1)
    for q in range(4):
        hit = narrow == 7 + part[384:480, 3:4]
        value = jnp.sum(jnp.where(hit, z[96 * (1 + q) : 96 * (2 + q)], 0.0), axis=-1, keepdims=True)
        out = jnp.where(wide == 24 + q, value, out)
    for q in range(2):
        for n, first in enumerate((2, 15)):
            hit = narrow == first + part[384:480, 4:5]
            value = jnp.sum(jnp.where(hit, z[96 * (5 + q) : 96 * (6 + q)], 0.0), axis=-1, keepdims=True)
            out = jnp.where(wide == 28 + 2 * n + q, value, out)
    mgrad[:, :, 5 * D : 5 * D + 128] = out.astype(low).reshape(2, 48, 128)


def index_table():
    table = np.zeros((384 + 672, 8), np.int32)
    r = np.arange(384)
    table[:384, 0] = r // 48
    table[:384, 1] = r % 48 // 6 * 48 + r % 6
    table[:384, 2] = r % 48 // 6 % 2
    r = np.arange(96)
    c, y, xh, i = r // 48, r % 48 // 12, r % 12 // 6, r % 6
    high = y * 4 + xh * 2 + c
    picks = [(high * 48 + i, 6)]
    picks += [(high % 4 * 192 + q * 6 + i, 24) for q in range(4)]
    picks += [(high % 8 * 96 + q * 6 + i, 12) for q in range(2)]
    for n, (base, step) in enumerate(picks):
        rows = slice(384 + 96 * n, 384 + 96 * (n + 1))
        table[rows, 0], table[rows, 1], table[rows, 2] = base, step, xh
        table[rows, 3], table[rows, 4] = y, y // 2
    return jnp.asarray(table)


def fill_orders(at, table, sa, sb, mix, pick):
    xh, xl = at["x"] // 2, at["x"] % 2
    rows = lax.broadcasted_iota(jnp.int32, (128, 48), 0)
    cols = lax.broadcasted_iota(jnp.int32, (128, 48), 1)
    for ref, dims in ((sa, FRAME_DIMS), (sb, CLIP_DIMS)):
        block = jnp.zeros((128, 48), jnp.int32)
        for p in range(8):
            to = moved(at, bits_at(dims, p))
            value = frame_of(to) if dims == FRAME_DIMS else dp_of(to) // 2
            block = jnp.where((rows >> 4) == p, value, block)
        for half in range(2):
            inner = (rows & 15) - 8 * half
            hit = (cols == block * 6 + inner) & (inner >= 0) & (inner < 6)
            ref[half] = hit.astype(f32).astype(low)
    lanes = lax.broadcasted_iota(jnp.int32, (384, 384), 1)
    p_col, base, same = table[0:384, 0:1], table[0:384, 1:2], table[0:384, 2:3] == xh
    for turn in range(3):
        frame = jnp.zeros((384, 1), jnp.int32)
        for p in range(8):
            to = moved(at, bits_at(rotated(FRAME_DIMS, turn), p))
            side = to["x"] % 2
            frame = jnp.where(p_col == p, jnp.where(same, 4 * side + to["z"], 4 * (1 - side) + to["z"]), frame)
        mix[turn] = (lanes == base + 6 * frame).astype(f32).astype(low)
    base, step, same = table[384:, 0:1], table[384:, 1:2], table[384:, 2:3] == xh
    pick[...] = base + step * jnp.where(same, 4 * xl + at["z"], 4 * (1 - xl) + at["z"])


CORE, S1, S2, S3 = 0, 1, 5, 7
KEEP = (4, 2, 1)
KIND = ("a", "s") * 3 + ("a", "b") * 3 + ("m",) * 2
TURN = (0, 0, 1, 1, 2, 2) * 2
N_PARTS = 14


GROUPS = (
    ((0, 2, 4), 16, 512, FRAME_DIMS), ((1, 3, 5), 32, 256, CLIP_DIMS), ((6, 8, 10), 16, 256, FRAME_DIMS),
    ((7, 9, 11), 16, 256, CLIP_DIMS), ((12,), 16, 1920, CLIP_DIMS), ((13,), 16, 128, CLIP_DIMS),
)
FEED_A, FEED_S, LATE_A, LATE_B, MESSAGE, VECTOR = range(6)


def order_of(n):
    return rotated(CLIP_DIMS if KIND[n] == "a" else FRAME_DIMS, TURN[n])


def mlp_back_kernel(cot, gpool, vec, hidden, dgate, second_low, we, ws, resid,
                    out_e, out_s, after, sums, gl, gb, gsec, tile_e, tile_s, got_e, got_s, put_e, put_s, wide,
                    send_sem, recv_sem, store_sem):
    j = pl.program_id(0)
    at = place()
    core = at["c"]
    other = device_of(moved(at, {"c": 1}))

    def pair_copies(n):
        return [pltpu.make_async_remote_copy(
            src_ref=tile.at[n % 2, :, 1 - core], dst_ref=got.at[n], send_sem=send_sem.at[k, n], recv_sem=recv_sem.at[k, n],
            device_id=other, device_id_type=MESH) for k, (tile, got) in enumerate(((tile_e, got_e), (tile_s, got_s)))]

    def puts(n):
        return [pltpu.make_async_copy(put_e.at[n % 2], out_e.at[:, :, pl.ds(n * D, D)], store_sem.at[0, n]),
                pltpu.make_async_copy(put_s.at[n % 2], out_s.at[:, pl.ds(48 * n, 48)], store_sem.at[1, n])]

    def fold(n):
        if n >= 2:
            for copy in puts(n - 2):
                copy.wait()
        for copy in pair_copies(n):
            copy.wait_recv()
        for k in range(3):
            first, stop = max(1024 * k, D * n) - D * n, min(1024 * (k + 1), D * (n + 1)) - D * n
            if first < stop:
                for p in range(8):
                    chunk = dp_of(moved(at, bits_at(order_of(2 * k), p))) // 2
                    put_e[n % 2, p, :, first:stop] = (
                        tile_e[n % 2, chunk, core, :, first:stop] + got_e[n, chunk, :, first:stop])
        for xh in range(2):
            wide[xh] = (tile_s[n % 2, xh, core] + got_s[n, xh]).astype(f32).reshape(8, 24, D)
        for k in range(3):
            cols = pl.ds(256 * k, 256)
            for p in range(8):
                to = moved(at, bits_at(order_of(2 * k + 1), p))
                rows = []
                for xh in range(2):
                    side = lax.rem(to["x"] % 2 + at["x"] // 2 + xh, 2)
                    rows.append(wide[xh, side * 4 + to["z"], :, cols])
                put_s[n % 2, p, :, cols] = jnp.concatenate(rows, axis=0).astype(low)
        for copy in puts(n):
            copy.start()

    @pl.when(j == 0)
    def _():
        greet([other])
        gl[...] = jnp.zeros((ALL, D), f32)
        for c in range(CLIPS_HERE):
            gl[pl.ds(c * ROWS, PATCH)] = cot[c, 0].astype(f32)
            gl[pl.ds(c * ROWS, 1)] += gpool[pl.ds(c, 1)]
        gb[...] = gl[...].astype(low)
        gsec[...] = jnp.zeros((ALL, D), f32)
        sums[...] = jnp.zeros((24, D), f32)
        sums[11:12] = jnp.sum(gb[...].astype(f32), axis=0, keepdims=True)

    for n in (2, 3):
        @pl.when(j == n)
        def _(n=n):
            for copy in pair_copies(n - 2):
                copy.wait_send()

    tile_s[j % 2] = dot_tl(hidden[...], gb[...]).astype(low).reshape(2, 2, 192, D)
    ghp = (dot_t(gb[...], ws[...]) * dgate[...].astype(f32)).astype(low)
    sums[pl.ds(7 + j, 1)] = jnp.sum(ghp.astype(f32), axis=0, keepdims=True)
    tile_e[j % 2] = dot_tl(second_low[...], ghp).astype(low).reshape(8, 2, 48, D)
    for n in range(4):
        @pl.when(j == n)
        def _(n=n):
            for copy in pair_copies(n):
                copy.start()

    gsec[...] += dot_t(ghp, we[...])
    for n in range(3):
        @pl.when(j == n + 1)
        def _(n=n):
            fold(n)

    @pl.when(j == 3)
    def _():
        gain = vec[R_SG : R_SG + 1]
        total = [jnp.zeros((1, D), f32) for _ in range(3)]
        for c in range(CLIPS_HERE):
            rows = pl.ds(c * ROWS, ROWS)
            u, inv = stats(resid[rows])
            g = gsec[rows]
            out = gl[rows] + norm_back(g, u, inv, gain)
            after[rows] = out
            total[0] += jnp.sum(g * u, axis=0, keepdims=True)
            total[1] += jnp.sum(g, axis=0, keepdims=True)
            total[2] += jnp.sum(out.astype(low).astype(f32), axis=0, keepdims=True)
        sums[5:6] = total[0]
        sums[6:7] = total[1]
        sums[4:5] = total[2]
        fold(3)
        for n in (2, 3):
            for copy in pair_copies(n):
                copy.wait_send()
            for copy in puts(n):
                copy.wait()


def mlp_back(cot, gpool, vec, hidden, dgate, second_low, we, ws, resid):
    tile = pl.BlockSpec((ALL, D), lambda j: (0, j))
    any_spec = pl.BlockSpec(memory_space=pl.ANY)
    S, V, SEM = jax.ShapeDtypeStruct, pltpu.VMEM, pltpu.SemaphoreType.DMA
    return pl.pallas_call(
        mlp_back_kernel,
        grid=(4,),
        in_specs=[const((CLIPS_HERE, 1, PATCH, D)), const((8, D)), const((24, D)), tile, tile, const((ALL, D)),
                  pl.BlockSpec((D, D), lambda j: (0, j)), pl.BlockSpec((D, D), lambda j: (j, 0)), const((ALL, D))],
        out_specs=[any_spec, any_spec, const((ALL, D)), const((24, D))],
        out_shape=[S((8, 48, FF), low), S((8, 192, D), low), S((ALL, D), f32), S((24, D), f32)],
        scratch_shapes=[V((ALL, D), f32), V((ALL, D), low), V((ALL, D), f32), V((2, 8, 2, 48, D), low),
                        V((2, 2, 2, 192, D), low), V((4, 8, 48, D), low), V((4, 2, 192, D), low), V((2, 8, 48, D), low),
                        V((2, 8, 48, D), low), V((2, 8, 24, D), f32), SEM((2, 4)), SEM((2, 4)), SEM((2, 4))],
        compiler_params=pltpu.CompilerParams(collective_id=1, has_side_effects=True, vmem_limit_bytes=BIG),
        name="mlp_back",
    )(cot, gpool, vec, hidden, dgate, second_low, we, ws, resid)


def back_kernel(
    e_ref, s_ref, after_ref, proj_ref, probs_ref, frames_ref, first_ref, mixed_ref, wp_ref, wo_ref, mw_ref, mp_ref, mo_ref,
    vec, message, sums_in, cls_all, pre, normed, qkv, msg_mixed, table,
    tokens, out, out_s, out_m,
    wp, wo, mw, mo, after, proj, probs, frames, first_low, mixed, xs, gm_all, heads, sums, gmsg, gcls, mgrad, mgot,
    gall, sums_low, sall, sa, sb, mix, pick, wide_s,
    own_a, ra1, ra2, ra3, own_s, rs1, rs2, rs3, late, got_l, rl1, rl2, rl3,
    t0, t1, t2, t3, t4, t5, v0, v1, v2, v3, v4, v5,
    load_sem, probs_sem, local_sem, send_sem, recv_sem, near_send, near_recv, last_send, last_recv,
):
    at = place()
    fr = lax.axis_index("frame")
    core = at["c"]
    around = frame_partners()
    partners = {d: device_of(moved(at, {d: 1})) for d in ("c",) + CLIP_DIMS + FRAME_DIMS}

    def load(n, src, dst):
        copy = pltpu.make_async_copy(src, dst, load_sem.at[n])
        copy.start()
        return copy

    def probs_copy(clip):
        return pltpu.make_async_copy(probs_ref.at[clip], probs.at[clip % 2], probs_sem.at[clip % 2])

    probs_copy(0).start()
    get_wo, get_after, get_proj = load(0, wo_ref, wo), load(1, after_ref, after), load(2, proj_ref, proj)
    clip_cube = [device_of(moved(at, bits_at(CLIP_DIMS, p))) for p in range(1, 8)]
    greet(around + clip_cube + [partners["c"]])

    def mine(n, lead):
        if n < 6:
            return (own_a if n % 2 == 0 else own_s).at[n // 2, lead]
        return late.at[n % 2, lead, core, :, pl.ds((n - 6) // 2 * 512, 512)]

    def got(n):
        return got_l.at[n - 6]

    def half(n, s):
        if n < 6:
            return ((ra1, ra2, ra3) if n % 2 == 0 else (rs1, rs2, rs3))[s - 1].at[n // 2]
        return (rl1, rl2, rl3)[s - 1].at[n - 6]

    kept_blocks, sent_blocks = (t0, t1, t2, t3, t4, t5), (v0, v1, v2, v3, v4, v5)

    def group_of(n):
        return next((g, group[0].index(n), group) for g, group in enumerate(GROUPS) if n in group[0])

    def chunk_at(n, p):
        return dp_of(moved(at, bits_at(order_of(n), p))) // 2

    def source(n, which):
        if n < 6:
            step = 1024 if n % 2 == 0 else 256
            return (e_ref if n % 2 == 0 else s_ref).at[pl.ds(4 * which, 4), :, pl.ds(n // 2 * step, step)]
        return late.at[n % 2, :, which, :, pl.ds((n - 6) // 2 * 512, 512)]

    def local(n):
        return pltpu.make_async_copy(source(n, 0), mine(n, pl.ds(0, 4)), local_sem.at[n])

    def by_chunk(n):
        return KIND[n] == "a" and n >= 6

    registry = {}

    def define(n, step, src, dst, dim):
        def make():
            return pltpu.make_async_remote_copy(
                src_ref=src(), dst_ref=dst(), send_sem=send_sem.at[n, step], recv_sem=recv_sem.at[n, step],
                device_id=partners[dim], device_id_type=MESH)
        registry[n, step] = make

    def define_part(n):
        if KIND[n] == "m":
            return
        if n >= 6:
            define(n, CORE, lambda: source(n, 1 - core), lambda: got(n), "c")
        for s, first in ((1, S1), (2, S2), (3, S3)):
            keep, dim = KEEP[s - 1], order_of(n)[s - 1]
            if by_chunk(n):
                for p in range(keep):
                    define(n, first + p, lambda p=p, keep=keep: mine(n, chunk_at(n, keep + p)),
                           lambda p=p, s=s: half(n, s).at[p], dim)
            elif s == 1 and n < 6:
                define(n, first, lambda: source(n, 1), lambda: half(n, 1), dim)
            else:
                define(n, first, lambda keep=keep: mine(n, pl.ds(keep, keep)), lambda s=s: half(n, s), dim)

    def last_copy(g, p):
        return pltpu.make_async_remote_copy(
            src_ref=kept_blocks[g].at[p], dst_ref=sent_blocks[g].at[p - 1], send_sem=last_send.at[g, p - 1],
            recv_sem=last_recv.at[g, p - 1], device_id=device_of(moved(at, bits_at(GROUPS[g][3], p))),
            device_id_type=MESH)

    for n in range(N_PARTS):
        define_part(n)

    def start(n, step):
        registry[n, step]().start()

    def arrived(n, step):
        registry[n, step]().wait_recv()

    for n in range(6):
        start(n, S1)
    fill_orders(at, table, sa, sb, mix, pick)
    sums[...] = sums_in[...]
    gmsg[...] = jnp.zeros((SLOT, D), f32)

    def steps_of(n, s):
        first = (S1, S2, S3)[s - 1]
        return range(first, first + KEEP[s - 1]) if by_chunk(n) else (first,)

    def begin(n):
        arrived(n, CORE)
        if KIND[n] == "a":
            for chunk in range(8):
                ref = mine(n, chunk)
                ref[...] = ref[...] + got(n)[chunk]
        else:
            ref = mine(n, pl.ds(0, 8))
            full = (ref[...] + got(n)[...]).reshape(384, 512)
            ref[...] = dot(mix[TURN[n]], full).astype(low).reshape(8, 48, 512)
        for step in steps_of(n, 1):
            start(n, step)

    def spread(n, last):
        g, k, (_, _, w, dims) = group_of(n)
        blocks, cols = kept_blocks[g], pl.ds(k * w, w)
        if KIND[n] == "s":
            wide_s[...] = last.astype(f32).reshape(8, 24, 256)
            for p in range(8):
                chunk = dp_of(moved(at, bits_at(dims, p))) // 2
                rows = jnp.concatenate([wide_s[chunk], jnp.zeros((8, 256), f32)], axis=0)
                blocks[p, :, cols] = rows.astype(low)
        else:
            orders = sa if dims == FRAME_DIMS else sb
            wide = dot(orders[0], last[:, :w])
            if KIND[n] != "m" or n == 12:
                wide += dot(orders[1], last[:, w:])
            blocks[:, :, cols] = wide.astype(low).reshape(8, 16, w)

    def send_last(g):
        for p in range(1, 8):
            last_copy(g, p).start()

    def finish(g):
        parts, _, w, _ = GROUPS[g]
        total = kept_blocks[g][0].astype(f32)
        for p in range(1, 8):
            last_copy(g, p).wait_recv()
            total = total + sent_blocks[g][p - 1].astype(f32)
        for k, n in enumerate(parts):
            if KIND[n] == "s":
                out_s[k] = total[:, k * w : (k + 1) * w]
            else:
                (out_m if n == 12 else out.at[n - n // 13])[:, 0:w] = total[:, k * w : (k + 1) * w]

    def middle(n, s):
        keep = KEEP[s - 1]
        if s == 1 and n < 6:
            local(n).wait()
        for step in steps_of(n, s):
            arrived(n, step)
        if s == 3:
            lead = chunk_at(n, 0) if by_chunk(n) else 0
            spread(n, mine(n, lead)[...] + half(n, 3)[0])
            return
        if by_chunk(n):
            for p in range(keep):
                kept = mine(n, chunk_at(n, p))
                kept[...] = kept[...] + half(n, s)[p]
        else:
            kept = mine(n, pl.ds(0, keep))
            kept[...] = kept[...] + half(n, s)[...]
        for step in steps_of(n, s + 1):
            start(n, step)

    def every(action, parts, *args):
        for n in parts:
            action(n, *args)

    lane = lax.broadcasted_iota(jnp.int32, (ROWS, 128), 1)
    zero = jnp.zeros((), low)
    get_wo.wait()
    get_after.wait()
    gm_all[...] = dot_t(after[...].astype(low), wo[...]).astype(low)
    get_proj.wait()
    for n in range(6):
        local(n).start()
    get_wp, get_first, get_mixed = load(4, wp_ref, wp), load(5, first_ref, first_low), load(6, mixed_ref, mixed)
    get_frames, get_mw, get_mo = load(3, frames_ref, frames), load(7, mw_ref, mw), load(8, mo_ref, mo)

    def one_clip(clip, carry):
        @pl.when(clip < CLIPS_HERE - 1)
        def _():
            probs_copy(clip + 1).start()

        rows = pl.ds(pl.multiple_of(clip * ROWS, 16), ROWS)
        probs_copy(clip).wait()
        for pair in range(6):
            cols = [pl.ds(n * D + pair * 128, 128) for n in range(3)]
            q, k, v = (proj[rows, c] for c in cols)
            gm = gm_all[rows, pair * 128 : pair * 128 + 128]
            totals = [0.0, 0.0, 0.0]
            for side in range(2):
                here = (lane < 64) if side == 0 else (lane >= 64)
                q_here, k_here, gm_here = (jnp.where(here, value, zero) for value in (q, k, gm))
                dp = dot_t(v, gm_here)
                p_low = probs[clip % 2, 2 * pair + side]
                p = p_low.astype(f32)
                gs = (p * (dp - jnp.sum(dp * p, axis=0, keepdims=True))).astype(low)
                parts = (dot_tl(gs, k_here), dot(gs, q_here), dot(p_low, gm_here))
                totals = [total + part for total, part in zip(totals, parts)]
            for n, scale in ((0, 0.125), (1, 0.125), (2, 1.0)):
                proj[rows, cols[n]] = (totals[n] * scale).astype(low)

        @pl.when(clip == 2)
        def _():
            every(middle, range(6), 1)

        return carry

    lax.fori_loop(0, CLIPS_HERE, one_clip, 0)

    get_wp.wait()
    ends = jnp.concatenate([proj[pl.ds(c * ROWS + 192, 16)] for c in range(CLIPS_HERE)], axis=0)
    grad = jnp.zeros((16 * CLIPS_HERE, D), f32)
    for n in range(3):
        grad += dot_t(ends[:, n * D : (n + 1) * D], wp[:, n * D : (n + 1) * D])
    for c in range(CLIPS_HERE):
        gmsg[c : c + 1] = grad[16 * c + 5 : 16 * c + 6]
    u, inv = stats(message[...])
    gmsg[...] = norm_back(gmsg[...], u, inv, vec[R_FG : R_FG + 1])
    near = []
    for k, partner in enumerate(around):
        near.append(remote(gmsg, gall.at[fr], near_send.at[0, k], near_recv.at[0, k], partner))
    gall[fr] = gmsg[...]
    get_first.wait()
    get_mixed.wait()

    def late_grad(side, first, stop, left, right):
        grad = dot_tl(left[...], right)
        late[side, :, :, :, pl.ds(first, stop - first)] = grad.astype(low).reshape(8, 2, 48, stop - first)

    late_grad(0, 0, 512, first_low, proj[:, 0:512])
    start(6, CORE)
    late_grad(0, 512, 1024, first_low, proj[:, 512:1024])
    start(8, CORE)
    late_grad(0, 1024, 1536, first_low, proj[:, 1024:1536])
    start(10, CORE)
    begin(6)
    late_grad(1, 0, 768, first_low, proj[:, 1536:2304])
    start(7, CORE)
    begin(8)
    late_grad(1, 768, 1536, mixed, after[...].astype(low))
    start(9, CORE)
    start(11, CORE)
    begin(10)
    every(middle, range(6), 2)
    begin(7)
    begin(9)
    begin(11)
    every(middle, range(6), 3)
    send_last(FEED_A)
    send_last(FEED_S)
    for n in (0, 2):
        total = jnp.zeros((1, D), f32)
        for c in range(CLIPS_HERE):
            total += jnp.sum(proj[pl.ds(c * ROWS, ROWS), n * D : (n + 1) * D].astype(f32), axis=0, keepdims=True)
        to = 2 if n == 0 else 3
        sums[to : to + 1] = total
    get_frames.wait()

    def token_grads(first):
        two = pl.ds(first * ROWS, 2 * ROWS)
        grad_two = jnp.zeros((2 * ROWS, D), f32)
        for n in range(3):
            grad_two += dot_t(proj[two, n * D : (n + 1) * D], wp[:, n * D : (n + 1) * D])
        for clip in (first, first + 1):
            grad = grad_two[(clip - first) * ROWS : (clip - first + 1) * ROWS]
            xs[pl.ds(192, 16)] = jnp.zeros((16, D), f32)
            xs[pl.ds(0, PATCH)] = frames[clip, 0].astype(f32)
            xs[pl.ds(PATCH, 1)] = message[clip : clip + 1]
            u, inv = stats(xs[...])
            sums[0:1] += jnp.sum(grad * u, axis=0, keepdims=True)
            sums[1:2] += jnp.sum(grad, axis=0, keepdims=True)
            xs[...] = after[pl.ds(clip * ROWS, ROWS)] + norm_back(grad, u, inv, vec[R_FG : R_FG + 1])
            tokens[clip, 0] = xs[pl.ds(0, PATCH)].astype(low)
            heads[clip] = xs[pl.ds(0, 16)]

    sums[0:2] = jnp.zeros((2, D), f32)
    token_grads(0)
    token_grads(2)
    get_mp = load(4, mp_ref, wp)
    sums_low[...] = sums[0:16].astype(low)
    for k, partner in enumerate(around):
        near.append(remote(sums_low, sall.at[fr], near_send.at[1, k], near_recv.at[1, k], partner))
    sall[fr] = sums_low[...]
    every(middle, range(6, 12), 1)
    for copy in near[:7]:
        copy.wait_recv()
    get_mw.wait()
    get_mo.wait()
    get_mp.wait()
    def between():
        every(middle, range(6, 12), 2)

    vectors = message_back(
        at, cls_all, pre, normed, qkv, msg_mixed, vec, mw, wp, mo, gall, pick, mgrad, gcls, between)
    core_m = []

    def send_message(k):
        cols = pl.ds(3840 * k, 3840 - 3712 * k)
        core_m.append(remote(mgrad.at[1 - core, :, cols], mgot.at[:, cols], send_sem.at[12 + k, CORE],
                             recv_sem.at[12 + k, CORE], partners["c"]))

    def spread_message(k):
        core_m[k].wait_recv()
        cols = pl.ds(3840 * k, 3840 - 3712 * k)
        spread(12 + k, mgrad[core, :, cols] + mgot[:, cols])
        send_last(MESSAGE + k)

    send_message(0)
    every(middle, range(6, 12), 3)
    send_last(LATE_A)
    send_last(LATE_B)
    spread_message(0)
    for copy in near[7:]:
        copy.wait_recv()
    total = sall[0].astype(f32)
    for k in range(1, FRAMES):
        total = total + sall[k].astype(f32)
    message_vectors(total, vectors, pick, table, mgrad)
    send_message(1)
    finish(FEED_A)
    finish(FEED_S)
    spread_message(1)
    top = lax.broadcasted_iota(jnp.int32, (16, 1), 0) == 0
    for clip in range(CLIPS_HERE):
        tokens[clip, 0, pl.ds(0, 16)] = (heads[clip] + jnp.where(top, gcls[clip : clip + 1], 0.0)).astype(low)
    for g in (LATE_A, LATE_B, MESSAGE, VECTOR):
        finish(g)
    for copy in core_m:
        copy.wait_send()
    for copy in near:
        copy.wait_send()
    for key in registry:
        registry[key]().wait_send()
    for g in range(len(GROUPS)):
        for p in range(1, 8):
            last_copy(g, p).wait_send()


def back_and_sums(d_expand, d_shrink, after, proj, probs, frames, first_low, mixed, wp, wo, mw, mp, mo, vec, message, sums,
                  saved):
    vmem = pl.BlockSpec(memory_space=pltpu.VMEM)
    any_spec = pl.BlockSpec(memory_space=pl.ANY)
    S, V, SEM = jax.ShapeDtypeStruct, pltpu.VMEM, pltpu.SemaphoreType.DMA

    def phase_one(count, rows, cols, own=True):
        leads = [4 if own else 8, 4, 2, 1]
        return [V((count, lead, rows, cols), low) for lead in leads]

    scratch = [
        V((D, 3 * D), low), V((D, D), low), V((D, D), low), V((D, D), low), V((ALL, D), f32), V((ALL, 3 * D), low),
        V((2, 12, ROWS, ROWS), low), V((CLIPS_HERE, 1, PATCH, D), low), V((ALL, D), low), V((ALL, D), low),
        V((ROWS, D), f32), V((ALL, D), low), V((CLIPS_HERE, 16, D), f32), V((SUMS, D), f32), V((SLOT, D), f32), V((SLOT, D), f32),
        V((2, 48, 5 * D + 128), low), V((48, 5 * D + 128), low), V((FRAMES, SLOT, D), f32), V((16, D), low), V((FRAMES, 16, D), low),
        V((2, 128, 48), low), V((2, 128, 48), low), V((3, 384, 384), low), V((672, 1), jnp.int32), V((8, 24, 256), f32),
        *phase_one(3, 48, 1024), *phase_one(3, 192, 256), V((2, 8, 2, 48, 1536), low), *phase_one(6, 48, 512, own=False),
        *[V((lead, rows, len(parts) * cols), low) for lead in (8, 7) for parts, rows, cols, _ in GROUPS],
        SEM((9,)), SEM((2,)), SEM((6,)), SEM((N_PARTS, 8)), SEM((N_PARTS, 8)), SEM((2, 7)), SEM((2, 7)), SEM((6, 7)), SEM((6, 7))]
    return pl.pallas_call(
        back_kernel,
        in_specs=[any_spec] * 13 + [vmem] * 9,
        out_specs=[vmem] * 4,
        out_shape=[S((CLIPS_HERE, 1, PATCH, D), low), S((13, 16, 512), f32), S((3, 32, 256), f32), S((16, 1920), f32)],
        scratch_shapes=scratch,
        compiler_params=pltpu.CompilerParams(collective_id=2, has_side_effects=True, vmem_limit_bytes=62 * 2**20),
        name="back_and_sums",
    )(d_expand, d_shrink, after, proj, probs, frames, first_low, mixed, wp, wo, mw, mp, mo,
      vec, message, sums, *saved, index_table())


def unpack_kernel(out, out_s, out_m, mw, mp, mo, ap, ao, ew, sw, *vectors):
    def piece(n, side, w):
        return out[n, 8 * side : 8 * side + 6, 0:w]

    message = (out_m[0:6], out_m[8:14])
    mw[...] = message[0][:, 0:D]
    mp[:, 0:1152] = message[0][:, D:1920]
    mp[:, 1152:2304] = message[1][:, 0:1152]
    mo[...] = message[1][:, 1152:1920]
    for k in range(3):
        for side in range(2):
            ap[:, 512 * k + 256 * side : 512 * k + 256 * side + 256] = piece(6 + 2 * k, side, 256)
            ew[:, 1024 * k + 512 * side : 1024 * k + 512 * side + 512] = piece(2 * k, side, 512)
            x = 512 * k + 256 * side
            target, x = (ap, x + 1536) if x < D else (ao, x - D)
            target[:, x : x + 256] = piece(7 + 2 * k, side, 256)
        sw[:, 256 * k : 256 * (k + 1)] = out_s[k, 0:24]
    lanes = lax.broadcasted_iota(jnp.int32, (6, 128), 1)
    rows = lax.broadcasted_iota(jnp.int32, (6, 128), 0)
    values = out[12, 0:6, 0:128]
    flat = jnp.zeros((128, 128), f32)
    for shift in range(4):
        place_at = (lanes == rows + 6 * shift).astype(f32)
        owner = jnp.where((lanes < 24) | (lanes >= 32), 0, jnp.where(lanes < 28, lanes - 24, (lanes - 28) & 1))
        part = jnp.where(owner == shift, values, 0.0)
        flat += lax.dot_general(part, place_at, (((0,), (0,)), ((), ())), precision=PRECISE, preferred_element_type=f32)
    for ref, (row, count) in zip(vectors, LANES):
        ref[...] = jnp.sum(flat[row : row + count], axis=0)[0 : 6 * count]


LANES = ((12, 1), (13, 1), (14, 1), (30, 2), (17, 1), (0, 1), (1, 1), (28, 2), (4, 1), (5, 1), (6, 1), (24, 4), (11, 1))


def unpack(out, out_s, out_m):
    S = jax.ShapeDtypeStruct
    vmem = pl.BlockSpec(memory_space=pltpu.VMEM)
    shapes = [(6, D), (6, 3 * D), (6, D), (6, 3 * D), (6, D), (6, FF), (24, D)] + [(6 * count,) for _, count in LANES]
    return pl.pallas_call(
        unpack_kernel,
        in_specs=[vmem] * 3,
        out_specs=[vmem] * len(shapes),
        out_shape=[S(shape, f32) for shape in shapes],
        compiler_params=pltpu.CompilerParams(vmem_limit_bytes=BIG),
        name="unpack",
    )(out, out_s, out_m)


def forward_kernel(*refs):
    vectors, refs = refs[: len(VECTORS)], refs[len(VECTORS) :]
    (gids, frames_ref, mw_ref, mp_ref, mo_ref, wp_ref, wo_ref, we_ref, ws_ref,
     vec, message, all_cls, pre_out, normed_out, qkv, msg_mixed,
     first_ref, proj_ref, probs_ref, mixed_ref, resid_ref, second_ref, hidden_ref, dgate_ref,
     result, loss, pooled_out, gpool,
     vw, vp, vo, wp, wo, we, ws, frames, cls, tops, first_low, proj, probs, mixed, resid, second_low, xs,
     hid, dg, acc, pool_all, every, natural, grads,
     load_sem, store_sem, probs_sem, send_sem, recv_sem, near_send, near_recv) = refs
    at = place()
    fr = lax.axis_index("frame")

    def load(n, src, dst):
        copy = pltpu.make_async_copy(src, dst, load_sem.at[n])
        copy.start()
        return copy

    def store(n, src, dst):
        copy = pltpu.make_async_copy(src, dst, store_sem.at[n])
        copy.start()
        return copy

    get_frames = load(0, frames_ref, frames)
    get_wp = [load(1 + j, wp_ref.at[:, pl.ds(j * D, D)], wp.at[j]) for j in range(3)]
    get_mw, get_mp, get_mo = load(4, mw_ref, vw), load(5, mp_ref, vp), load(6, mo_ref, vo)
    vec[...] = jnp.zeros((24, D), f32)
    for ref, rows in zip(vectors, VECTORS):
        for k, row in enumerate(rows):
            vec[row : row + 1] = ref[pl.ds(k * D, D)].astype(f32).reshape(1, D)
    cls[...] = jnp.zeros((SLOT, D), f32)
    around = frame_partners()
    order = ("c",) + CLIP_DIMS
    partner = {d: device_of(moved(at, {d: 1})) for d in order}
    greet(around + [partner[d] for d in order])
    get_frames.wait()
    for c in range(CLIPS_HERE):
        cls[c : c + 1] = frames[c, 0, 0:16].astype(f32)[0:1]
    first_near = [remote(cls, all_cls.at[fr], near_send.at[0, k], near_recv.at[0, k], p) for k, p in enumerate(around)]
    all_cls[fr] = cls[...]

    gain, shift = vec[R_FG : R_FG + 1], vec[R_FS : R_FS + 1]
    xs[pl.ds(192, 16)] = jnp.zeros((16, D), f32)
    for c in range(CLIPS_HERE):
        xs[pl.ds(0, PATCH)] = frames[c, 0].astype(f32)
        u, _ = stats(xs[...])
        first_low[pl.ds(c * ROWS, ROWS)] = (u * gain + shift).astype(low)
    for j in range(3):
        get_wp[j].wait()
        for part in range(2):
            rows = pl.ds(part * 2 * ROWS, 2 * ROWS)
            value = dot(first_low[rows], wp[j]) + vec[R_APB + j : R_APB + j + 1]
            proj[rows, j * D : (j + 1) * D] = value.astype(low)
    get_wo = load(7, wo_ref, wo)
    get_we = [load(8 + j, we_ref.at[:, pl.ds(j * D, D)], we.at[j]) for j in range(4)]
    get_ws = [load(12 + j, ws_ref.at[pl.ds(j * D, D)], ws.at[j]) for j in range(4)]

    get_mw.wait()
    for copy in first_near:
        copy.wait_recv()
    x = all_cls[...].reshape(MROWS, D).astype(low)
    pre = dot(x, vw[...]) + vec[R_MB : R_MB + 1]
    pre_out[...] = pre
    u, _ = stats(pre)
    normed = (u * vec[R_MG : R_MG + 1] + vec[R_MS : R_MS + 1]).astype(low)
    normed_out[...] = normed
    get_mp.wait()
    for j in range(3):
        qkv[:, j * D : (j + 1) * D] = (dot(normed, vp[:, j * D : (j + 1) * D]) + vec[R_MPB + j : R_MPB + j + 1]).astype(low)
    keep = same_clip()
    lane = lax.broadcasted_iota(jnp.int32, (MROWS, 128), 1)
    zero = jnp.zeros((), low)
    for pair in range(6):
        q = qkv[:, pair * 128 : pair * 128 + 128]
        k = qkv[:, D + pair * 128 : D + pair * 128 + 128]
        v = qkv[:, 2 * D + pair * 128 : 2 * D + pair * 128 + 128]
        outs = []
        for half in range(2):
            mine = (lane < 64) if half == 0 else (lane >= 64)
            s = jnp.where(keep, dot_t(jnp.where(mine, q, zero), k) * 0.125, -1e30)
            outs.append(dot(soft(s).astype(low), v))
        msg_mixed[:, pair * 128 : pair * 128 + 128] = jnp.where(lane < 64, outs[0], outs[1]).astype(low)
    get_mo.wait()
    branch = pre + dot(msg_mixed[...], vo[...]) + vec[R_MOB : R_MOB + 1]
    rows = lax.broadcasted_iota(jnp.int32, (MROWS, 1), 0) // SLOT
    message[...] = jnp.sum(jnp.where(rows == fr, branch, 0.0).reshape(FRAMES, SLOT, D), axis=0)

    u, _ = stats(message[...])
    ends = (u * gain + shift).astype(low)
    spot = lax.broadcasted_iota(jnp.int32, (16, 1), 0) == PATCH - 192
    for c in range(CLIPS_HERE):
        window = pl.ds(c * ROWS + 192, 16)
        row = ends[c : c + 1].astype(f32)
        first_low[window] = jnp.where(spot, row, first_low[window].astype(f32)).astype(low)
    for j in range(3):
        row = dot(ends, wp[j]) + vec[R_APB + j : R_APB + j + 1]
        for c in range(CLIPS_HERE):
            window = pl.ds(c * ROWS + 192, 16)
            old = proj[window, j * D : (j + 1) * D].astype(f32)
            proj[window, j * D : (j + 1) * D] = jnp.where(spot, row[c : c + 1], old).astype(low)
    stores = [store(0, first_low, first_ref), store(1, proj, proj_ref)]

    lane = lax.broadcasted_iota(jnp.int32, (ROWS, 128), 1)
    seen = lax.broadcasted_iota(jnp.int32, (ROWS, ROWS), 0) < PATCH + 1

    def probs_out(clip):
        return pltpu.make_async_copy(probs.at[clip % 2], probs_ref.at[clip], probs_sem.at[clip % 2])

    def one_clip(clip, carry):
        @pl.when(clip >= 2)
        def _():
            probs_out(clip - 2).wait()

        rows = pl.ds(pl.multiple_of(clip * ROWS, 16), ROWS)
        for pair in range(6):
            q, k, v = (proj[rows, n * D + pair * 128 : n * D + pair * 128 + 128] for n in range(3))
            total = 0.0
            for half in range(2):
                mine = (lane < 64) if half == 0 else (lane >= 64)
                s = dot_t(jnp.where(mine, k, zero), q) * 0.125
                s = jnp.where(seen, s, -1e30)
                e = jnp.exp(s - jnp.max(s, axis=0, keepdims=True))
                p = (e * (1.0 / jnp.sum(e, axis=0, keepdims=True))).astype(low)
                probs[clip % 2, 2 * pair + half] = p
                total = total + dot_tl(p, jnp.where(mine, v, zero))
            mixed[rows, pair * 128 : pair * 128 + 128] = total.astype(low)
        probs_out(clip).start()
        return carry

    lax.fori_loop(0, CLIPS_HERE, one_clip, 0)
    stores.append(store(2, mixed, mixed_ref))
    get_wo.wait()
    for part in range(2):
        branch = dot(mixed[pl.ds(part * 2 * ROWS, 2 * ROWS)], wo[...]) + vec[R_AOB : R_AOB + 1]
        for c in (2 * part, 2 * part + 1):
            xs[pl.ds(192, 16)] = jnp.zeros((16, D), f32)
            xs[pl.ds(0, PATCH)] = frames[c, 0].astype(f32)
            after = xs[...] + branch[(c - 2 * part) * ROWS : (c - 2 * part + 1) * ROWS]
            rows = pl.ds(c * ROWS, ROWS)
            resid[rows] = after
            u2, _ = stats(after)
            second_low[rows] = (u2 * vec[R_SG : R_SG + 1] + vec[R_SS : R_SS + 1]).astype(low)
    stores += [store(3, resid, resid_ref), store(4, second_low, second_ref)]

    def gate(h):
        sg = 1.0 / (1.0 + jnp.exp(-1.702 * h))
        hs = h * sg
        return sg, hs

    heads = jnp.concatenate([second_low[pl.ds(c * ROWS, 16)] for c in range(CLIPS_HERE)], axis=0)
    total = jnp.zeros((16 * CLIPS_HERE, D), f32)
    for j in range(4):
        get_we[j].wait()
        _, hs = gate(dot(heads, we[j]) + vec[R_EB + j : R_EB + j + 1])
        get_ws[j].wait()
        total += dot(hs.astype(low), ws[j])
    tops[...] = jnp.zeros((SLOT, D), f32)
    for c in range(CLIPS_HERE):
        tops[c : c + 1] = resid[c * ROWS : c * ROWS + 1] + vec[R_SB : R_SB + 1] + total[16 * c : 16 * c + 1]
    near = [remote(tops, pool_all.at[fr], near_send.at[1, k], near_recv.at[1, k], p) for k, p in enumerate(around)]
    pool_all[fr] = tops[...]

    copies, state = [], {}

    def exchange(k):
        copy = remote(every.at[pl.ds(0, 2**k)], every.at[pl.ds(2**k, 2**k)], send_sem.at[k], recv_sem.at[k],
                      partner[order[k]])
        copies.append(copy)

    def step(k):
        if k == 0:
            for copy in near:
                copy.wait_recv()
            s = pool_all[0]
            for f in range(1, FRAMES):
                s = s + pool_all[f]
            pooled = s * 0.125
            pooled_out[...] = pooled[:CLIPS_HERE]
            inv_len = lax.rsqrt(jnp.sum(pooled * pooled, axis=-1, keepdims=True) + 1e-06)
            state.update(pooled=pooled, inv_len=inv_len)
            every[0] = pooled * inv_len
        else:
            copies[k - 1].wait_recv()
        if k < 4:
            exchange(k)

    tile_stores = []
    for j in range(4):
        if j >= 2:
            for copy in tile_stores[2 * (j - 2) : 2 * (j - 1)]:
                copy.wait()
        for part in range(2):
            rows = pl.ds(part * 2 * ROWS, 2 * ROWS)
            h = dot(second_low[rows], we[j]) + vec[R_EB + j : R_EB + j + 1]
            sg, hs = gate(h)
            hidden = hs.astype(low)
            hid[j % 2, rows] = hidden
            dg[j % 2, rows] = (sg + 1.702 * hs * (1.0 - sg)).astype(low)
            out = dot(hidden, ws[j])
            acc[rows] = (resid[rows] + vec[R_SB : R_SB + 1] if j == 0 else acc[rows]) + out
            k = 2 * j + part - 2
            if 0 <= k <= 4:
                step(k)
        for n, (src, dst) in enumerate(((hid, hidden_ref), (dg, dgate_ref))):
            copy = pltpu.make_async_copy(src.at[j % 2], dst.at[:, pl.ds(j * D, D)], store_sem.at[5 + 4 * n + j])
            copy.start()
            tile_stores.append(copy)
    for c in range(CLIPS_HERE):
        result[c, 0] = acc[pl.ds(c * ROWS, PATCH)].astype(low)
    for p in range(16):
        to = moved(at, {d: (p >> k) & 1 for k, d in enumerate(order)})
        natural[dp_of(to)] = every[p]
    n = natural[...].reshape(128, D)
    sims = 50.0 * lax.dot_general(n, n, (((1,), (1,)), ((), ())), precision=PRECISE, preferred_element_type=f32)
    rows = lax.broadcasted_iota(jnp.int32, (128, 128), 0)
    cols = lax.broadcasted_iota(jnp.int32, (128, 128), 1)
    here = (cols & 7) < CLIPS_HERE
    other = here & (rows != cols)
    slot = lax.broadcasted_iota(jnp.int32, (128, 64), 0)
    clip = lax.broadcasted_iota(jnp.int32, (128, 64), 1)
    spot = (((slot >> 3) * CLIPS_HERE + (slot & 7)) == clip) & ((slot & 7) < CLIPS_HERE)
    wide = jnp.broadcast_to(gids[...].astype(f32), (128, 64))
    mine = jnp.where(spot, wide, 0.0)
    gid_col = jnp.sum(mine, axis=-1, keepdims=True)
    gid_row = lax.dot_general(wide, spot.astype(f32), (((1,), (1,)), ((), ())), precision=PRECISE, preferred_element_type=f32)
    same = other & (gid_col == gid_row)
    valid = (lax.broadcasted_iota(jnp.int32, (128, 1), 0) & 7) < CLIPS_HERE

    def log_soft(logits):
        top = jnp.max(logits, axis=-1, keepdims=True)
        e = jnp.exp(logits - top)
        total = jnp.sum(e, axis=-1, keepdims=True)
        return top + jnp.log(total), e / total

    all_log, all_p = log_soft(jnp.where(other, sims, -1e30))
    pos_log, pos_p = log_soft(jnp.where(same, sims, -1e30))
    terms = jnp.where(valid, all_log - pos_log, 0.0)
    loss[...] = jnp.sum(terms, axis=0, keepdims=True) * (1.0 / 64.0)
    gs = jnp.where(valid & here, all_p - pos_p, 0.0)
    grad_all = 50.0 * jnp.dot(gs + gs.T, n, precision=PRECISE, preferred_element_type=f32)
    grads[...] = grad_all.reshape(16, SLOT, D)
    g = grads[lax.axis_index("dp")]
    pooled, inv_len = state["pooled"], state["inv_len"]
    back = inv_len * g - inv_len * inv_len * inv_len * pooled * jnp.sum(pooled * g, axis=-1, keepdims=True)
    gpool[...] = back * 0.125
    for copy in tile_stores[4:] + stores:
        copy.wait()
    for clip in (CLIPS_HERE - 2, CLIPS_HERE - 1):
        probs_out(clip).wait()
    for copy in first_near + near + copies:
        copy.wait_send()


def forward(vectors, gids, frames, mw, mp, mo, wp, wo, we, ws):
    vmem = pl.BlockSpec(memory_space=pltpu.VMEM)
    any_spec = pl.BlockSpec(memory_space=pl.ANY)
    S, V, SEM = jax.ShapeDtypeStruct, pltpu.VMEM, pltpu.SemaphoreType.DMA
    return pl.pallas_call(
        forward_kernel,
        in_specs=[vmem] * (len(VECTORS) + 1) + [any_spec] * 8,
        out_specs=[vmem] * 7 + [any_spec] * 8 + [vmem] * 4,
        out_shape=[
            S((24, D), f32), S((SLOT, D), f32), S((FRAMES, SLOT, D), f32), S((MROWS, D), f32), S((MROWS, D), low),
            S((MROWS, 3 * D), low), S((MROWS, D), low),
            S((ALL, D), low), S((ALL, 3 * D), low), S((CLIPS_HERE, 12, ROWS, ROWS), low), S((ALL, D), low), S((ALL, D), f32),
            S((ALL, D), low), S((ALL, FF), low), S((ALL, FF), low),
            S((CLIPS_HERE, 1, PATCH, D), low), S((1, 1), f32), S((CLIPS_HERE, D), f32), S((SLOT, D), f32)],
        scratch_shapes=[
            V((D, D), low), V((D, 3 * D), low), V((D, D), low), V((3, D, D), low), V((D, D), low), V((4, D, D), low),
            V((4, D, D), low), V((CLIPS_HERE, 1, PATCH, D), low), V((SLOT, D), f32), V((SLOT, D), f32), V((ALL, D), low),
            V((ALL, 3 * D), low), V((2, 12, ROWS, ROWS), low), V((ALL, D), low), V((ALL, D), f32), V((ALL, D), low),
            V((ROWS, D), f32), V((2, ALL, D), low), V((2, ALL, D), low), V((ALL, D), f32), V((FRAMES, SLOT, D), f32),
            V((16, SLOT, D), f32), V((16, SLOT, D), f32), V((16, SLOT, D), f32),
            SEM((16,)), SEM((13,)), SEM((2,)), SEM((4,)), SEM((4,)), SEM((2, 7)), SEM((2, 7))],
        compiler_params=pltpu.CompilerParams(collective_id=0, has_side_effects=True, vmem_limit_bytes=62 * 2**20),
        name="forward",
    )(*vectors, gids, frames, mw, mp, mo, wp, wo, we, ws)


def on_device(
    frames, cotangent, group_ids, message_weight, message_bias, message_gain, message_shift, message_project,
    message_project_bias, message_output, message_output_bias, first_gain, first_shift, attend_project,
    attend_project_bias, attend_output, attend_output_bias, second_gain, second_shift, expand_weight, expand_bias,
    shrink_weight, shrink_bias,
):
    vectors = (
        message_bias, message_gain, message_shift, message_project_bias, message_output_bias, first_gain, first_shift,
        attend_project_bias, attend_output_bias, second_gain, second_shift, expand_bias, shrink_bias,
    )
    (vec, message, *saved, first_low, proj, probs, mixed, resid, second_low, hidden, dgate, result, loss, pooled,
     gpool) = forward(
        vectors, group_ids.reshape(1, 64), frames, message_weight, message_project, message_output, attend_project,
        attend_output, expand_weight, shrink_weight)
    d_expand, d_shrink, after, sums = mlp_back(
        cotangent, gpool, vec, hidden, dgate, second_low, expand_weight, shrink_weight, resid)
    delta_frames, out, out_s, out_m = back_and_sums(
        d_expand, d_shrink, after, proj, probs, frames, first_low, mixed, attend_project, attend_output, message_weight,
        message_project, message_output, vec, message, sums, saved)
    mw, mp, mo, ap, ao, ew, sw, mb, mg, ms, mpb, mob, fg, fs, apb, aob, sg, ss, eb, sb = unpack(out, out_s, out_m)
    return (
        result, loss.reshape(()), pooled, delta_frames, mw, mb, mg, ms, mp, mpb, mo, mob, fg, fs, ap, apb, ao, aob, sg, ss,
        ew, eb, sw, sb,
    )


def solution(mesh):
    placed = (
        P("dp", "frame", None, None),
        P("dp", "frame", None, None),
        P(),
        P(),
        P(),
        P(),
        P(),
        P(),
        P(),
        P(),
        P(),
        P(),
        P(),
        P(),
        P(),
        P(),
        P(),
        P(),
        P(),
        P(),
        P(),
        P(),
        P(),
    )
    return jax.shard_map(
        on_device,
        mesh=mesh,
        in_specs=placed,
        out_specs=(
            P("dp", "frame", None, None),
            P(),
            P("dp", None),
            P("dp", "frame", None, None),
            P(("dp", "frame"), None),
            P(("dp", "frame")),
            P(("dp", "frame")),
            P(("dp", "frame")),
            P(("dp", "frame"), None),
            P(("dp", "frame")),
            P(("dp", "frame"), None),
            P(("dp", "frame")),
            P(("dp", "frame")),
            P(("dp", "frame")),
            P(("dp", "frame"), None),
            P(("dp", "frame")),
            P(("dp", "frame"), None),
            P(("dp", "frame")),
            P(("dp", "frame")),
            P(("dp", "frame")),
            P(("dp", "frame"), None),
            P(("dp", "frame")),
            P(("dp", "frame"), None),
            P(("dp", "frame")),
        ),
        check_vma=False,
    )
```

```python
import functools

import jax
import jax.numpy as jnp
import numpy as np
from jax import lax
from jax.experimental import pallas as pl
from jax.experimental.pallas import tpu as pltpu
from jax.sharding import PartitionSpec as P

f32, low = jnp.float32, jnp.bfloat16
CLIPS_HERE, PATCH, ROWS, D, FF = 4, 197, 208, 768, 3072
ALL = CLIPS_HERE * ROWS
BIG = 58 * 2**20
(R_MB, R_MG, R_MS, R_MPB, R_MOB, R_FG, R_FS, R_APB, R_AOB, R_SG, R_SS, R_EB, R_SB) = (
    0, 1, 2, 3, 6, 7, 8, 9, 12, 13, 14, 15, 19)


def dot(a, b):
    return jnp.dot(a, b, preferred_element_type=f32)


def dot_t(a, b):
    return lax.dot_general(a, b, (((1,), (1,)), ((), ())), preferred_element_type=f32)


def dot_tl(a, b):
    return lax.dot_general(a, b, (((0,), (0,)), ((), ())), preferred_element_type=f32)


def stats(x):
    mean = jnp.mean(x, axis=-1, keepdims=True)
    centered = x - mean
    inv = lax.rsqrt(jnp.mean(centered * centered, axis=-1, keepdims=True) + 1e-05)
    return centered * inv, inv


def norm_back(grad, u, inv, gain):
    h = grad * gain
    return (h - jnp.mean(h, axis=-1, keepdims=True) - u * jnp.mean(h * u, axis=-1, keepdims=True)) * inv


def const(shape):
    return pl.BlockSpec(shape, lambda *i: (0,) * len(shape))


MESH = pl.DeviceIdType.MESH


def flip_low(index):
    return index + 1 - 2 * (index % 2)


def flip_pair(index, high, low):
    index = 3 - index if high else index
    return flip_low(index) if low else index


def place():
    dp, fr = lax.axis_index("dp"), lax.axis_index("frame")
    return dict(y=dp // 4, x=(dp // 2 % 2) * 2 + fr // 4, z=fr % 4, c=dp % 2)


def moved(at, bits):
    return dict(
        y=flip_pair(at["y"], bits.get("yu"), bits.get("yv")),
        x=flip_pair(at["x"], bits.get("xu"), bits.get("xv")),
        z=flip_pair(at["z"], bits.get("zu"), bits.get("zv")),
        c=1 - at["c"] if bits.get("c") else at["c"],
    )


def dp_of(at):
    return at["y"] * 4 + (at["x"] // 2) * 2 + at["c"]


def frame_of(at):
    return (at["x"] % 2) * 4 + at["z"]


def device_of(at):
    return (dp_of(at), frame_of(at))


CLIP_DIMS = ("yu", "yv", "xu")
FRAME_DIMS = ("xv", "zu", "zv")


def rotated(dims, turn):
    return dims[turn:] + dims[:turn]


def bits_at(dims, position):
    return {dims[k]: (position >> (2 - k)) & 1 for k in range(3)}


def to_units(full):
    return full.reshape(8, 2, 48, full.shape[-1])


FRAMES = 8
SLOT = 8
MROWS = FRAMES * SLOT
SUMS = 24


def greet(partners):
    barrier = pltpu.get_barrier_semaphore()
    for partner in partners:
        pl.semaphore_signal(barrier, inc=1, device_id=partner, device_id_type=MESH)
    pl.semaphore_wait(barrier, len(partners))


def frame_partners():
    dp, fr = lax.axis_index("dp"), lax.axis_index("frame")
    return [(dp, lax.rem(fr + k, FRAMES)) for k in range(1, FRAMES)]


def remote(src, dst, send_sem, recv_sem, device):
    copy = pltpu.make_async_remote_copy(
        src_ref=src, dst_ref=dst, send_sem=send_sem, recv_sem=recv_sem, device_id=device, device_id_type=MESH)
    copy.start()
    return copy


def same_clip():
    rows = lax.broadcasted_iota(jnp.int32, (MROWS, MROWS), 0)
    cols = lax.broadcasted_iota(jnp.int32, (MROWS, MROWS), 1)
    return rows % SLOT == cols % SLOT


def soft(s):
    e = jnp.exp(s - jnp.max(s, axis=-1, keepdims=True))
    return e / jnp.sum(e, axis=-1, keepdims=True)


VECTORS = ((R_MB,), (R_MG,), (R_MS,), (R_MPB, R_MPB + 2), (R_MOB,), (R_FG,), (R_FS,), (R_APB, R_APB + 2), (R_AOB,), (R_SG,),
           (R_SS,), (R_EB, R_EB + 1, R_EB + 2, R_EB + 3), (R_SB,))


PRECISE = lax.Precision.HIGHEST


def message_back(at, cls_all, pre, normed, qkv, mixed, vec, vw, vp, vo, gall, pick, mgrad, gcls, between):
    fr = lax.axis_index("frame")
    g = gall[...].reshape(MROWS, D)
    g_low = g.astype(low)
    gmm = dot_t(g_low, vo[...]).astype(low)
    keep = same_clip()
    lane = lax.broadcasted_iota(jnp.int32, (MROWS, 128), 1)
    zero = jnp.zeros((), low)
    parts = ([], [], [])
    for pair in range(6):
        q = qkv[:, pair * 128 : pair * 128 + 128]
        k = qkv[:, D + pair * 128 : D + pair * 128 + 128]
        v = qkv[:, 2 * D + pair * 128 : 2 * D + pair * 128 + 128]
        gm = gmm[:, pair * 128 : pair * 128 + 128]
        totals = [0.0, 0.0, 0.0]
        for half in range(2):
            mine = (lane < 64) if half == 0 else (lane >= 64)
            q_here, k_here, gm_here = (jnp.where(mine, value, zero) for value in (q, k, gm))
            s = jnp.where(keep, dot_t(k_here, q) * 0.125, -1e30)
            e = jnp.exp(s - jnp.max(s, axis=0, keepdims=True))
            p = e / jnp.sum(e, axis=0, keepdims=True)
            dp = dot_t(v, gm_here)
            gs = (p * (dp - jnp.sum(dp * p, axis=0, keepdims=True))).astype(low)
            products = (dot_tl(gs, k_here), dot(gs, q_here), dot(p.astype(low), gm_here))
            totals = [total + product for total, product in zip(totals, products)]
        for n, scale in ((0, 0.125), (1, 0.125), (2, 1.0)):
            parts[n].append((totals[n] * scale).astype(low))
    gq, gk, gv = (jnp.concatenate(part, axis=1) for part in parts)
    between()
    gnorm = dot_t(gq, vp[:, :D]) + dot_t(gk, vp[:, D : 2 * D]) + dot_t(gv, vp[:, 2 * D :])
    u, inv = stats(pre[...])
    gpre = (g + norm_back(gnorm, u, inv, vec[R_MG : R_MG + 1])).astype(low)

    def total(value):
        return jnp.sum(value.astype(f32), axis=0, keepdims=True)

    mine = (lax.broadcasted_iota(jnp.int32, (96, D), 1) == pick[0:96]).astype(low)
    x = cls_all[...].reshape(MROWS, D).astype(low)
    for unit, (left, right) in enumerate(((x, gpre), (normed[...], gq), (normed[...], gk), (normed[...], gv),
                                          (mixed[...], g_low))):
        turned = dot_t(mine, left).astype(low)
        mgrad[:, :, unit * D : (unit + 1) * D] = dot(turned, right).astype(low).reshape(2, 48, D)
    back = dot_t(gpre, vw[...])
    rows = lax.broadcasted_iota(jnp.int32, (MROWS, 1), 0) // SLOT
    gcls[...] = jnp.sum(jnp.where(rows == fr, back, 0.0).reshape(FRAMES, SLOT, D), axis=0)
    return [total(gpre), total(gnorm * u), total(gnorm), total(gq), total(gv), total(g_low)]


def message_vectors(sums, message_sums, pick, part, mgrad):
    table = jnp.concatenate([sums[0:12], *message_sums, jnp.zeros((SUMS - 18, D), f32)], axis=0).astype(low)
    choose = (lax.broadcasted_iota(jnp.int32, (672, D), 1) == pick[...]).astype(low)
    z = dot_t(choose, table)
    wide = lax.broadcasted_iota(jnp.int32, (96, 128), 1)
    narrow = lax.broadcasted_iota(jnp.int32, (96, SUMS), 1)
    out = jnp.zeros((96, 128), f32)
    out += jnp.concatenate([z[:96], jnp.zeros((96, 128 - SUMS), f32)], axis=1)
    for q in range(4):
        hit = narrow == 7 + part[384:480, 3:4]
        value = jnp.sum(jnp.where(hit, z[96 * (1 + q) : 96 * (2 + q)], 0.0), axis=-1, keepdims=True)
        out = jnp.where(wide == 24 + q, value, out)
    for q in range(2):
        for n, first in enumerate((2, 15)):
            hit = narrow == first + part[384:480, 4:5]
            value = jnp.sum(jnp.where(hit, z[96 * (5 + q) : 96 * (6 + q)], 0.0), axis=-1, keepdims=True)
            out = jnp.where(wide == 28 + 2 * n + q, value, out)
    mgrad[:, :, 5 * D : 5 * D + 128] = out.astype(low).reshape(2, 48, 128)


def index_table():
    table = np.zeros((384 + 672, 8), np.int32)
    r = np.arange(384)
    table[:384, 0] = r // 48
    table[:384, 1] = r % 48 // 6 * 48 + r % 6
    table[:384, 2] = r % 48 // 6 % 2
    r = np.arange(96)
    c, y, xh, i = r // 48, r % 48 // 12, r % 12 // 6, r % 6
    high = y * 4 + xh * 2 + c
    picks = [(high * 48 + i, 6)]
    picks += [(high % 4 * 192 + q * 6 + i, 24) for q in range(4)]
    picks += [(high % 8 * 96 + q * 6 + i, 12) for q in range(2)]
    for n, (base, step) in enumerate(picks):
        rows = slice(384 + 96 * n, 384 + 96 * (n + 1))
        table[rows, 0], table[rows, 1], table[rows, 2] = base, step, xh
        table[rows, 3], table[rows, 4] = y, y // 2
    return jnp.asarray(table)


def fill_orders(at, table, sa, sb, mix, pick):
    xh, xl = at["x"] // 2, at["x"] % 2
    rows = lax.broadcasted_iota(jnp.int32, (128, 48), 0)
    cols = lax.broadcasted_iota(jnp.int32, (128, 48), 1)
    for ref, dims in ((sa, FRAME_DIMS), (sb, CLIP_DIMS)):
        block = jnp.zeros((128, 48), jnp.int32)
        for p in range(8):
            to = moved(at, bits_at(dims, p))
            value = frame_of(to) if dims == FRAME_DIMS else dp_of(to) // 2
            block = jnp.where((rows >> 4) == p, value, block)
        for half in range(2):
            inner = (rows & 15) - 8 * half
            hit = (cols == block * 6 + inner) & (inner >= 0) & (inner < 6)
            ref[half] = hit.astype(f32).astype(low)
    lanes = lax.broadcasted_iota(jnp.int32, (384, 384), 1)
    p_col, base, same = table[0:384, 0:1], table[0:384, 1:2], table[0:384, 2:3] == xh
    for turn in range(3):
        frame = jnp.zeros((384, 1), jnp.int32)
        for p in range(8):
            to = moved(at, bits_at(rotated(FRAME_DIMS, turn), p))
            side = to["x"] % 2
            frame = jnp.where(p_col == p, jnp.where(same, 4 * side + to["z"], 4 * (1 - side) + to["z"]), frame)
        mix[turn] = (lanes == base + 6 * frame).astype(f32).astype(low)
    base, step, same = table[384:, 0:1], table[384:, 1:2], table[384:, 2:3] == xh
    pick[...] = base + step * jnp.where(same, 4 * xl + at["z"], 4 * (1 - xl) + at["z"])


CORE, S1, S2, S3 = range(4)
KEEP = (4, 2, 1)
KIND = ("a", "s") * 3 + ("a", "b") * 3 + ("m",) * 2
TURN = (0, 0, 1, 1, 2, 2) * 2
N_PARTS = 14


GROUPS = (
    ((0, 2, 4), 16, 512, FRAME_DIMS), ((1, 3, 5), 32, 256, CLIP_DIMS), ((6, 8, 10), 16, 256, FRAME_DIMS),
    ((7, 9, 11), 16, 256, CLIP_DIMS), ((12,), 16, 1920, CLIP_DIMS), ((13,), 16, 128, CLIP_DIMS),
)
FEED_A, FEED_S, LATE_A, LATE_B, MESSAGE, VECTOR = range(6)


def order_of(n):
    return rotated(CLIP_DIMS if KIND[n] == "a" else FRAME_DIMS, TURN[n])


def mlp_back_kernel(cot, gpool, vec, hidden, dgate, second_low, we, ws, resid,
                    out_e, out_s, after, sums, gl, gb, gsec, tile_e, tile_s, got_e, got_s, put_e, put_s, wide,
                    send_sem, recv_sem, store_sem):
    j = pl.program_id(0)
    at = place()
    core = at["c"]
    other = device_of(moved(at, {"c": 1}))

    def pair_copies(n):
        return [pltpu.make_async_remote_copy(
            src_ref=tile.at[n % 2, :, 1 - core], dst_ref=got.at[n], send_sem=send_sem.at[k, n], recv_sem=recv_sem.at[k, n],
            device_id=other, device_id_type=MESH) for k, (tile, got) in enumerate(((tile_e, got_e), (tile_s, got_s)))]

    def puts(n):
        return [pltpu.make_async_copy(put_e.at[n % 2], out_e.at[:, :, pl.ds(n * D, D)], store_sem.at[0, n]),
                pltpu.make_async_copy(put_s.at[n % 2], out_s.at[:, pl.ds(48 * n, 48)], store_sem.at[1, n])]

    def fold(n):
        if n >= 2:
            for copy in puts(n - 2):
                copy.wait()
        for copy in pair_copies(n):
            copy.wait_recv()
        for k in range(3):
            first, stop = max(1024 * k, D * n) - D * n, min(1024 * (k + 1), D * (n + 1)) - D * n
            if first < stop:
                for p in range(8):
                    chunk = dp_of(moved(at, bits_at(order_of(2 * k), p))) // 2
                    put_e[n % 2, p, :, first:stop] = (
                        tile_e[n % 2, chunk, core, :, first:stop] + got_e[n, chunk, :, first:stop])
        for xh in range(2):
            wide[xh] = (tile_s[n % 2, xh, core] + got_s[n, xh]).astype(f32).reshape(8, 24, D)
        for k in range(3):
            cols = pl.ds(256 * k, 256)
            for p in range(8):
                to = moved(at, bits_at(order_of(2 * k + 1), p))
                rows = []
                for xh in range(2):
                    side = lax.rem(to["x"] % 2 + at["x"] // 2 + xh, 2)
                    rows.append(wide[xh, side * 4 + to["z"], :, cols])
                put_s[n % 2, p, :, cols] = jnp.concatenate(rows, axis=0).astype(low)
        for copy in puts(n):
            copy.start()

    @pl.when(j == 0)
    def _():
        greet([other])
        gl[...] = jnp.zeros((ALL, D), f32)
        for c in range(CLIPS_HERE):
            gl[pl.ds(c * ROWS, PATCH)] = cot[c, 0].astype(f32)
            gl[pl.ds(c * ROWS, 1)] += gpool[pl.ds(c, 1)]
        gb[...] = gl[...].astype(low)
        gsec[...] = jnp.zeros((ALL, D), f32)
        sums[...] = jnp.zeros((24, D), f32)
        sums[11:12] = jnp.sum(gb[...].astype(f32), axis=0, keepdims=True)

    for n in (2, 3):
        @pl.when(j == n)
        def _(n=n):
            for copy in pair_copies(n - 2):
                copy.wait_send()

    tile_s[j % 2] = dot_tl(hidden[...], gb[...]).astype(low).reshape(2, 2, 192, D)
    ghp = (dot_t(gb[...], ws[...]) * dgate[...].astype(f32)).astype(low)
    sums[pl.ds(7 + j, 1)] = jnp.sum(ghp.astype(f32), axis=0, keepdims=True)
    tile_e[j % 2] = dot_tl(second_low[...], ghp).astype(low).reshape(8, 2, 48, D)
    for n in range(4):
        @pl.when(j == n)
        def _(n=n):
            for copy in pair_copies(n):
                copy.start()

    gsec[...] += dot_t(ghp, we[...])
    for n in range(3):
        @pl.when(j == n + 1)
        def _(n=n):
            fold(n)

    @pl.when(j == 3)
    def _():
        gain = vec[R_SG : R_SG + 1]
        total = [jnp.zeros((1, D), f32) for _ in range(3)]
        for c in range(CLIPS_HERE):
            rows = pl.ds(c * ROWS, ROWS)
            u, inv = stats(resid[rows])
            g = gsec[rows]
            out = gl[rows] + norm_back(g, u, inv, gain)
            after[rows] = out
            total[0] += jnp.sum(g * u, axis=0, keepdims=True)
            total[1] += jnp.sum(g, axis=0, keepdims=True)
            total[2] += jnp.sum(out.astype(low).astype(f32), axis=0, keepdims=True)
        sums[5:6] = total[0]
        sums[6:7] = total[1]
        sums[4:5] = total[2]
        fold(3)
        for n in (2, 3):
            for copy in pair_copies(n):
                copy.wait_send()
            for copy in puts(n):
                copy.wait()


def mlp_back(cot, gpool, vec, hidden, dgate, second_low, we, ws, resid):
    tile = pl.BlockSpec((ALL, D), lambda j: (0, j))
    any_spec = pl.BlockSpec(memory_space=pl.ANY)
    S, V, SEM = jax.ShapeDtypeStruct, pltpu.VMEM, pltpu.SemaphoreType.DMA
    return pl.pallas_call(
        mlp_back_kernel,
        grid=(4,),
        in_specs=[const((CLIPS_HERE, 1, PATCH, D)), const((8, D)), const((24, D)), tile, tile, const((ALL, D)),
                  pl.BlockSpec((D, D), lambda j: (0, j)), pl.BlockSpec((D, D), lambda j: (j, 0)), const((ALL, D))],
        out_specs=[any_spec, any_spec, const((ALL, D)), const((24, D))],
        out_shape=[S((8, 48, FF), low), S((8, 192, D), low), S((ALL, D), f32), S((24, D), f32)],
        scratch_shapes=[V((ALL, D), f32), V((ALL, D), low), V((ALL, D), f32), V((2, 8, 2, 48, D), low),
                        V((2, 2, 2, 192, D), low), V((4, 8, 48, D), low), V((4, 2, 192, D), low), V((2, 8, 48, D), low),
                        V((2, 8, 48, D), low), V((2, 8, 24, D), f32), SEM((2, 4)), SEM((2, 4)), SEM((2, 4))],
        compiler_params=pltpu.CompilerParams(collective_id=1, has_side_effects=True, vmem_limit_bytes=BIG),
        name="mlp_back",
    )(cot, gpool, vec, hidden, dgate, second_low, we, ws, resid)


def back_kernel(
    e_ref, s_ref, after_ref, proj_ref, probs_ref, frames_ref, first_ref, mixed_ref, wp_ref, wo_ref, mw_ref, mp_ref, mo_ref,
    vec, message, sums_in, cls_all, pre, normed, qkv, msg_mixed, table,
    tokens, out, out_s, out_m,
    wp, wo, mw, mo, after, proj, probs, frames, first_low, mixed, xs, gm_all, heads, sums, gmsg, gcls, mgrad, mgot,
    gall, sums_low, sall, sa, sb, mix, pick, wide_s,
    own_a, ra1, ra2, ra3, own_s, rs1, rs2, rs3, late, acc_l, got_l, rl1, rl2, rl3,
    t0, t1, t2, t3, t4, t5, v0, v1, v2, v3, v4, v5,
    load_sem, probs_sem, local_sem, send_sem, recv_sem, near_send, near_recv, last_send, last_recv,
):
    at = place()
    fr = lax.axis_index("frame")
    core = at["c"]
    around = frame_partners()
    partners = {d: device_of(moved(at, {d: 1})) for d in ("c",) + CLIP_DIMS + FRAME_DIMS}

    def load(n, src, dst):
        copy = pltpu.make_async_copy(src, dst, load_sem.at[n])
        copy.start()
        return copy

    def probs_copy(clip):
        return pltpu.make_async_copy(probs_ref.at[clip], probs.at[clip % 2], probs_sem.at[clip % 2])

    probs_copy(0).start()
    get_wo, get_after, get_proj = load(0, wo_ref, wo), load(1, after_ref, after), load(2, proj_ref, proj)
    clip_cube = [device_of(moved(at, bits_at(CLIP_DIMS, p))) for p in range(1, 8)]
    greet(around + clip_cube + [partners["c"]])

    def mine(n, lead):
        if n < 6:
            return (own_a if n % 2 == 0 else own_s).at[n // 2, lead]
        return acc_l.at[n - 6, lead]

    def got(n):
        return got_l.at[n - 6]

    def half(n, s):
        if n < 6:
            return ((ra1, ra2, ra3) if n % 2 == 0 else (rs1, rs2, rs3))[s - 1].at[n // 2]
        return (rl1, rl2, rl3)[s - 1].at[n - 6]

    kept_blocks, sent_blocks = (t0, t1, t2, t3, t4, t5), (v0, v1, v2, v3, v4, v5)

    def group_of(n):
        return next((g, group[0].index(n), group) for g, group in enumerate(GROUPS) if n in group[0])

    def chunk_at(n, p):
        return dp_of(moved(at, bits_at(order_of(n), p))) // 2

    def source(n, which):
        if n < 6:
            step = 1024 if n % 2 == 0 else 256
            return (e_ref if n % 2 == 0 else s_ref).at[pl.ds(4 * which, 4), :, pl.ds(n // 2 * step, step)]
        return late.at[n % 2, :, which, :, pl.ds((n - 6) // 2 * 512, 512)]

    def local(n):
        return pltpu.make_async_copy(source(n, 0), mine(n, pl.ds(0, 4)), local_sem.at[n])

    registry = {}

    def define(n, step, src, dst, dim):
        def make():
            return pltpu.make_async_remote_copy(
                src_ref=src(), dst_ref=dst(), send_sem=send_sem.at[n, step], recv_sem=recv_sem.at[n, step],
                device_id=partners[dim], device_id_type=MESH)
        registry[n, step] = make

    def define_part(n):
        if KIND[n] == "m":
            return
        if n >= 6:
            define(n, CORE, lambda: source(n, 1 - core), lambda: got(n), "c")
        for s, first in ((1, S1), (2, S2), (3, S3)):
            keep, dim = KEEP[s - 1], order_of(n)[s - 1]
            if s == 1 and n < 6:
                define(n, first, lambda: source(n, 1), lambda: half(n, 1), dim)
            else:
                define(n, first, lambda keep=keep: mine(n, pl.ds(keep, keep)), lambda s=s: half(n, s), dim)

    def last_copy(g, p):
        return pltpu.make_async_remote_copy(
            src_ref=kept_blocks[g].at[p], dst_ref=sent_blocks[g].at[p - 1], send_sem=last_send.at[g, p - 1],
            recv_sem=last_recv.at[g, p - 1], device_id=device_of(moved(at, bits_at(GROUPS[g][3], p))),
            device_id_type=MESH)

    for n in range(N_PARTS):
        define_part(n)

    def start(n, step):
        registry[n, step]().start()

    def arrived(n, step):
        registry[n, step]().wait_recv()

    for n in range(6):
        start(n, S1)
    fill_orders(at, table, sa, sb, mix, pick)
    sums[...] = sums_in[...]
    gmsg[...] = jnp.zeros((SLOT, D), f32)

    def begin(n):
        arrived(n, CORE)
        own = source(n, core)
        if KIND[n] == "a":
            for p in range(8):
                chunk = chunk_at(n, p)
                mine(n, p)[...] = own[chunk] + got(n)[chunk]
        else:
            full = (own[...] + got(n)[...]).reshape(384, 512)
            mine(n, pl.ds(0, 8))[...] = dot(mix[TURN[n]], full).astype(low).reshape(8, 48, 512)
        start(n, S1)

    def spread(n, last):
        g, k, (_, _, w, dims) = group_of(n)
        blocks, cols = kept_blocks[g], pl.ds(k * w, w)
        if KIND[n] == "s":
            wide_s[...] = last.astype(f32).reshape(8, 24, 256)
            for p in range(8):
                chunk = dp_of(moved(at, bits_at(dims, p))) // 2
                rows = jnp.concatenate([wide_s[chunk], jnp.zeros((8, 256), f32)], axis=0)
                blocks[p, :, cols] = rows.astype(low)
        else:
            orders = sa if dims == FRAME_DIMS else sb
            wide = dot(orders[0], last[:, :w])
            if KIND[n] != "m" or n == 12:
                wide += dot(orders[1], last[:, w:])
            blocks[:, :, cols] = wide.astype(low).reshape(8, 16, w)

    def send_last(g):
        for p in range(1, 8):
            last_copy(g, p).start()

    def finish(g):
        parts, _, w, _ = GROUPS[g]
        total = kept_blocks[g][0].astype(f32)
        for p in range(1, 8):
            last_copy(g, p).wait_recv()
            total = total + sent_blocks[g][p - 1].astype(f32)
        for k, n in enumerate(parts):
            if KIND[n] == "s":
                out_s[k] = total[:, k * w : (k + 1) * w]
            else:
                (out_m if n == 12 else out.at[n - n // 13])[:, 0:w] = total[:, k * w : (k + 1) * w]

    def middle(n, s):
        keep = KEEP[s - 1]
        if s == 1 and n < 6:
            local(n).wait()
        arrived(n, (S1, S2, S3)[s - 1])
        if s == 3:
            spread(n, mine(n, 0)[...] + half(n, 3)[0])
            return
        kept = mine(n, pl.ds(0, keep))
        kept[...] = kept[...] + half(n, s)[...]
        start(n, (S2, S3)[s - 1])

    def every(action, parts, *args):
        for n in parts:
            action(n, *args)

    lane = lax.broadcasted_iota(jnp.int32, (ROWS, 128), 1)
    zero = jnp.zeros((), low)
    get_wo.wait()
    get_after.wait()
    gm_all[...] = dot_t(after[...].astype(low), wo[...]).astype(low)
    get_proj.wait()
    for n in range(6):
        local(n).start()
    get_wp, get_first, get_mixed = load(4, wp_ref, wp), load(5, first_ref, first_low), load(6, mixed_ref, mixed)
    get_frames, get_mw, get_mo = load(3, frames_ref, frames), load(7, mw_ref, mw), load(8, mo_ref, mo)

    def one_clip(clip, carry):
        @pl.when(clip < CLIPS_HERE - 1)
        def _():
            probs_copy(clip + 1).start()

        rows = pl.ds(pl.multiple_of(clip * ROWS, 16), ROWS)
        probs_copy(clip).wait()
        for pair in range(6):
            cols = [pl.ds(n * D + pair * 128, 128) for n in range(3)]
            q, k, v = (proj[rows, c] for c in cols)
            gm = gm_all[rows, pair * 128 : pair * 128 + 128]
            totals = [0.0, 0.0, 0.0]
            for side in range(2):
                here = (lane < 64) if side == 0 else (lane >= 64)
                q_here, k_here, gm_here = (jnp.where(here, value, zero) for value in (q, k, gm))
                dp = dot_t(v, gm_here)
                p_low = probs[clip % 2, 2 * pair + side]
                p = p_low.astype(f32)
                gs = (p * (dp - jnp.sum(dp * p, axis=0, keepdims=True))).astype(low)
                parts = (dot_tl(gs, k_here), dot(gs, q_here), dot(p_low, gm_here))
                totals = [total + part for total, part in zip(totals, parts)]
            for n, scale in ((0, 0.125), (1, 0.125), (2, 1.0)):
                proj[rows, cols[n]] = (totals[n] * scale).astype(low)

        @pl.when(clip == 2)
        def _():
            every(middle, range(6), 1)

        return carry

    lax.fori_loop(0, CLIPS_HERE, one_clip, 0)

    get_wp.wait()
    ends = jnp.concatenate([proj[pl.ds(c * ROWS + 192, 16)] for c in range(CLIPS_HERE)], axis=0)
    grad = jnp.zeros((16 * CLIPS_HERE, D), f32)
    for n in range(3):
        grad += dot_t(ends[:, n * D : (n + 1) * D], wp[:, n * D : (n + 1) * D])
    for c in range(CLIPS_HERE):
        gmsg[c : c + 1] = grad[16 * c + 5 : 16 * c + 6]
    u, inv = stats(message[...])
    gmsg[...] = norm_back(gmsg[...], u, inv, vec[R_FG : R_FG + 1])
    near = []
    for k, partner in enumerate(around):
        near.append(remote(gmsg, gall.at[fr], near_send.at[0, k], near_recv.at[0, k], partner))
    gall[fr] = gmsg[...]
    get_first.wait()
    get_mixed.wait()

    def late_grad(side, first, stop, left, right):
        grad = dot_tl(left[...], right)
        late[side, :, :, :, pl.ds(first, stop - first)] = grad.astype(low).reshape(8, 2, 48, stop - first)

    late_grad(0, 0, 512, first_low, proj[:, 0:512])
    start(6, CORE)
    late_grad(0, 512, 1024, first_low, proj[:, 512:1024])
    start(8, CORE)
    late_grad(0, 1024, 1536, first_low, proj[:, 1024:1536])
    start(10, CORE)
    begin(6)
    late_grad(1, 0, 768, first_low, proj[:, 1536:2304])
    start(7, CORE)
    begin(8)
    late_grad(1, 768, 1536, mixed, after[...].astype(low))
    start(9, CORE)
    start(11, CORE)
    begin(10)
    every(middle, range(6), 2)
    begin(7)
    begin(9)
    begin(11)
    every(middle, range(6), 3)
    send_last(FEED_A)
    send_last(FEED_S)
    for n in (0, 2):
        total = jnp.zeros((1, D), f32)
        for c in range(CLIPS_HERE):
            total += jnp.sum(proj[pl.ds(c * ROWS, ROWS), n * D : (n + 1) * D].astype(f32), axis=0, keepdims=True)
        to = 2 if n == 0 else 3
        sums[to : to + 1] = total
    get_frames.wait()

    def token_grads(first):
        two = pl.ds(first * ROWS, 2 * ROWS)
        grad_two = jnp.zeros((2 * ROWS, D), f32)
        for n in range(3):
            grad_two += dot_t(proj[two, n * D : (n + 1) * D], wp[:, n * D : (n + 1) * D])
        for clip in (first, first + 1):
            grad = grad_two[(clip - first) * ROWS : (clip - first + 1) * ROWS]
            xs[pl.ds(192, 16)] = jnp.zeros((16, D), f32)
            xs[pl.ds(0, PATCH)] = frames[clip, 0].astype(f32)
            xs[pl.ds(PATCH, 1)] = message[clip : clip + 1]
            u, inv = stats(xs[...])
            sums[0:1] += jnp.sum(grad * u, axis=0, keepdims=True)
            sums[1:2] += jnp.sum(grad, axis=0, keepdims=True)
            xs[...] = after[pl.ds(clip * ROWS, ROWS)] + norm_back(grad, u, inv, vec[R_FG : R_FG + 1])
            tokens[clip, 0] = xs[pl.ds(0, PATCH)].astype(low)
            heads[clip] = xs[pl.ds(0, 16)]

    sums[0:2] = jnp.zeros((2, D), f32)
    token_grads(0)
    token_grads(2)
    get_mp = load(4, mp_ref, wp)
    sums_low[...] = sums[0:16].astype(low)
    for k, partner in enumerate(around):
        near.append(remote(sums_low, sall.at[fr], near_send.at[1, k], near_recv.at[1, k], partner))
    sall[fr] = sums_low[...]
    every(middle, range(6, 12), 1)
    for copy in near[:7]:
        copy.wait_recv()
    get_mw.wait()
    get_mo.wait()
    get_mp.wait()
    def between():
        every(middle, range(6, 12), 2)

    vectors = message_back(
        at, cls_all, pre, normed, qkv, msg_mixed, vec, mw, wp, mo, gall, pick, mgrad, gcls, between)
    core_m = []

    def send_message(k):
        cols = pl.ds(3840 * k, 3840 - 3712 * k)
        core_m.append(remote(mgrad.at[1 - core, :, cols], mgot.at[:, cols], send_sem.at[12 + k, CORE],
                             recv_sem.at[12 + k, CORE], partners["c"]))

    def spread_message(k):
        core_m[k].wait_recv()
        cols = pl.ds(3840 * k, 3840 - 3712 * k)
        spread(12 + k, mgrad[core, :, cols] + mgot[:, cols])
        send_last(MESSAGE + k)

    send_message(0)
    every(middle, range(6, 12), 3)
    send_last(LATE_A)
    send_last(LATE_B)
    spread_message(0)
    for copy in near[7:]:
        copy.wait_recv()
    total = sall[0].astype(f32)
    for k in range(1, FRAMES):
        total = total + sall[k].astype(f32)
    message_vectors(total, vectors, pick, table, mgrad)
    send_message(1)
    finish(FEED_A)
    finish(FEED_S)
    spread_message(1)
    top = lax.broadcasted_iota(jnp.int32, (16, 1), 0) == 0
    for clip in range(CLIPS_HERE):
        tokens[clip, 0, pl.ds(0, 16)] = (heads[clip] + jnp.where(top, gcls[clip : clip + 1], 0.0)).astype(low)
    def sent(g):
        for p in range(1, 8):
            last_copy(g, p).wait_send()

    for key in registry:
        registry[key]().wait_send()
    for g in (FEED_A, FEED_S):
        sent(g)
    for copy in near:
        copy.wait_send()
    core_m[0].wait_send()
    for g in (LATE_A, LATE_B):
        finish(g)
        sent(g)
    for g in (MESSAGE, VECTOR):
        finish(g)
        sent(g)
    core_m[1].wait_send()


def back_and_sums(d_expand, d_shrink, after, proj, probs, frames, first_low, mixed, wp, wo, mw, mp, mo, vec, message, sums,
                  saved):
    vmem = pl.BlockSpec(memory_space=pltpu.VMEM)
    any_spec = pl.BlockSpec(memory_space=pl.ANY)
    S, V, SEM = jax.ShapeDtypeStruct, pltpu.VMEM, pltpu.SemaphoreType.DMA

    def phase_one(count, rows, cols, own=True):
        leads = [4 if own else 8, 4, 2, 1]
        return [V((count, lead, rows, cols), low) for lead in leads]

    scratch = [
        V((D, 3 * D), low), V((D, D), low), V((D, D), low), V((D, D), low), V((ALL, D), f32), V((ALL, 3 * D), low),
        V((2, 12, ROWS, ROWS), low), V((CLIPS_HERE, 1, PATCH, D), low), V((ALL, D), low), V((ALL, D), low),
        V((ROWS, D), f32), V((ALL, D), low), V((CLIPS_HERE, 16, D), f32), V((SUMS, D), f32), V((SLOT, D), f32), V((SLOT, D), f32),
        V((2, 48, 5 * D + 128), low), V((48, 5 * D + 128), low), V((FRAMES, SLOT, D), f32), V((16, D), low), V((FRAMES, 16, D), low),
        V((2, 128, 48), low), V((2, 128, 48), low), V((3, 384, 384), low), V((672, 1), jnp.int32), V((8, 24, 256), f32),
        *phase_one(3, 48, 1024), *phase_one(3, 192, 256), V((2, 8, 2, 48, 1536), low), V((6, 8, 48, 512), low), *phase_one(6, 48, 512, own=False),
        *[V((lead, rows, len(parts) * cols), low) for lead in (8, 7) for parts, rows, cols, _ in GROUPS],
        SEM((9,)), SEM((2,)), SEM((6,)), SEM((N_PARTS, 4)), SEM((N_PARTS, 4)), SEM((2, 7)), SEM((2, 7)), SEM((6, 7)), SEM((6, 7))]
    return pl.pallas_call(
        back_kernel,
        in_specs=[any_spec] * 13 + [vmem] * 9,
        out_specs=[vmem] * 4,
        out_shape=[S((CLIPS_HERE, 1, PATCH, D), low), S((13, 16, 512), f32), S((3, 32, 256), f32), S((16, 1920), f32)],
        scratch_shapes=scratch,
        compiler_params=pltpu.CompilerParams(collective_id=2, has_side_effects=True, vmem_limit_bytes=62 * 2**20),
        name="back_and_sums",
    )(d_expand, d_shrink, after, proj, probs, frames, first_low, mixed, wp, wo, mw, mp, mo,
      vec, message, sums, *saved, index_table())


def unpack_kernel(out, out_s, out_m, mw, mp, mo, ap, ao, ew, sw, *vectors):
    def piece(n, side, w):
        return out[n, 8 * side : 8 * side + 6, 0:w]

    message = (out_m[0:6], out_m[8:14])
    mw[...] = message[0][:, 0:D]
    mp[:, 0:1152] = message[0][:, D:1920]
    mp[:, 1152:2304] = message[1][:, 0:1152]
    mo[...] = message[1][:, 1152:1920]
    for k in range(3):
        for side in range(2):
            ap[:, 512 * k + 256 * side : 512 * k + 256 * side + 256] = piece(6 + 2 * k, side, 256)
            ew[:, 1024 * k + 512 * side : 1024 * k + 512 * side + 512] = piece(2 * k, side, 512)
            x = 512 * k + 256 * side
            target, x = (ap, x + 1536) if x < D else (ao, x - D)
            target[:, x : x + 256] = piece(7 + 2 * k, side, 256)
        sw[:, 256 * k : 256 * (k + 1)] = out_s[k, 0:24]
    lanes = lax.broadcasted_iota(jnp.int32, (6, 128), 1)
    rows = lax.broadcasted_iota(jnp.int32, (6, 128), 0)
    values = out[12, 0:6, 0:128]
    flat = jnp.zeros((128, 128), f32)
    for shift in range(4):
        place_at = (lanes == rows + 6 * shift).astype(f32)
        owner = jnp.where((lanes < 24) | (lanes >= 32), 0, jnp.where(lanes < 28, lanes - 24, (lanes - 28) & 1))
        part = jnp.where(owner == shift, values, 0.0)
        flat += lax.dot_general(part, place_at, (((0,), (0,)), ((), ())), precision=PRECISE, preferred_element_type=f32)
    for ref, (row, count) in zip(vectors, LANES):
        ref[...] = jnp.sum(flat[row : row + count], axis=0)[0 : 6 * count]


LANES = ((12, 1), (13, 1), (14, 1), (30, 2), (17, 1), (0, 1), (1, 1), (28, 2), (4, 1), (5, 1), (6, 1), (24, 4), (11, 1))


def unpack(out, out_s, out_m):
    S = jax.ShapeDtypeStruct
    vmem = pl.BlockSpec(memory_space=pltpu.VMEM)
    shapes = [(6, D), (6, 3 * D), (6, D), (6, 3 * D), (6, D), (6, FF), (24, D)] + [(6 * count,) for _, count in LANES]
    return pl.pallas_call(
        unpack_kernel,
        in_specs=[vmem] * 3,
        out_specs=[vmem] * len(shapes),
        out_shape=[S(shape, f32) for shape in shapes],
        compiler_params=pltpu.CompilerParams(vmem_limit_bytes=BIG),
        name="unpack",
    )(out, out_s, out_m)


def forward_kernel(*refs):
    vectors, refs = refs[: len(VECTORS)], refs[len(VECTORS) :]
    (gids, frames_ref, mw_ref, mp_ref, mo_ref, wp_ref, wo_ref, we_ref, ws_ref,
     vec, message, all_cls, pre_out, normed_out, qkv, msg_mixed,
     first_ref, proj_ref, probs_ref, mixed_ref, resid_ref, second_ref, hidden_ref, dgate_ref,
     result, loss, pooled_out, gpool,
     vw, vp, vo, wp, wo, we, ws, frames, cls, tops, first_low, proj, probs, mixed, resid, second_low, xs,
     hid, dg, acc, pool_all, every, natural, grads,
     load_sem, store_sem, probs_sem, send_sem, recv_sem, near_send, near_recv) = refs
    at = place()
    fr = lax.axis_index("frame")

    def load(n, src, dst):
        copy = pltpu.make_async_copy(src, dst, load_sem.at[n])
        copy.start()
        return copy

    def store(n, src, dst):
        copy = pltpu.make_async_copy(src, dst, store_sem.at[n])
        copy.start()
        return copy

    get_frames = load(0, frames_ref, frames)
    get_wp = [load(1 + j, wp_ref.at[:, pl.ds(j * D, D)], wp.at[j]) for j in range(3)]
    get_mw, get_mp, get_mo = load(4, mw_ref, vw), load(5, mp_ref, vp), load(6, mo_ref, vo)
    vec[...] = jnp.zeros((24, D), f32)
    for ref, rows in zip(vectors, VECTORS):
        for k, row in enumerate(rows):
            vec[row : row + 1] = ref[pl.ds(k * D, D)].astype(f32).reshape(1, D)
    cls[...] = jnp.zeros((SLOT, D), f32)
    around = frame_partners()
    order = ("c",) + CLIP_DIMS
    partner = {d: device_of(moved(at, {d: 1})) for d in order}
    greet(around + [partner[d] for d in order])
    get_frames.wait()
    for c in range(CLIPS_HERE):
        cls[c : c + 1] = frames[c, 0, 0:16].astype(f32)[0:1]
    first_near = [remote(cls, all_cls.at[fr], near_send.at[0, k], near_recv.at[0, k], p) for k, p in enumerate(around)]
    all_cls[fr] = cls[...]

    gain, shift = vec[R_FG : R_FG + 1], vec[R_FS : R_FS + 1]
    xs[pl.ds(192, 16)] = jnp.zeros((16, D), f32)
    for c in range(CLIPS_HERE):
        xs[pl.ds(0, PATCH)] = frames[c, 0].astype(f32)
        u, _ = stats(xs[...])
        first_low[pl.ds(c * ROWS, ROWS)] = (u * gain + shift).astype(low)
    for j in range(3):
        get_wp[j].wait()
        for part in range(2):
            rows = pl.ds(part * 2 * ROWS, 2 * ROWS)
            value = dot(first_low[rows], wp[j]) + vec[R_APB + j : R_APB + j + 1]
            proj[rows, j * D : (j + 1) * D] = value.astype(low)
    get_wo = load(7, wo_ref, wo)
    get_we = [load(8 + j, we_ref.at[:, pl.ds(j * D, D)], we.at[j]) for j in range(4)]
    get_ws = [load(12 + j, ws_ref.at[pl.ds(j * D, D)], ws.at[j]) for j in range(4)]

    get_mw.wait()
    for copy in first_near:
        copy.wait_recv()
    x = all_cls[...].reshape(MROWS, D).astype(low)
    pre = dot(x, vw[...]) + vec[R_MB : R_MB + 1]
    pre_out[...] = pre
    u, _ = stats(pre)
    normed = (u * vec[R_MG : R_MG + 1] + vec[R_MS : R_MS + 1]).astype(low)
    normed_out[...] = normed
    get_mp.wait()
    for j in range(3):
        qkv[:, j * D : (j + 1) * D] = (dot(normed, vp[:, j * D : (j + 1) * D]) + vec[R_MPB + j : R_MPB + j + 1]).astype(low)
    keep = same_clip()
    lane = lax.broadcasted_iota(jnp.int32, (MROWS, 128), 1)
    zero = jnp.zeros((), low)
    for pair in range(6):
        q = qkv[:, pair * 128 : pair * 128 + 128]
        k = qkv[:, D + pair * 128 : D + pair * 128 + 128]
        v = qkv[:, 2 * D + pair * 128 : 2 * D + pair * 128 + 128]
        outs = []
        for half in range(2):
            mine = (lane < 64) if half == 0 else (lane >= 64)
            s = jnp.where(keep, dot_t(jnp.where(mine, q, zero), k) * 0.125, -1e30)
            outs.append(dot(soft(s).astype(low), v))
        msg_mixed[:, pair * 128 : pair * 128 + 128] = jnp.where(lane < 64, outs[0], outs[1]).astype(low)
    get_mo.wait()
    branch = pre + dot(msg_mixed[...], vo[...]) + vec[R_MOB : R_MOB + 1]
    rows = lax.broadcasted_iota(jnp.int32, (MROWS, 1), 0) // SLOT
    message[...] = jnp.sum(jnp.where(rows == fr, branch, 0.0).reshape(FRAMES, SLOT, D), axis=0)

    u, _ = stats(message[...])
    ends = (u * gain + shift).astype(low)
    spot = lax.broadcasted_iota(jnp.int32, (16, 1), 0) == PATCH - 192
    for c in range(CLIPS_HERE):
        window = pl.ds(c * ROWS + 192, 16)
        row = ends[c : c + 1].astype(f32)
        first_low[window] = jnp.where(spot, row, first_low[window].astype(f32)).astype(low)
    for j in range(3):
        row = dot(ends, wp[j]) + vec[R_APB + j : R_APB + j + 1]
        for c in range(CLIPS_HERE):
            window = pl.ds(c * ROWS + 192, 16)
            old = proj[window, j * D : (j + 1) * D].astype(f32)
            proj[window, j * D : (j + 1) * D] = jnp.where(spot, row[c : c + 1], old).astype(low)
    stores = [store(0, first_low, first_ref), store(1, proj, proj_ref)]

    lane = lax.broadcasted_iota(jnp.int32, (ROWS, 128), 1)
    seen = lax.broadcasted_iota(jnp.int32, (ROWS, ROWS), 0) < PATCH + 1

    def probs_out(clip):
        return pltpu.make_async_copy(probs.at[clip % 2], probs_ref.at[clip], probs_sem.at[clip % 2])

    def one_clip(clip, carry):
        @pl.when(clip >= 2)
        def _():
            probs_out(clip - 2).wait()

        rows = pl.ds(pl.multiple_of(clip * ROWS, 16), ROWS)
        for pair in range(6):
            q, k, v = (proj[rows, n * D + pair * 128 : n * D + pair * 128 + 128] for n in range(3))
            total = 0.0
            for half in range(2):
                mine = (lane < 64) if half == 0 else (lane >= 64)
                s = dot_t(jnp.where(mine, k, zero), q) * 0.125
                s = jnp.where(seen, s, -1e30)
                e = jnp.exp(s - jnp.max(s, axis=0, keepdims=True))
                p = (e * (1.0 / jnp.sum(e, axis=0, keepdims=True))).astype(low)
                probs[clip % 2, 2 * pair + half] = p
                total = total + dot_tl(p, jnp.where(mine, v, zero))
            mixed[rows, pair * 128 : pair * 128 + 128] = total.astype(low)
        probs_out(clip).start()
        return carry

    lax.fori_loop(0, CLIPS_HERE, one_clip, 0)
    stores.append(store(2, mixed, mixed_ref))
    get_wo.wait()
    for part in range(2):
        branch = dot(mixed[pl.ds(part * 2 * ROWS, 2 * ROWS)], wo[...]) + vec[R_AOB : R_AOB + 1]
        for c in (2 * part, 2 * part + 1):
            xs[pl.ds(192, 16)] = jnp.zeros((16, D), f32)
            xs[pl.ds(0, PATCH)] = frames[c, 0].astype(f32)
            after = xs[...] + branch[(c - 2 * part) * ROWS : (c - 2 * part + 1) * ROWS]
            rows = pl.ds(c * ROWS, ROWS)
            resid[rows] = after
            u2, _ = stats(after)
            second_low[rows] = (u2 * vec[R_SG : R_SG + 1] + vec[R_SS : R_SS + 1]).astype(low)
    stores += [store(3, resid, resid_ref), store(4, second_low, second_ref)]

    def gate(h):
        sg = 1.0 / (1.0 + jnp.exp(-1.702 * h))
        hs = h * sg
        return sg, hs

    heads = jnp.concatenate([second_low[pl.ds(c * ROWS, 16)] for c in range(CLIPS_HERE)], axis=0)
    total = jnp.zeros((16 * CLIPS_HERE, D), f32)
    for j in range(4):
        get_we[j].wait()
        _, hs = gate(dot(heads, we[j]) + vec[R_EB + j : R_EB + j + 1])
        get_ws[j].wait()
        total += dot(hs.astype(low), ws[j])
    tops[...] = jnp.zeros((SLOT, D), f32)
    for c in range(CLIPS_HERE):
        tops[c : c + 1] = resid[c * ROWS : c * ROWS + 1] + vec[R_SB : R_SB + 1] + total[16 * c : 16 * c + 1]
    near = [remote(tops, pool_all.at[fr], near_send.at[1, k], near_recv.at[1, k], p) for k, p in enumerate(around)]
    pool_all[fr] = tops[...]

    copies, state = [], {}

    def exchange(k):
        copy = remote(every.at[pl.ds(0, 2**k)], every.at[pl.ds(2**k, 2**k)], send_sem.at[k], recv_sem.at[k],
                      partner[order[k]])
        copies.append(copy)

    def step(k):
        if k == 0:
            for copy in near:
                copy.wait_recv()
            s = pool_all[0]
            for f in range(1, FRAMES):
                s = s + pool_all[f]
            pooled = s * 0.125
            pooled_out[...] = pooled[:CLIPS_HERE]
            inv_len = lax.rsqrt(jnp.sum(pooled * pooled, axis=-1, keepdims=True) + 1e-06)
            state.update(pooled=pooled, inv_len=inv_len)
            every[0] = pooled * inv_len
        else:
            copies[k - 1].wait_recv()
        if k < 4:
            exchange(k)

    tile_stores = []
    for j in range(4):
        if j >= 2:
            for copy in tile_stores[2 * (j - 2) : 2 * (j - 1)]:
                copy.wait()
        for part in range(2):
            rows = pl.ds(part * 2 * ROWS, 2 * ROWS)
            h = dot(second_low[rows], we[j]) + vec[R_EB + j : R_EB + j + 1]
            sg, hs = gate(h)
            hidden = hs.astype(low)
            hid[j % 2, rows] = hidden
            dg[j % 2, rows] = (sg + 1.702 * hs * (1.0 - sg)).astype(low)
            out = dot(hidden, ws[j])
            acc[rows] = (resid[rows] + vec[R_SB : R_SB + 1] if j == 0 else acc[rows]) + out
            k = 2 * j + part - 2
            if 0 <= k <= 4:
                step(k)
        for n, (src, dst) in enumerate(((hid, hidden_ref), (dg, dgate_ref))):
            copy = pltpu.make_async_copy(src.at[j % 2], dst.at[:, pl.ds(j * D, D)], store_sem.at[5 + 4 * n + j])
            copy.start()
            tile_stores.append(copy)
    for c in range(CLIPS_HERE):
        result[c, 0] = acc[pl.ds(c * ROWS, PATCH)].astype(low)
    for p in range(16):
        to = moved(at, {d: (p >> k) & 1 for k, d in enumerate(order)})
        natural[dp_of(to)] = every[p]
    n = natural[...].reshape(128, D)
    sims = 50.0 * lax.dot_general(n, n, (((1,), (1,)), ((), ())), precision=PRECISE, preferred_element_type=f32)
    rows = lax.broadcasted_iota(jnp.int32, (128, 128), 0)
    cols = lax.broadcasted_iota(jnp.int32, (128, 128), 1)
    here = (cols & 7) < CLIPS_HERE
    other = here & (rows != cols)
    slot = lax.broadcasted_iota(jnp.int32, (128, 64), 0)
    clip = lax.broadcasted_iota(jnp.int32, (128, 64), 1)
    spot = (((slot >> 3) * CLIPS_HERE + (slot & 7)) == clip) & ((slot & 7) < CLIPS_HERE)
    wide = jnp.broadcast_to(gids[...].astype(f32), (128, 64))
    mine = jnp.where(spot, wide, 0.0)
    gid_col = jnp.sum(mine, axis=-1, keepdims=True)
    gid_row = lax.dot_general(wide, spot.astype(f32), (((1,), (1,)), ((), ())), precision=PRECISE, preferred_element_type=f32)
    same = other & (gid_col == gid_row)
    valid = (lax.broadcasted_iota(jnp.int32, (128, 1), 0) & 7) < CLIPS_HERE

    def log_soft(logits):
        top = jnp.max(logits, axis=-1, keepdims=True)
        e = jnp.exp(logits - top)
        total = jnp.sum(e, axis=-1, keepdims=True)
        return top + jnp.log(total), e / total

    all_log, all_p = log_soft(jnp.where(other, sims, -1e30))
    pos_log, pos_p = log_soft(jnp.where(same, sims, -1e30))
    terms = jnp.where(valid, all_log - pos_log, 0.0)
    loss[...] = jnp.sum(terms, axis=0, keepdims=True) * (1.0 / 64.0)
    gs = jnp.where(valid & here, all_p - pos_p, 0.0)
    grad_all = 50.0 * jnp.dot(gs + gs.T, n, precision=PRECISE, preferred_element_type=f32)
    grads[...] = grad_all.reshape(16, SLOT, D)
    g = grads[lax.axis_index("dp")]
    pooled, inv_len = state["pooled"], state["inv_len"]
    back = inv_len * g - inv_len * inv_len * inv_len * pooled * jnp.sum(pooled * g, axis=-1, keepdims=True)
    gpool[...] = back * 0.125
    for copy in tile_stores[4:] + stores:
        copy.wait()
    for clip in (CLIPS_HERE - 2, CLIPS_HERE - 1):
        probs_out(clip).wait()
    for copy in first_near + near + copies:
        copy.wait_send()


def forward(vectors, gids, frames, mw, mp, mo, wp, wo, we, ws):
    vmem = pl.BlockSpec(memory_space=pltpu.VMEM)
    any_spec = pl.BlockSpec(memory_space=pl.ANY)
    S, V, SEM = jax.ShapeDtypeStruct, pltpu.VMEM, pltpu.SemaphoreType.DMA
    return pl.pallas_call(
        forward_kernel,
        in_specs=[vmem] * (len(VECTORS) + 1) + [any_spec] * 8,
        out_specs=[vmem] * 7 + [any_spec] * 8 + [vmem] * 4,
        out_shape=[
            S((24, D), f32), S((SLOT, D), f32), S((FRAMES, SLOT, D), f32), S((MROWS, D), f32), S((MROWS, D), low),
            S((MROWS, 3 * D), low), S((MROWS, D), low),
            S((ALL, D), low), S((ALL, 3 * D), low), S((CLIPS_HERE, 12, ROWS, ROWS), low), S((ALL, D), low), S((ALL, D), f32),
            S((ALL, D), low), S((ALL, FF), low), S((ALL, FF), low),
            S((CLIPS_HERE, 1, PATCH, D), low), S((1, 1), f32), S((CLIPS_HERE, D), f32), S((SLOT, D), f32)],
        scratch_shapes=[
            V((D, D), low), V((D, 3 * D), low), V((D, D), low), V((3, D, D), low), V((D, D), low), V((4, D, D), low),
            V((4, D, D), low), V((CLIPS_HERE, 1, PATCH, D), low), V((SLOT, D), f32), V((SLOT, D), f32), V((ALL, D), low),
            V((ALL, 3 * D), low), V((2, 12, ROWS, ROWS), low), V((ALL, D), low), V((ALL, D), f32), V((ALL, D), low),
            V((ROWS, D), f32), V((2, ALL, D), low), V((2, ALL, D), low), V((ALL, D), f32), V((FRAMES, SLOT, D), f32),
            V((16, SLOT, D), f32), V((16, SLOT, D), f32), V((16, SLOT, D), f32),
            SEM((16,)), SEM((13,)), SEM((2,)), SEM((4,)), SEM((4,)), SEM((2, 7)), SEM((2, 7))],
        compiler_params=pltpu.CompilerParams(collective_id=0, has_side_effects=True, vmem_limit_bytes=62 * 2**20),
        name="forward",
    )(*vectors, gids, frames, mw, mp, mo, wp, wo, we, ws)


def on_device(
    frames, cotangent, group_ids, message_weight, message_bias, message_gain, message_shift, message_project,
    message_project_bias, message_output, message_output_bias, first_gain, first_shift, attend_project,
    attend_project_bias, attend_output, attend_output_bias, second_gain, second_shift, expand_weight, expand_bias,
    shrink_weight, shrink_bias,
):
    vectors = (
        message_bias, message_gain, message_shift, message_project_bias, message_output_bias, first_gain, first_shift,
        attend_project_bias, attend_output_bias, second_gain, second_shift, expand_bias, shrink_bias,
    )
    (vec, message, *saved, first_low, proj, probs, mixed, resid, second_low, hidden, dgate, result, loss, pooled,
     gpool) = forward(
        vectors, group_ids.reshape(1, 64), frames, message_weight, message_project, message_output, attend_project,
        attend_output, expand_weight, shrink_weight)
    d_expand, d_shrink, after, sums = mlp_back(
        cotangent, gpool, vec, hidden, dgate, second_low, expand_weight, shrink_weight, resid)
    delta_frames, out, out_s, out_m = back_and_sums(
        d_expand, d_shrink, after, proj, probs, frames, first_low, mixed, attend_project, attend_output, message_weight,
        message_project, message_output, vec, message, sums, saved)
    mw, mp, mo, ap, ao, ew, sw, mb, mg, ms, mpb, mob, fg, fs, apb, aob, sg, ss, eb, sb = unpack(out, out_s, out_m)
    return (
        result, loss.reshape(()), pooled, delta_frames, mw, mb, mg, ms, mp, mpb, mo, mob, fg, fs, ap, apb, ao, aob, sg, ss,
        ew, eb, sw, sb,
    )


def solution(mesh):
    placed = (
        P("dp", "frame", None, None),
        P("dp", "frame", None, None),
        P(),
        P(),
        P(),
        P(),
        P(),
        P(),
        P(),
        P(),
        P(),
        P(),
        P(),
        P(),
        P(),
        P(),
        P(),
        P(),
        P(),
        P(),
        P(),
        P(),
        P(),
    )
    return jax.shard_map(
        on_device,
        mesh=mesh,
        in_specs=placed,
        out_specs=(
            P("dp", "frame", None, None),
            P(),
            P("dp", None),
            P("dp", "frame", None, None),
            P(("dp", "frame"), None),
            P(("dp", "frame")),
            P(("dp", "frame")),
            P(("dp", "frame")),
            P(("dp", "frame"), None),
            P(("dp", "frame")),
            P(("dp", "frame"), None),
            P(("dp", "frame")),
            P(("dp", "frame")),
            P(("dp", "frame")),
            P(("dp", "frame"), None),
            P(("dp", "frame")),
            P(("dp", "frame"), None),
            P(("dp", "frame")),
            P(("dp", "frame")),
            P(("dp", "frame")),
            P(("dp", "frame"), None),
            P(("dp", "frame")),
            P(("dp", "frame"), None),
            P(("dp", "frame")),
        ),
        check_vma=False,
    )
```

```python
import functools

import jax
import jax.numpy as jnp
import numpy as np
from jax import lax
from jax.experimental import pallas as pl
from jax.experimental.pallas import tpu as pltpu
from jax.sharding import PartitionSpec as P

f32, low = jnp.float32, jnp.bfloat16
CLIPS_HERE, PATCH, ROWS, D, FF = 4, 197, 208, 768, 3072
ALL = CLIPS_HERE * ROWS
BIG = 58 * 2**20
(R_MB, R_MG, R_MS, R_MPB, R_MOB, R_FG, R_FS, R_APB, R_AOB, R_SG, R_SS, R_EB, R_SB) = (
    0, 1, 2, 3, 6, 7, 8, 9, 12, 13, 14, 15, 19)


def dot(a, b):
    return jnp.dot(a, b, preferred_element_type=f32)


def dot_t(a, b):
    return lax.dot_general(a, b, (((1,), (1,)), ((), ())), preferred_element_type=f32)


def dot_tl(a, b):
    return lax.dot_general(a, b, (((0,), (0,)), ((), ())), preferred_element_type=f32)


def stats(x):
    mean = jnp.mean(x, axis=-1, keepdims=True)
    centered = x - mean
    inv = lax.rsqrt(jnp.mean(centered * centered, axis=-1, keepdims=True) + 1e-05)
    return centered * inv, inv


def norm_back(grad, u, inv, gain):
    h = grad * gain
    return (h - jnp.mean(h, axis=-1, keepdims=True) - u * jnp.mean(h * u, axis=-1, keepdims=True)) * inv


def const(shape):
    return pl.BlockSpec(shape, lambda *i: (0,) * len(shape))


MESH = pl.DeviceIdType.MESH


def flip_low(index):
    return index + 1 - 2 * (index % 2)


def flip_pair(index, high, low):
    index = 3 - index if high else index
    return flip_low(index) if low else index


def place():
    dp, fr = lax.axis_index("dp"), lax.axis_index("frame")
    return dict(y=dp // 4, x=(dp // 2 % 2) * 2 + fr // 4, z=fr % 4, c=dp % 2)


def moved(at, bits):
    return dict(
        y=flip_pair(at["y"], bits.get("yu"), bits.get("yv")),
        x=flip_pair(at["x"], bits.get("xu"), bits.get("xv")),
        z=flip_pair(at["z"], bits.get("zu"), bits.get("zv")),
        c=1 - at["c"] if bits.get("c") else at["c"],
    )


def dp_of(at):
    return at["y"] * 4 + (at["x"] // 2) * 2 + at["c"]


def frame_of(at):
    return (at["x"] % 2) * 4 + at["z"]


def device_of(at):
    return (dp_of(at), frame_of(at))


CLIP_DIMS = ("yu", "yv", "xu")
FRAME_DIMS = ("xv", "zu", "zv")


def rotated(dims, turn):
    return dims[turn:] + dims[:turn]


def bits_at(dims, position):
    return {dims[k]: (position >> (2 - k)) & 1 for k in range(3)}


def to_units(full):
    return full.reshape(8, 2, 48, full.shape[-1])


FRAMES = 8
SLOT = 8
MROWS = FRAMES * SLOT
SUMS = 24


def hail(partners):
    barrier = pltpu.get_barrier_semaphore()
    for partner in partners:
        pl.semaphore_signal(barrier, inc=1, device_id=partner, device_id_type=MESH)


def meet(partners):
    pl.semaphore_wait(pltpu.get_barrier_semaphore(), len(partners))


def greet(partners):
    hail(partners)
    meet(partners)


def frame_partners():
    dp, fr = lax.axis_index("dp"), lax.axis_index("frame")
    return [(dp, lax.rem(fr + k, FRAMES)) for k in range(1, FRAMES)]


def remote(src, dst, send_sem, recv_sem, device):
    copy = pltpu.make_async_remote_copy(
        src_ref=src, dst_ref=dst, send_sem=send_sem, recv_sem=recv_sem, device_id=device, device_id_type=MESH)
    copy.start()
    return copy


def same_clip():
    rows = lax.broadcasted_iota(jnp.int32, (MROWS, MROWS), 0)
    cols = lax.broadcasted_iota(jnp.int32, (MROWS, MROWS), 1)
    return rows % SLOT == cols % SLOT


def soft(s):
    e = jnp.exp(s - jnp.max(s, axis=-1, keepdims=True))
    return e / jnp.sum(e, axis=-1, keepdims=True)


VECTORS = ((R_MB,), (R_MG,), (R_MS,), (R_MPB, R_MPB + 2), (R_MOB,), (R_FG,), (R_FS,), (R_APB, R_APB + 2), (R_AOB,), (R_SG,),
           (R_SS,), (R_EB, R_EB + 1, R_EB + 2, R_EB + 3), (R_SB,))


PRECISE = lax.Precision.HIGHEST


def message_back(at, cls_all, pre, normed, qkv, mixed, vec, vw, vp, vo, gall, pick, mgrad, gcls, between):
    fr = lax.axis_index("frame")
    g = gall[...].reshape(MROWS, D)
    g_low = g.astype(low)
    gmm = dot_t(g_low, vo[...]).astype(low)
    keep = same_clip()
    lane = lax.broadcasted_iota(jnp.int32, (MROWS, 128), 1)
    zero = jnp.zeros((), low)
    parts = ([], [], [])
    for pair in range(6):
        q = qkv[:, pair * 128 : pair * 128 + 128]
        k = qkv[:, D + pair * 128 : D + pair * 128 + 128]
        v = qkv[:, 2 * D + pair * 128 : 2 * D + pair * 128 + 128]
        gm = gmm[:, pair * 128 : pair * 128 + 128]
        totals = [0.0, 0.0, 0.0]
        for half in range(2):
            mine = (lane < 64) if half == 0 else (lane >= 64)
            q_here, k_here, gm_here = (jnp.where(mine, value, zero) for value in (q, k, gm))
            s = jnp.where(keep, dot_t(k_here, q) * 0.125, -1e30)
            e = jnp.exp(s - jnp.max(s, axis=0, keepdims=True))
            p = e / jnp.sum(e, axis=0, keepdims=True)
            dp = dot_t(v, gm_here)
            gs = (p * (dp - jnp.sum(dp * p, axis=0, keepdims=True))).astype(low)
            products = (dot_tl(gs, k_here), dot(gs, q_here), dot(p.astype(low), gm_here))
            totals = [total + product for total, product in zip(totals, products)]
        for n, scale in ((0, 0.125), (1, 0.125), (2, 1.0)):
            parts[n].append((totals[n] * scale).astype(low))
    gq, gk, gv = (jnp.concatenate(part, axis=1) for part in parts)
    between()
    gnorm = dot_t(gq, vp[:, :D]) + dot_t(gk, vp[:, D : 2 * D]) + dot_t(gv, vp[:, 2 * D :])
    u, inv = stats(pre[...])
    gpre = (g + norm_back(gnorm, u, inv, vec[R_MG : R_MG + 1])).astype(low)

    def total(value):
        return jnp.sum(value.astype(f32), axis=0, keepdims=True)

    mine = (lax.broadcasted_iota(jnp.int32, (96, D), 1) == pick[0:96]).astype(low)
    x = cls_all[...].reshape(MROWS, D).astype(low)
    for unit, (left, right) in enumerate(((x, gpre), (normed[...], gq), (normed[...], gk), (normed[...], gv),
                                          (mixed[...], g_low))):
        turned = dot_t(mine, left).astype(low)
        mgrad[:, :, unit * D : (unit + 1) * D] = dot(turned, right).astype(low).reshape(2, 48, D)
    back = dot_t(gpre, vw[...])
    rows = lax.broadcasted_iota(jnp.int32, (MROWS, 1), 0) // SLOT
    gcls[...] = jnp.sum(jnp.where(rows == fr, back, 0.0).reshape(FRAMES, SLOT, D), axis=0)
    return [total(gpre), total(gnorm * u), total(gnorm), total(gq), total(gv), total(g_low)]


def message_vectors(sums, message_sums, pick, part, mgrad):
    table = jnp.concatenate([sums[0:12], *message_sums, jnp.zeros((SUMS - 18, D), f32)], axis=0).astype(low)
    choose = (lax.broadcasted_iota(jnp.int32, (672, D), 1) == pick[...]).astype(low)
    z = dot_t(choose, table)
    wide = lax.broadcasted_iota(jnp.int32, (96, 128), 1)
    narrow = lax.broadcasted_iota(jnp.int32, (96, SUMS), 1)
    out = jnp.zeros((96, 128), f32)
    out += jnp.concatenate([z[:96], jnp.zeros((96, 128 - SUMS), f32)], axis=1)
    for q in range(4):
        hit = narrow == 7 + part[384:480, 3:4]
        value = jnp.sum(jnp.where(hit, z[96 * (1 + q) : 96 * (2 + q)], 0.0), axis=-1, keepdims=True)
        out = jnp.where(wide == 24 + q, value, out)
    for q in range(2):
        for n, first in enumerate((2, 15)):
            hit = narrow == first + part[384:480, 4:5]
            value = jnp.sum(jnp.where(hit, z[96 * (5 + q) : 96 * (6 + q)], 0.0), axis=-1, keepdims=True)
            out = jnp.where(wide == 28 + 2 * n + q, value, out)
    mgrad[:, :, 5 * D : 5 * D + 128] = out.astype(low).reshape(2, 48, 128)


def index_table():
    table = np.zeros((384 + 672, 8), np.int32)
    r = np.arange(384)
    table[:384, 0] = r // 48
    table[:384, 1] = r % 48 // 6 * 48 + r % 6
    table[:384, 2] = r % 48 // 6 % 2
    r = np.arange(96)
    c, y, xh, i = r // 48, r % 48 // 12, r % 12 // 6, r % 6
    high = y * 4 + xh * 2 + c
    picks = [(high * 48 + i, 6)]
    picks += [(high % 4 * 192 + q * 6 + i, 24) for q in range(4)]
    picks += [(high % 8 * 96 + q * 6 + i, 12) for q in range(2)]
    for n, (base, step) in enumerate(picks):
        rows = slice(384 + 96 * n, 384 + 96 * (n + 1))
        table[rows, 0], table[rows, 1], table[rows, 2] = base, step, xh
        table[rows, 3], table[rows, 4] = y, y // 2
    return jnp.asarray(table)


def fill_orders(at, table, sa, sb, mix, pick):
    xh, xl = at["x"] // 2, at["x"] % 2
    rows = lax.broadcasted_iota(jnp.int32, (128, 48), 0)
    cols = lax.broadcasted_iota(jnp.int32, (128, 48), 1)
    for ref, dims in ((sa, FRAME_DIMS), (sb, CLIP_DIMS)):
        block = jnp.zeros((128, 48), jnp.int32)
        for p in range(8):
            to = moved(at, bits_at(dims, p))
            value = frame_of(to) if dims == FRAME_DIMS else dp_of(to) // 2
            block = jnp.where((rows >> 4) == p, value, block)
        for half in range(2):
            inner = (rows & 15) - 8 * half
            hit = (cols == block * 6 + inner) & (inner >= 0) & (inner < 6)
            ref[half] = hit.astype(f32).astype(low)
    lanes = lax.broadcasted_iota(jnp.int32, (384, 384), 1)
    p_col, base, same = table[0:384, 0:1], table[0:384, 1:2], table[0:384, 2:3] == xh
    for turn in range(3):
        frame = jnp.zeros((384, 1), jnp.int32)
        for p in range(8):
            to = moved(at, bits_at(rotated(FRAME_DIMS, turn), p))
            side = to["x"] % 2
            frame = jnp.where(p_col == p, jnp.where(same, 4 * side + to["z"], 4 * (1 - side) + to["z"]), frame)
        mix[turn] = (lanes == base + 6 * frame).astype(f32).astype(low)
    base, step, same = table[384:, 0:1], table[384:, 1:2], table[384:, 2:3] == xh
    pick[...] = base + step * jnp.where(same, 4 * xl + at["z"], 4 * (1 - xl) + at["z"])


CORE, S1, S2, S3 = range(4)
KEEP = (4, 2, 1)
KIND = ("a", "s") * 3 + ("a", "b") * 3 + ("m",) * 2
TURN = (0, 0, 1, 1, 2, 2) * 2
N_PARTS = 14


GROUPS = (
    ((0, 2, 4), 16, 512, FRAME_DIMS), ((1, 3, 5), 32, 256, CLIP_DIMS), ((6, 8, 10), 16, 256, FRAME_DIMS),
    ((7, 9, 11), 16, 256, CLIP_DIMS), ((12,), 16, 1920, CLIP_DIMS), ((13,), 16, 128, CLIP_DIMS),
)
FEED_A, FEED_S, LATE_A, LATE_B, MESSAGE, VECTOR = range(6)


def order_of(n):
    return rotated(CLIP_DIMS if KIND[n] == "a" else FRAME_DIMS, TURN[n])


def mlp_back_kernel(cot, gpool, vec, hidden, dgate, second_low, we, ws, resid,
                    out_e, out_s, after, sums, gl, gb, gsec, tile_e, tile_s, got_e, got_s, put_e, put_s, wide,
                    send_sem, recv_sem, store_sem):
    j = pl.program_id(0)
    at = place()
    core = at["c"]
    other = device_of(moved(at, {"c": 1}))

    def pair_copies(n):
        return [pltpu.make_async_remote_copy(
            src_ref=tile.at[n % 2, :, 1 - core], dst_ref=got.at[n], send_sem=send_sem.at[k, n], recv_sem=recv_sem.at[k, n],
            device_id=other, device_id_type=MESH) for k, (tile, got) in enumerate(((tile_e, got_e), (tile_s, got_s)))]

    def puts(n):
        return [pltpu.make_async_copy(put_e.at[n % 2], out_e.at[:, :, pl.ds(n * D, D)], store_sem.at[0, n]),
                pltpu.make_async_copy(put_s.at[n % 2], out_s.at[:, pl.ds(48 * n, 48)], store_sem.at[1, n])]

    def fold(n):
        if n >= 2:
            for copy in puts(n - 2):
                copy.wait()
        for copy in pair_copies(n):
            copy.wait_recv()
        for k in range(3):
            first, stop = max(1024 * k, D * n) - D * n, min(1024 * (k + 1), D * (n + 1)) - D * n
            if first < stop:
                for p in range(8):
                    chunk = dp_of(moved(at, bits_at(order_of(2 * k), p))) // 2
                    put_e[n % 2, p, :, first:stop] = (
                        tile_e[n % 2, chunk, core, :, first:stop] + got_e[n, chunk, :, first:stop])
        for xh in range(2):
            wide[xh] = (tile_s[n % 2, xh, core] + got_s[n, xh]).astype(f32).reshape(8, 24, D)
        for k in range(3):
            cols = pl.ds(256 * k, 256)
            for p in range(8):
                to = moved(at, bits_at(order_of(2 * k + 1), p))
                rows = []
                for xh in range(2):
                    side = lax.rem(to["x"] % 2 + at["x"] // 2 + xh, 2)
                    rows.append(wide[xh, side * 4 + to["z"], :, cols])
                put_s[n % 2, p, :, cols] = jnp.concatenate(rows, axis=0).astype(low)
        for copy in puts(n):
            copy.start()

    @pl.when(j == 0)
    def _():
        hail([other])
        gl[...] = jnp.zeros((ALL, D), f32)
        for c in range(CLIPS_HERE):
            gl[pl.ds(c * ROWS, PATCH)] = cot[c, 0].astype(f32)
            gl[pl.ds(c * ROWS, 1)] += gpool[pl.ds(c, 1)]
        gb[...] = gl[...].astype(low)
        gsec[...] = jnp.zeros((ALL, D), f32)
        sums[...] = jnp.zeros((24, D), f32)
        sums[11:12] = jnp.sum(gb[...].astype(f32), axis=0, keepdims=True)
        meet([other])

    for n in (2, 3):
        @pl.when(j == n)
        def _(n=n):
            for copy in pair_copies(n - 2):
                copy.wait_send()

    tile_s[j % 2] = dot_tl(hidden[...], gb[...]).astype(low).reshape(2, 2, 192, D)
    ghp = (dot_t(gb[...], ws[...]) * dgate[...].astype(f32)).astype(low)
    sums[pl.ds(7 + j, 1)] = jnp.sum(ghp.astype(f32), axis=0, keepdims=True)
    tile_e[j % 2] = dot_tl(second_low[...], ghp).astype(low).reshape(8, 2, 48, D)
    for n in range(4):
        @pl.when(j == n)
        def _(n=n):
            for copy in pair_copies(n):
                copy.start()

    gsec[...] += dot_t(ghp, we[...])
    for n in range(3):
        @pl.when(j == n + 1)
        def _(n=n):
            fold(n)

    @pl.when(j == 3)
    def _():
        gain = vec[R_SG : R_SG + 1]
        total = [jnp.zeros((1, D), f32) for _ in range(3)]
        for c in range(CLIPS_HERE):
            rows = pl.ds(c * ROWS, ROWS)
            u, inv = stats(resid[rows])
            g = gsec[rows]
            out = gl[rows] + norm_back(g, u, inv, gain)
            after[rows] = out
            total[0] += jnp.sum(g * u, axis=0, keepdims=True)
            total[1] += jnp.sum(g, axis=0, keepdims=True)
            total[2] += jnp.sum(out.astype(low).astype(f32), axis=0, keepdims=True)
        sums[5:6] = total[0]
        sums[6:7] = total[1]
        sums[4:5] = total[2]
        fold(3)
        for n in (2, 3):
            for copy in pair_copies(n):
                copy.wait_send()
            for copy in puts(n):
                copy.wait()


def mlp_back(cot, gpool, vec, hidden, dgate, second_low, we, ws, resid):
    tile = pl.BlockSpec((ALL, D), lambda j: (0, j))
    any_spec = pl.BlockSpec(memory_space=pl.ANY)
    S, V, SEM = jax.ShapeDtypeStruct, pltpu.VMEM, pltpu.SemaphoreType.DMA
    return pl.pallas_call(
        mlp_back_kernel,
        grid=(4,),
        in_specs=[const((CLIPS_HERE, 1, PATCH, D)), const((8, D)), const((24, D)), tile, tile, const((ALL, D)),
                  pl.BlockSpec((D, D), lambda j: (0, j)), pl.BlockSpec((D, D), lambda j: (j, 0)), const((ALL, D))],
        out_specs=[any_spec, any_spec, const((ALL, D)), const((24, D))],
        out_shape=[S((8, 48, FF), low), S((8, 192, D), low), S((ALL, D), f32), S((24, D), f32)],
        scratch_shapes=[V((ALL, D), f32), V((ALL, D), low), V((ALL, D), f32), V((2, 8, 2, 48, D), low),
                        V((2, 2, 2, 192, D), low), V((4, 8, 48, D), low), V((4, 2, 192, D), low), V((2, 8, 48, D), low),
                        V((2, 8, 48, D), low), V((2, 8, 24, D), f32), SEM((2, 4)), SEM((2, 4)), SEM((2, 4))],
        compiler_params=pltpu.CompilerParams(collective_id=1, has_side_effects=True, vmem_limit_bytes=BIG),
        name="mlp_back",
    )(cot, gpool, vec, hidden, dgate, second_low, we, ws, resid)


def back_kernel(
    e_ref, s_ref, after_ref, proj_ref, probs_ref, frames_ref, first_ref, mixed_ref, wp_ref, wo_ref, mw_ref, mp_ref, mo_ref,
    vec, message, sums_in, cls_all, pre, normed, qkv, msg_mixed, table,
    tokens, out, out_s, out_m,
    wp, wo, mw, mo, after, proj, probs, frames, first_low, mixed, xs, gm_all, heads, sums, gmsg, gcls, mgrad, mgot,
    gall, sums_low, sall, sa, sb, mix, pick, wide_s,
    own_a, ra1, ra2, ra3, own_s, rs1, rs2, rs3, late, acc_l, got_l, rl1, rl2, rl3,
    t0, t1, t2, t3, t4, t5, v0, v1, v2, v3, v4, v5,
    load_sem, probs_sem, local_sem, send_sem, recv_sem, near_send, near_recv, last_send, last_recv,
):
    at = place()
    fr = lax.axis_index("frame")
    core = at["c"]
    around = frame_partners()
    partners = {d: device_of(moved(at, {d: 1})) for d in ("c",) + CLIP_DIMS + FRAME_DIMS}

    def load(n, src, dst):
        copy = pltpu.make_async_copy(src, dst, load_sem.at[n])
        copy.start()
        return copy

    def probs_copy(clip):
        return pltpu.make_async_copy(probs_ref.at[clip], probs.at[clip % 2], probs_sem.at[clip % 2])

    probs_copy(0).start()
    get_wo, get_after, get_proj = load(0, wo_ref, wo), load(1, after_ref, after), load(2, proj_ref, proj)
    clip_cube = [device_of(moved(at, bits_at(CLIP_DIMS, p))) for p in range(1, 8)]
    hail(around + clip_cube + [partners["c"]])
    fill_orders(at, table, sa, sb, mix, pick)
    meet(around + clip_cube + [partners["c"]])

    def mine(n, lead):
        if n < 6:
            return (own_a if n % 2 == 0 else own_s).at[n // 2, lead]
        return acc_l.at[n - 6, lead]

    def got(n):
        return got_l.at[n - 6]

    def half(n, s):
        if n < 6:
            return ((ra1, ra2, ra3) if n % 2 == 0 else (rs1, rs2, rs3))[s - 1].at[n // 2]
        return (rl1, rl2, rl3)[s - 1].at[n - 6]

    kept_blocks, sent_blocks = (t0, t1, t2, t3, t4, t5), (v0, v1, v2, v3, v4, v5)

    def group_of(n):
        return next((g, group[0].index(n), group) for g, group in enumerate(GROUPS) if n in group[0])

    def chunk_at(n, p):
        return dp_of(moved(at, bits_at(order_of(n), p))) // 2

    def source(n, which):
        if n < 6:
            step = 1024 if n % 2 == 0 else 256
            return (e_ref if n % 2 == 0 else s_ref).at[pl.ds(4 * which, 4), :, pl.ds(n // 2 * step, step)]
        return late.at[n % 2, :, which, :, pl.ds((n - 6) // 2 * 512, 512)]

    def local(n):
        return pltpu.make_async_copy(source(n, 0), mine(n, pl.ds(0, 4)), local_sem.at[n])

    registry = {}

    def define(n, step, src, dst, dim):
        def make():
            return pltpu.make_async_remote_copy(
                src_ref=src(), dst_ref=dst(), send_sem=send_sem.at[n, step], recv_sem=recv_sem.at[n, step],
                device_id=partners[dim], device_id_type=MESH)
        registry[n, step] = make

    def define_part(n):
        if KIND[n] == "m":
            return
        if n >= 6:
            define(n, CORE, lambda: source(n, 1 - core), lambda: got(n), "c")
        for s, first in ((1, S1), (2, S2), (3, S3)):
            keep, dim = KEEP[s - 1], order_of(n)[s - 1]
            if s == 1 and n < 6:
                define(n, first, lambda: source(n, 1), lambda: half(n, 1), dim)
            else:
                define(n, first, lambda keep=keep: mine(n, pl.ds(keep, keep)), lambda s=s: half(n, s), dim)

    def last_copy(g, p):
        return pltpu.make_async_remote_copy(
            src_ref=kept_blocks[g].at[p], dst_ref=sent_blocks[g].at[p - 1], send_sem=last_send.at[g, p - 1],
            recv_sem=last_recv.at[g, p - 1], device_id=device_of(moved(at, bits_at(GROUPS[g][3], p))),
            device_id_type=MESH)

    for n in range(N_PARTS):
        define_part(n)

    def start(n, step):
        registry[n, step]().start()

    def arrived(n, step):
        registry[n, step]().wait_recv()

    for n in range(6):
        start(n, S1)
    sums[...] = sums_in[...]
    gmsg[...] = jnp.zeros((SLOT, D), f32)

    def begin(n):
        arrived(n, CORE)
        own = source(n, core)
        if KIND[n] == "a":
            for p in range(8):
                chunk = chunk_at(n, p)
                mine(n, p)[...] = own[chunk] + got(n)[chunk]
        else:
            full = (own[...] + got(n)[...]).reshape(384, 512)
            mine(n, pl.ds(0, 8))[...] = dot(mix[TURN[n]], full).astype(low).reshape(8, 48, 512)
        start(n, S1)

    def spread(n, last):
        g, k, (_, _, w, dims) = group_of(n)
        blocks, cols = kept_blocks[g], pl.ds(k * w, w)
        if KIND[n] == "s":
            wide_s[...] = last.astype(f32).reshape(8, 24, 256)
            for p in range(8):
                chunk = dp_of(moved(at, bits_at(dims, p))) // 2
                rows = jnp.concatenate([wide_s[chunk], jnp.zeros((8, 256), f32)], axis=0)
                blocks[p, :, cols] = rows.astype(low)
        else:
            orders = sa if dims == FRAME_DIMS else sb
            wide = dot(orders[0], last[:, :w])
            if KIND[n] != "m" or n == 12:
                wide += dot(orders[1], last[:, w:])
            blocks[:, :, cols] = wide.astype(low).reshape(8, 16, w)

    def send_last(g):
        for p in range(1, 8):
            last_copy(g, p).start()

    def finish(g):
        parts, _, w, _ = GROUPS[g]
        total = kept_blocks[g][0].astype(f32)
        for p in range(1, 8):
            last_copy(g, p).wait_recv()
            total = total + sent_blocks[g][p - 1].astype(f32)
        for k, n in enumerate(parts):
            if KIND[n] == "s":
                out_s[k] = total[:, k * w : (k + 1) * w]
            else:
                (out_m if n == 12 else out.at[n - n // 13])[:, 0:w] = total[:, k * w : (k + 1) * w]

    def middle(n, s):
        keep = KEEP[s - 1]
        if s == 1 and n < 6:
            local(n).wait()
        arrived(n, (S1, S2, S3)[s - 1])
        if s == 3:
            spread(n, mine(n, 0)[...] + half(n, 3)[0])
            return
        kept = mine(n, pl.ds(0, keep))
        kept[...] = kept[...] + half(n, s)[...]
        start(n, (S2, S3)[s - 1])

    def every(action, parts, *args):
        for n in parts:
            action(n, *args)

    lane = lax.broadcasted_iota(jnp.int32, (ROWS, 128), 1)
    zero = jnp.zeros((), low)
    get_wo.wait()
    get_after.wait()
    gm_all[...] = dot_t(after[...].astype(low), wo[...]).astype(low)
    get_proj.wait()
    for n in range(6):
        local(n).start()
    get_wp, get_first, get_mixed = load(4, wp_ref, wp), load(5, first_ref, first_low), load(6, mixed_ref, mixed)
    get_frames, get_mw, get_mo = load(3, frames_ref, frames), load(7, mw_ref, mw), load(8, mo_ref, mo)

    def one_clip(clip, carry):
        @pl.when(clip < CLIPS_HERE - 1)
        def _():
            probs_copy(clip + 1).start()

        rows = pl.ds(pl.multiple_of(clip * ROWS, 16), ROWS)
        probs_copy(clip).wait()
        for pair in range(6):
            cols = [pl.ds(n * D + pair * 128, 128) for n in range(3)]
            q, k, v = (proj[rows, c] for c in cols)
            gm = gm_all[rows, pair * 128 : pair * 128 + 128]
            totals = [0.0, 0.0, 0.0]
            for side in range(2):
                here = (lane < 64) if side == 0 else (lane >= 64)
                q_here, k_here, gm_here = (jnp.where(here, value, zero) for value in (q, k, gm))
                dp = dot_t(v, gm_here)
                p_low = probs[clip % 2, 2 * pair + side]
                p = p_low.astype(f32)
                gs = (p * (dp - jnp.sum(dp * p, axis=0, keepdims=True))).astype(low)
                parts = (dot_tl(gs, k_here), dot(gs, q_here), dot(p_low, gm_here))
                totals = [total + part for total, part in zip(totals, parts)]
            for n, scale in ((0, 0.125), (1, 0.125), (2, 1.0)):
                proj[rows, cols[n]] = (totals[n] * scale).astype(low)

        @pl.when(clip == 2)
        def _():
            every(middle, range(6), 1)

        return carry

    lax.fori_loop(0, CLIPS_HERE, one_clip, 0)

    get_wp.wait()
    ends = jnp.concatenate([proj[pl.ds(c * ROWS + 192, 16)] for c in range(CLIPS_HERE)], axis=0)
    grad = jnp.zeros((16 * CLIPS_HERE, D), f32)
    for n in range(3):
        grad += dot_t(ends[:, n * D : (n + 1) * D], wp[:, n * D : (n + 1) * D])
    for c in range(CLIPS_HERE):
        gmsg[c : c + 1] = grad[16 * c + 5 : 16 * c + 6]
    u, inv = stats(message[...])
    gmsg[...] = norm_back(gmsg[...], u, inv, vec[R_FG : R_FG + 1])
    near = []
    for k, partner in enumerate(around):
        near.append(remote(gmsg, gall.at[fr], near_send.at[0, k], near_recv.at[0, k], partner))
    gall[fr] = gmsg[...]
    get_first.wait()
    get_mixed.wait()

    def late_grad(side, first, stop, left, right):
        grad = dot_tl(left[...], right)
        late[side, :, :, :, pl.ds(first, stop - first)] = grad.astype(low).reshape(8, 2, 48, stop - first)

    late_grad(0, 0, 512, first_low, proj[:, 0:512])
    start(6, CORE)
    late_grad(0, 512, 1024, first_low, proj[:, 512:1024])
    start(8, CORE)
    late_grad(0, 1024, 1536, first_low, proj[:, 1024:1536])
    start(10, CORE)
    begin(6)
    late_grad(1, 0, 768, first_low, proj[:, 1536:2304])
    start(7, CORE)
    begin(8)
    late_grad(1, 768, 1536, mixed, after[...].astype(low))
    start(9, CORE)
    start(11, CORE)
    begin(10)
    every(middle, range(6), 2)
    begin(7)
    begin(9)
    begin(11)
    every(middle, range(6), 3)
    send_last(FEED_A)
    send_last(FEED_S)
    for n in (0, 2):
        total = jnp.zeros((1, D), f32)
        for c in range(CLIPS_HERE):
            total += jnp.sum(proj[pl.ds(c * ROWS, ROWS), n * D : (n + 1) * D].astype(f32), axis=0, keepdims=True)
        to = 2 if n == 0 else 3
        sums[to : to + 1] = total
    get_frames.wait()

    def token_grads(first):
        two = pl.ds(first * ROWS, 2 * ROWS)
        grad_two = jnp.zeros((2 * ROWS, D), f32)
        for n in range(3):
            grad_two += dot_t(proj[two, n * D : (n + 1) * D], wp[:, n * D : (n + 1) * D])
        for clip in (first, first + 1):
            grad = grad_two[(clip - first) * ROWS : (clip - first + 1) * ROWS]
            xs[pl.ds(192, 16)] = jnp.zeros((16, D), f32)
            xs[pl.ds(0, PATCH)] = frames[clip, 0].astype(f32)
            xs[pl.ds(PATCH, 1)] = message[clip : clip + 1]
            u, inv = stats(xs[...])
            sums[0:1] += jnp.sum(grad * u, axis=0, keepdims=True)
            sums[1:2] += jnp.sum(grad, axis=0, keepdims=True)
            xs[...] = after[pl.ds(clip * ROWS, ROWS)] + norm_back(grad, u, inv, vec[R_FG : R_FG + 1])
            tokens[clip, 0] = xs[pl.ds(0, PATCH)].astype(low)
            heads[clip] = xs[pl.ds(0, 16)]

    sums[0:2] = jnp.zeros((2, D), f32)
    token_grads(0)
    token_grads(2)
    get_mp = load(4, mp_ref, wp)
    sums_low[...] = sums[0:16].astype(low)
    for k, partner in enumerate(around):
        near.append(remote(sums_low, sall.at[fr], near_send.at[1, k], near_recv.at[1, k], partner))
    sall[fr] = sums_low[...]
    every(middle, range(6, 12), 1)
    for copy in near[:7]:
        copy.wait_recv()
    get_mw.wait()
    get_mo.wait()
    get_mp.wait()
    def between():
        every(middle, range(6, 12), 2)

    vectors = message_back(
        at, cls_all, pre, normed, qkv, msg_mixed, vec, mw, wp, mo, gall, pick, mgrad, gcls, between)
    core_m = []

    def send_message(k):
        cols = pl.ds(3840 * k, 3840 - 3712 * k)
        core_m.append(remote(mgrad.at[1 - core, :, cols], mgot.at[:, cols], send_sem.at[12 + k, CORE],
                             recv_sem.at[12 + k, CORE], partners["c"]))

    def spread_message(k):
        core_m[k].wait_recv()
        cols = pl.ds(3840 * k, 3840 - 3712 * k)
        spread(12 + k, mgrad[core, :, cols] + mgot[:, cols])
        send_last(MESSAGE + k)

    send_message(0)
    every(middle, range(6, 12), 3)
    send_last(LATE_A)
    send_last(LATE_B)
    spread_message(0)
    for copy in near[7:]:
        copy.wait_recv()
    total = sall[0].astype(f32)
    for k in range(1, FRAMES):
        total = total + sall[k].astype(f32)
    message_vectors(total, vectors, pick, table, mgrad)
    send_message(1)
    finish(FEED_A)
    finish(FEED_S)
    spread_message(1)
    top = lax.broadcasted_iota(jnp.int32, (16, 1), 0) == 0
    for clip in range(CLIPS_HERE):
        tokens[clip, 0, pl.ds(0, 16)] = (heads[clip] + jnp.where(top, gcls[clip : clip + 1], 0.0)).astype(low)
    def sent(g):
        for p in range(1, 8):
            last_copy(g, p).wait_send()

    for key in registry:
        registry[key]().wait_send()
    for g in (FEED_A, FEED_S):
        sent(g)
    for copy in near:
        copy.wait_send()
    core_m[0].wait_send()
    for g in (LATE_A, LATE_B):
        finish(g)
        sent(g)
    for g in (MESSAGE, VECTOR):
        finish(g)
        sent(g)
    core_m[1].wait_send()


def back_and_sums(d_expand, d_shrink, after, proj, probs, frames, first_low, mixed, wp, wo, mw, mp, mo, vec, message, sums,
                  saved):
    vmem = pl.BlockSpec(memory_space=pltpu.VMEM)
    any_spec = pl.BlockSpec(memory_space=pl.ANY)
    S, V, SEM = jax.ShapeDtypeStruct, pltpu.VMEM, pltpu.SemaphoreType.DMA

    def phase_one(count, rows, cols, own=True):
        leads = [4 if own else 8, 4, 2, 1]
        return [V((count, lead, rows, cols), low) for lead in leads]

    scratch = [
        V((D, 3 * D), low), V((D, D), low), V((D, D), low), V((D, D), low), V((ALL, D), f32), V((ALL, 3 * D), low),
        V((2, 12, ROWS, ROWS), low), V((CLIPS_HERE, 1, PATCH, D), low), V((ALL, D), low), V((ALL, D), low),
        V((ROWS, D), f32), V((ALL, D), low), V((CLIPS_HERE, 16, D), f32), V((SUMS, D), f32), V((SLOT, D), f32), V((SLOT, D), f32),
        V((2, 48, 5 * D + 128), low), V((48, 5 * D + 128), low), V((FRAMES, SLOT, D), f32), V((16, D), low), V((FRAMES, 16, D), low),
        V((2, 128, 48), low), V((2, 128, 48), low), V((3, 384, 384), low), V((672, 1), jnp.int32), V((8, 24, 256), f32),
        *phase_one(3, 48, 1024), *phase_one(3, 192, 256), V((2, 8, 2, 48, 1536), low), V((6, 8, 48, 512), low), *phase_one(6, 48, 512, own=False),
        *[V((lead, rows, len(parts) * cols), low) for lead in (8, 7) for parts, rows, cols, _ in GROUPS],
        SEM((9,)), SEM((2,)), SEM((6,)), SEM((N_PARTS, 4)), SEM((N_PARTS, 4)), SEM((2, 7)), SEM((2, 7)), SEM((6, 7)), SEM((6, 7))]
    return pl.pallas_call(
        back_kernel,
        in_specs=[any_spec] * 13 + [vmem] * 9,
        out_specs=[vmem] * 4,
        out_shape=[S((CLIPS_HERE, 1, PATCH, D), low), S((13, 16, 512), f32), S((3, 32, 256), f32), S((16, 1920), f32)],
        scratch_shapes=scratch,
        compiler_params=pltpu.CompilerParams(collective_id=2, has_side_effects=True, vmem_limit_bytes=62 * 2**20),
        name="back_and_sums",
    )(d_expand, d_shrink, after, proj, probs, frames, first_low, mixed, wp, wo, mw, mp, mo,
      vec, message, sums, *saved, index_table())


def unpack_kernel(out, out_s, out_m, mw, mp, mo, ap, ao, ew, sw, *vectors):
    def piece(n, side, w):
        return out[n, 8 * side : 8 * side + 6, 0:w]

    message = (out_m[0:6], out_m[8:14])
    mw[...] = message[0][:, 0:D]
    mp[:, 0:1152] = message[0][:, D:1920]
    mp[:, 1152:2304] = message[1][:, 0:1152]
    mo[...] = message[1][:, 1152:1920]
    for k in range(3):
        for side in range(2):
            ap[:, 512 * k + 256 * side : 512 * k + 256 * side + 256] = piece(6 + 2 * k, side, 256)
            ew[:, 1024 * k + 512 * side : 1024 * k + 512 * side + 512] = piece(2 * k, side, 512)
            x = 512 * k + 256 * side
            target, x = (ap, x + 1536) if x < D else (ao, x - D)
            target[:, x : x + 256] = piece(7 + 2 * k, side, 256)
        sw[:, 256 * k : 256 * (k + 1)] = out_s[k, 0:24]
    lanes = lax.broadcasted_iota(jnp.int32, (6, 128), 1)
    rows = lax.broadcasted_iota(jnp.int32, (6, 128), 0)
    values = out[12, 0:6, 0:128]
    flat = jnp.zeros((128, 128), f32)
    for shift in range(4):
        place_at = (lanes == rows + 6 * shift).astype(f32)
        owner = jnp.where((lanes < 24) | (lanes >= 32), 0, jnp.where(lanes < 28, lanes - 24, (lanes - 28) & 1))
        part = jnp.where(owner == shift, values, 0.0)
        flat += lax.dot_general(part, place_at, (((0,), (0,)), ((), ())), precision=PRECISE, preferred_element_type=f32)
    for ref, (row, count) in zip(vectors, LANES):
        ref[...] = jnp.sum(flat[row : row + count], axis=0)[0 : 6 * count]


LANES = ((12, 1), (13, 1), (14, 1), (30, 2), (17, 1), (0, 1), (1, 1), (28, 2), (4, 1), (5, 1), (6, 1), (24, 4), (11, 1))


def unpack(out, out_s, out_m):
    S = jax.ShapeDtypeStruct
    vmem = pl.BlockSpec(memory_space=pltpu.VMEM)
    shapes = [(6, D), (6, 3 * D), (6, D), (6, 3 * D), (6, D), (6, FF), (24, D)] + [(6 * count,) for _, count in LANES]
    return pl.pallas_call(
        unpack_kernel,
        in_specs=[vmem] * 3,
        out_specs=[vmem] * len(shapes),
        out_shape=[S(shape, f32) for shape in shapes],
        compiler_params=pltpu.CompilerParams(vmem_limit_bytes=BIG),
        name="unpack",
    )(out, out_s, out_m)


def forward_kernel(*refs):
    vectors, refs = refs[: len(VECTORS)], refs[len(VECTORS) :]
    (gids, frames_ref, mw_ref, mp_ref, mo_ref, wp_ref, wo_ref, we_ref, ws_ref,
     vec, message, all_cls, pre_out, normed_out, qkv, msg_mixed,
     first_ref, proj_ref, probs_ref, mixed_ref, resid_ref, second_ref, hidden_ref, dgate_ref,
     result, loss, pooled_out, gpool,
     vw, vp, vo, wp, wo, we, ws, frames, cls, tops, first_low, proj, probs, mixed, resid, second_low, xs,
     hid, dg, acc, pool_all, every, natural, grads,
     load_sem, store_sem, probs_sem, send_sem, recv_sem, near_send, near_recv) = refs
    at = place()
    fr = lax.axis_index("frame")

    def load(n, src, dst):
        copy = pltpu.make_async_copy(src, dst, load_sem.at[n])
        copy.start()
        return copy

    def store(n, src, dst):
        copy = pltpu.make_async_copy(src, dst, store_sem.at[n])
        copy.start()
        return copy

    get_frames = load(0, frames_ref, frames)
    get_wp = [load(1 + j, wp_ref.at[:, pl.ds(j * D, D)], wp.at[j]) for j in range(3)]
    get_mw, get_mp, get_mo = load(4, mw_ref, vw), load(5, mp_ref, vp), load(6, mo_ref, vo)
    vec[...] = jnp.zeros((24, D), f32)
    for ref, rows in zip(vectors, VECTORS):
        for k, row in enumerate(rows):
            vec[row : row + 1] = ref[pl.ds(k * D, D)].astype(f32).reshape(1, D)
    cls[...] = jnp.zeros((SLOT, D), f32)
    around = frame_partners()
    order = ("c",) + CLIP_DIMS
    partner = {d: device_of(moved(at, {d: 1})) for d in order}
    greet(around + [partner[d] for d in order])
    get_frames.wait()
    for c in range(CLIPS_HERE):
        cls[c : c + 1] = frames[c, 0, 0:16].astype(f32)[0:1]
    first_near = [remote(cls, all_cls.at[fr], near_send.at[0, k], near_recv.at[0, k], p) for k, p in enumerate(around)]
    all_cls[fr] = cls[...]

    gain, shift = vec[R_FG : R_FG + 1], vec[R_FS : R_FS + 1]
    xs[pl.ds(192, 16)] = jnp.zeros((16, D), f32)
    for c in range(CLIPS_HERE):
        xs[pl.ds(0, PATCH)] = frames[c, 0].astype(f32)
        u, _ = stats(xs[...])
        first_low[pl.ds(c * ROWS, ROWS)] = (u * gain + shift).astype(low)
    for j in range(3):
        get_wp[j].wait()
        for part in range(2):
            rows = pl.ds(part * 2 * ROWS, 2 * ROWS)
            value = dot(first_low[rows], wp[j]) + vec[R_APB + j : R_APB + j + 1]
            proj[rows, j * D : (j + 1) * D] = value.astype(low)
    get_wo = load(7, wo_ref, wo)
    get_we = [load(8 + j, we_ref.at[:, pl.ds(j * D, D)], we.at[j]) for j in range(4)]
    get_ws = [load(12 + j, ws_ref.at[pl.ds(j * D, D)], ws.at[j]) for j in range(4)]

    get_mw.wait()
    for copy in first_near:
        copy.wait_recv()
    x = all_cls[...].reshape(MROWS, D).astype(low)
    pre = dot(x, vw[...]) + vec[R_MB : R_MB + 1]
    pre_out[...] = pre
    u, _ = stats(pre)
    normed = (u * vec[R_MG : R_MG + 1] + vec[R_MS : R_MS + 1]).astype(low)
    normed_out[...] = normed
    get_mp.wait()
    for j in range(3):
        qkv[:, j * D : (j + 1) * D] = (dot(normed, vp[:, j * D : (j + 1) * D]) + vec[R_MPB + j : R_MPB + j + 1]).astype(low)
    keep = same_clip()
    lane = lax.broadcasted_iota(jnp.int32, (MROWS, 128), 1)
    zero = jnp.zeros((), low)
    for pair in range(6):
        q = qkv[:, pair * 128 : pair * 128 + 128]
        k = qkv[:, D + pair * 128 : D + pair * 128 + 128]
        v = qkv[:, 2 * D + pair * 128 : 2 * D + pair * 128 + 128]
        outs = []
        for half in range(2):
            mine = (lane < 64) if half == 0 else (lane >= 64)
            s = jnp.where(keep, dot_t(jnp.where(mine, q, zero), k) * 0.125, -1e30)
            outs.append(dot(soft(s).astype(low), v))
        msg_mixed[:, pair * 128 : pair * 128 + 128] = jnp.where(lane < 64, outs[0], outs[1]).astype(low)
    get_mo.wait()
    branch = pre + dot(msg_mixed[...], vo[...]) + vec[R_MOB : R_MOB + 1]
    rows = lax.broadcasted_iota(jnp.int32, (MROWS, 1), 0) // SLOT
    message[...] = jnp.sum(jnp.where(rows == fr, branch, 0.0).reshape(FRAMES, SLOT, D), axis=0)

    u, _ = stats(message[...])
    ends = (u * gain + shift).astype(low)
    spot = lax.broadcasted_iota(jnp.int32, (16, 1), 0) == PATCH - 192
    for c in range(CLIPS_HERE):
        window = pl.ds(c * ROWS + 192, 16)
        row = ends[c : c + 1].astype(f32)
        first_low[window] = jnp.where(spot, row, first_low[window].astype(f32)).astype(low)
    for j in range(3):
        row = dot(ends, wp[j]) + vec[R_APB + j : R_APB + j + 1]
        for c in range(CLIPS_HERE):
            window = pl.ds(c * ROWS + 192, 16)
            old = proj[window, j * D : (j + 1) * D].astype(f32)
            proj[window, j * D : (j + 1) * D] = jnp.where(spot, row[c : c + 1], old).astype(low)
    stores = [store(0, first_low, first_ref), store(1, proj, proj_ref)]

    lane = lax.broadcasted_iota(jnp.int32, (ROWS, 128), 1)
    seen = lax.broadcasted_iota(jnp.int32, (ROWS, ROWS), 0) < PATCH + 1

    def probs_out(clip):
        return pltpu.make_async_copy(probs.at[clip % 2], probs_ref.at[clip], probs_sem.at[clip % 2])

    def one_clip(clip, carry):
        @pl.when(clip >= 2)
        def _():
            probs_out(clip - 2).wait()

        rows = pl.ds(pl.multiple_of(clip * ROWS, 16), ROWS)
        for pair in range(6):
            q, k, v = (proj[rows, n * D + pair * 128 : n * D + pair * 128 + 128] for n in range(3))
            total = 0.0
            for half in range(2):
                mine = (lane < 64) if half == 0 else (lane >= 64)
                s = dot_t(jnp.where(mine, k, zero), q) * 0.125
                s = jnp.where(seen, s, -1e30)
                e = jnp.exp(s - jnp.max(s, axis=0, keepdims=True))
                p = (e * (1.0 / jnp.sum(e, axis=0, keepdims=True))).astype(low)
                probs[clip % 2, 2 * pair + half] = p
                total = total + dot_tl(p, jnp.where(mine, v, zero))
            mixed[rows, pair * 128 : pair * 128 + 128] = total.astype(low)
        probs_out(clip).start()
        return carry

    lax.fori_loop(0, CLIPS_HERE, one_clip, 0)
    stores.append(store(2, mixed, mixed_ref))
    get_wo.wait()
    for part in range(2):
        branch = dot(mixed[pl.ds(part * 2 * ROWS, 2 * ROWS)], wo[...]) + vec[R_AOB : R_AOB + 1]
        for c in (2 * part, 2 * part + 1):
            xs[pl.ds(192, 16)] = jnp.zeros((16, D), f32)
            xs[pl.ds(0, PATCH)] = frames[c, 0].astype(f32)
            after = xs[...] + branch[(c - 2 * part) * ROWS : (c - 2 * part + 1) * ROWS]
            rows = pl.ds(c * ROWS, ROWS)
            resid[rows] = after
            u2, _ = stats(after)
            second_low[rows] = (u2 * vec[R_SG : R_SG + 1] + vec[R_SS : R_SS + 1]).astype(low)
    stores += [store(3, resid, resid_ref), store(4, second_low, second_ref)]

    def gate(h):
        sg = 1.0 / (1.0 + jnp.exp(-1.702 * h))
        hs = h * sg
        return sg, hs

    heads = jnp.concatenate([second_low[pl.ds(c * ROWS, 16)] for c in range(CLIPS_HERE)], axis=0)
    total = jnp.zeros((16 * CLIPS_HERE, D), f32)
    for j in range(4):
        get_we[j].wait()
        _, hs = gate(dot(heads, we[j]) + vec[R_EB + j : R_EB + j + 1])
        get_ws[j].wait()
        total += dot(hs.astype(low), ws[j])
    tops[...] = jnp.zeros((SLOT, D), f32)
    for c in range(CLIPS_HERE):
        tops[c : c + 1] = resid[c * ROWS : c * ROWS + 1] + vec[R_SB : R_SB + 1] + total[16 * c : 16 * c + 1]
    near = [remote(tops, pool_all.at[fr], near_send.at[1, k], near_recv.at[1, k], p) for k, p in enumerate(around)]
    pool_all[fr] = tops[...]

    copies, state = [], {}

    def exchange(k):
        copy = remote(every.at[pl.ds(0, 2**k)], every.at[pl.ds(2**k, 2**k)], send_sem.at[k], recv_sem.at[k],
                      partner[order[k]])
        copies.append(copy)

    def step(k):
        if k == 0:
            for copy in near:
                copy.wait_recv()
            s = pool_all[0]
            for f in range(1, FRAMES):
                s = s + pool_all[f]
            pooled = s * 0.125
            pooled_out[...] = pooled[:CLIPS_HERE]
            inv_len = lax.rsqrt(jnp.sum(pooled * pooled, axis=-1, keepdims=True) + 1e-06)
            state.update(pooled=pooled, inv_len=inv_len)
            every[0] = pooled * inv_len
        else:
            copies[k - 1].wait_recv()
        if k < 4:
            exchange(k)

    tile_stores = []
    for j in range(4):
        if j >= 2:
            for copy in tile_stores[2 * (j - 2) : 2 * (j - 1)]:
                copy.wait()
        for part in range(2):
            rows = pl.ds(part * 2 * ROWS, 2 * ROWS)
            h = dot(second_low[rows], we[j]) + vec[R_EB + j : R_EB + j + 1]
            sg, hs = gate(h)
            hidden = hs.astype(low)
            hid[j % 2, rows] = hidden
            dg[j % 2, rows] = (sg + 1.702 * hs * (1.0 - sg)).astype(low)
            out = dot(hidden, ws[j])
            acc[rows] = (resid[rows] + vec[R_SB : R_SB + 1] if j == 0 else acc[rows]) + out
            k = 2 * j + part - 2
            if 0 <= k <= 4:
                step(k)
        for n, (src, dst) in enumerate(((hid, hidden_ref), (dg, dgate_ref))):
            copy = pltpu.make_async_copy(src.at[j % 2], dst.at[:, pl.ds(j * D, D)], store_sem.at[5 + 4 * n + j])
            copy.start()
            tile_stores.append(copy)
    for c in range(CLIPS_HERE):
        result[c, 0] = acc[pl.ds(c * ROWS, PATCH)].astype(low)
    for p in range(16):
        to = moved(at, {d: (p >> k) & 1 for k, d in enumerate(order)})
        natural[dp_of(to)] = every[p]
    n = natural[...].reshape(128, D)
    sims = 50.0 * lax.dot_general(n, n, (((1,), (1,)), ((), ())), precision=PRECISE, preferred_element_type=f32)
    rows = lax.broadcasted_iota(jnp.int32, (128, 128), 0)
    cols = lax.broadcasted_iota(jnp.int32, (128, 128), 1)
    here = (cols & 7) < CLIPS_HERE
    other = here & (rows != cols)
    slot = lax.broadcasted_iota(jnp.int32, (128, 64), 0)
    clip = lax.broadcasted_iota(jnp.int32, (128, 64), 1)
    spot = (((slot >> 3) * CLIPS_HERE + (slot & 7)) == clip) & ((slot & 7) < CLIPS_HERE)
    wide = jnp.broadcast_to(gids[...].astype(f32), (128, 64))
    mine = jnp.where(spot, wide, 0.0)
    gid_col = jnp.sum(mine, axis=-1, keepdims=True)
    gid_row = lax.dot_general(wide, spot.astype(f32), (((1,), (1,)), ((), ())), precision=PRECISE, preferred_element_type=f32)
    same = other & (gid_col == gid_row)
    valid = (lax.broadcasted_iota(jnp.int32, (128, 1), 0) & 7) < CLIPS_HERE

    def log_soft(logits):
        top = jnp.max(logits, axis=-1, keepdims=True)
        e = jnp.exp(logits - top)
        total = jnp.sum(e, axis=-1, keepdims=True)
        return top + jnp.log(total), e / total

    all_log, all_p = log_soft(jnp.where(other, sims, -1e30))
    pos_log, pos_p = log_soft(jnp.where(same, sims, -1e30))
    terms = jnp.where(valid, all_log - pos_log, 0.0)
    loss[...] = jnp.sum(terms, axis=0, keepdims=True) * (1.0 / 64.0)
    gs = jnp.where(valid & here, all_p - pos_p, 0.0)
    grad_all = 50.0 * jnp.dot(gs + gs.T, n, precision=PRECISE, preferred_element_type=f32)
    grads[...] = grad_all.reshape(16, SLOT, D)
    g = grads[lax.axis_index("dp")]
    pooled, inv_len = state["pooled"], state["inv_len"]
    back = inv_len * g - inv_len * inv_len * inv_len * pooled * jnp.sum(pooled * g, axis=-1, keepdims=True)
    gpool[...] = back * 0.125
    for copy in tile_stores[4:] + stores:
        copy.wait()
    for clip in (CLIPS_HERE - 2, CLIPS_HERE - 1):
        probs_out(clip).wait()
    for copy in first_near + near + copies:
        copy.wait_send()


def forward(vectors, gids, frames, mw, mp, mo, wp, wo, we, ws):
    vmem = pl.BlockSpec(memory_space=pltpu.VMEM)
    any_spec = pl.BlockSpec(memory_space=pl.ANY)
    S, V, SEM = jax.ShapeDtypeStruct, pltpu.VMEM, pltpu.SemaphoreType.DMA
    return pl.pallas_call(
        forward_kernel,
        in_specs=[vmem] * (len(VECTORS) + 1) + [any_spec] * 8,
        out_specs=[vmem] * 7 + [any_spec] * 8 + [vmem] * 4,
        out_shape=[
            S((24, D), f32), S((SLOT, D), f32), S((FRAMES, SLOT, D), f32), S((MROWS, D), f32), S((MROWS, D), low),
            S((MROWS, 3 * D), low), S((MROWS, D), low),
            S((ALL, D), low), S((ALL, 3 * D), low), S((CLIPS_HERE, 12, ROWS, ROWS), low), S((ALL, D), low), S((ALL, D), f32),
            S((ALL, D), low), S((ALL, FF), low), S((ALL, FF), low),
            S((CLIPS_HERE, 1, PATCH, D), low), S((1, 1), f32), S((CLIPS_HERE, D), f32), S((SLOT, D), f32)],
        scratch_shapes=[
            V((D, D), low), V((D, 3 * D), low), V((D, D), low), V((3, D, D), low), V((D, D), low), V((4, D, D), low),
            V((4, D, D), low), V((CLIPS_HERE, 1, PATCH, D), low), V((SLOT, D), f32), V((SLOT, D), f32), V((ALL, D), low),
            V((ALL, 3 * D), low), V((2, 12, ROWS, ROWS), low), V((ALL, D), low), V((ALL, D), f32), V((ALL, D), low),
            V((ROWS, D), f32), V((2, ALL, D), low), V((2, ALL, D), low), V((ALL, D), f32), V((FRAMES, SLOT, D), f32),
            V((16, SLOT, D), f32), V((16, SLOT, D), f32), V((16, SLOT, D), f32),
            SEM((16,)), SEM((13,)), SEM((2,)), SEM((4,)), SEM((4,)), SEM((2, 7)), SEM((2, 7))],
        compiler_params=pltpu.CompilerParams(collective_id=0, has_side_effects=True, vmem_limit_bytes=62 * 2**20),
        name="forward",
    )(*vectors, gids, frames, mw, mp, mo, wp, wo, we, ws)


def on_device(
    frames, cotangent, group_ids, message_weight, message_bias, message_gain, message_shift, message_project,
    message_project_bias, message_output, message_output_bias, first_gain, first_shift, attend_project,
    attend_project_bias, attend_output, attend_output_bias, second_gain, second_shift, expand_weight, expand_bias,
    shrink_weight, shrink_bias,
):
    vectors = (
        message_bias, message_gain, message_shift, message_project_bias, message_output_bias, first_gain, first_shift,
        attend_project_bias, attend_output_bias, second_gain, second_shift, expand_bias, shrink_bias,
    )
    (vec, message, *saved, first_low, proj, probs, mixed, resid, second_low, hidden, dgate, result, loss, pooled,
     gpool) = forward(
        vectors, group_ids.reshape(1, 64), frames, message_weight, message_project, message_output, attend_project,
        attend_output, expand_weight, shrink_weight)
    d_expand, d_shrink, after, sums = mlp_back(
        cotangent, gpool, vec, hidden, dgate, second_low, expand_weight, shrink_weight, resid)
    delta_frames, out, out_s, out_m = back_and_sums(
        d_expand, d_shrink, after, proj, probs, frames, first_low, mixed, attend_project, attend_output, message_weight,
        message_project, message_output, vec, message, sums, saved)
    mw, mp, mo, ap, ao, ew, sw, mb, mg, ms, mpb, mob, fg, fs, apb, aob, sg, ss, eb, sb = unpack(out, out_s, out_m)
    return (
        result, loss.reshape(()), pooled, delta_frames, mw, mb, mg, ms, mp, mpb, mo, mob, fg, fs, ap, apb, ao, aob, sg, ss,
        ew, eb, sw, sb,
    )


def solution(mesh):
    placed = (
        P("dp", "frame", None, None),
        P("dp", "frame", None, None),
        P(),
        P(),
        P(),
        P(),
        P(),
        P(),
        P(),
        P(),
        P(),
        P(),
        P(),
        P(),
        P(),
        P(),
        P(),
        P(),
        P(),
        P(),
        P(),
        P(),
        P(),
    )
    return jax.shard_map(
        on_device,
        mesh=mesh,
        in_specs=placed,
        out_specs=(
            P("dp", "frame", None, None),
            P(),
            P("dp", None),
            P("dp", "frame", None, None),
            P(("dp", "frame"), None),
            P(("dp", "frame")),
            P(("dp", "frame")),
            P(("dp", "frame")),
            P(("dp", "frame"), None),
            P(("dp", "frame")),
            P(("dp", "frame"), None),
            P(("dp", "frame")),
            P(("dp", "frame")),
            P(("dp", "frame")),
            P(("dp", "frame"), None),
            P(("dp", "frame")),
            P(("dp", "frame"), None),
            P(("dp", "frame")),
            P(("dp", "frame")),
            P(("dp", "frame")),
            P(("dp", "frame"), None),
            P(("dp", "frame")),
            P(("dp", "frame"), None),
            P(("dp", "frame")),
        ),
        check_vma=False,
    )
```
